32 devices in a mesh: expert: 4 (over x, core), split: 8 (over z, y).
Axes of the slice: x: 2, y: 2, z: 4, core: 2. Of those that a mesh axis runs over, the one named last changes fastest.
Arguments:
- tokens: bfloat16 [1024, 3072], P('expert', 'split'), may hold values from -6 to 6
- expert_ids: int32 [1024, 2], P('expert'), may hold values from 0 to 3, all different within a row; in each aligned block of 256 rows (0 to 255, 256 to 511, ...) at most 256 rows name the same one
- pair_logits: float32 [1024, 2], P('expert'), may hold values from -6 to 6
- gate_weight: bfloat16 [4, 3072, 8192], P('expert', None, 'split'), may hold values from -0.109375 to 0.109375
- up_weight: bfloat16 [4, 3072, 8192], P('expert', None, 'split'), may hold values from -0.109375 to 0.109375
- down_weight: bfloat16 [4, 8192, 3072], P('expert', 'split'), may hold values from -0.0625 to 0.0625
Outputs:
- mixed: bfloat16 [1024, 3072], P('expert', 'split')
The draws below stay inside these ranges and needn't reach their ends.
Inputs may be any that keep to these rules, and one draw needn't show every extreme that they name: `expert_ids`: the two experts of a token differ. Within each aligned block of 256 tokens (the tokens of one index of expert) no expert is named by more than 256 pairs, a bound that some block reaches.
All inputs are finite; a program needn't handle non-finite values.
Results may differ from the reference program's by a relative error of at most 0.019.
Values may be sent and summed in bfloat16 or wider, within the bound.
No kernel may reach another device: no remote copies, remote signals or barrier semaphores. Data moves between devices by JAX's collectives and lax.ppermute only.
A program may use at most 64 MiB of HBM per device.

```python
import math
import jax
import jax.numpy as jnp
import numpy as np
from jax import lax

D = 3072
FF = 8192
TOK_E = 256
EXPERTS = 4
CAP = 256
TOKENS = 1024
N_EXPERT = 4
N_SPLIT = 8


def levels(rng, dims, cuts, least, largest):
    def one(dim, blocks):
        steps = jax.random.uniform(jax.random.fold_in(jax.random.fold_in(rng, 6), dim), (blocks,), jnp.float32, least / len(cuts), largest / len(cuts))
        return jnp.repeat(jnp.exp(steps), dims[dim] // blocks).reshape((-1,) + (1,) * (len(dims) - dim - 1))

    factor_of = one(*cuts[0])
    for cut in cuts[1:]:
        factor_of = factor_of * one(*cut)
    return factor_of


def shared_out(key, own, number, rows, number_of, top, bound, skew):
    order = jax.random.permutation(key, number_of)
    heavy_load, common = load_shares(number_of, rows * top, bound, skew, True), load_shares(number_of, rows * top, bound, skew, False)
    places = jnp.arange(number_of)

    def named(lengths, offset_by):
        used = int((lengths > 0).sum())
        fixed = max(1, used // 4)
        shifted = fixed + (places - fixed + offset_by * (used - fixed)) % max(1, number_of - fixed)
        return jnp.zeros((number_of,), jnp.int32).at[order[jnp.where(places < fixed, places, shifted)]].set(jnp.asarray(lengths, jnp.int32))

    lengths = jnp.where(number % 4 == 0, named(heavy_load, number // 4), named(common, number - number // 4 - 1))
    mixed = jax.random.permutation(jax.random.fold_in(own, 3), number_of)
    giver, receiver = mixed[0:number_of // 2 * 2:2], mixed[1:number_of // 2 * 2:2]
    slack = jnp.minimum(lengths[giver] - 1, bound - lengths[receiver]) // 2
    slack = jnp.where((giver == order[0]) | (receiver == order[0]) | (lengths[receiver] == 0), 0, jnp.maximum(slack, 0))
    shifted = jax.random.randint(jax.random.fold_in(own, 4), (number_of // 2,), 0, 1 << 20) % (slack + 1)
    lengths = lengths.at[giver].add(-shifted).at[receiver].add(shifted)
    members = jnp.searchsorted(jnp.cumsum(lengths), jnp.arange(rows * top), side="right").astype(jnp.int32)
    table = members.reshape(top, rows).T
    table = table[jax.random.permutation(jax.random.fold_in(own, 1), rows)]
    offset_by = jax.random.randint(jax.random.fold_in(own, 2), (rows, 1), 0, top)
    return jnp.take_along_axis(table, (jnp.arange(top)[None, :] + offset_by) % top, axis=1)


def load_shares(amount, total, limit, lean, full):
    weights = [(1 << 20) // math.isqrt(rank ** lean) + 1 for rank in range(1, amount + 1)]
    largest = limit if full else min(limit, max(-(-total // amount), total * weights[0] // sum(weights)))
    least = 1 if total - largest >= amount - 1 else 0
    counts, surplus = [largest] + [least] * (amount - 1), total - largest - least * (amount - 1)
    while surplus > 0:
        movable = [i for i in range(1, amount) if counts[i] < largest] or [i for i in range(1, amount) if counts[i] < limit]
        whole, budget = sum([weights[i] for i in movable]), surplus
        for i in movable:
            extra = min(limit - counts[i], max(1, budget * weights[i] // whole), surplus)
            counts[i] = counts[i] + extra
            surplus = surplus - extra
    return np.array(counts)


def noise(rng, shape, scale, limit, split=(), kind=jnp.bfloat16):
    entries = jax.random.normal(rng, shape, jnp.float32) * scale
    if len(split) > 0:
        entries = levels(rng, shape, split, -0.22, 0.18) * entries
    return jnp.clip(entries, min=-limit, max=limit).astype(kind)


def setup_inputs(seed: int = 0) -> dict:
    splits = jax.random.split(jax.random.key(seed), 7)
    tokens = noise(splits[0], (TOKENS, D), 1.0, 6.0, ((0, 4), (1, 8)))
    expert_ids_keys = jax.random.split(jax.random.fold_in(splits[1], 1), TOKENS // TOK_E)
    expert_ids_turns = jax.random.permutation(jax.random.fold_in(splits[1], 3), TOKENS // TOK_E)
    expert_ids = jax.vmap(lambda own, number: shared_out(jax.random.fold_in(splits[1], 2), own, number, TOK_E, EXPERTS, 2, CAP, 2))(expert_ids_keys, expert_ids_turns).reshape((TOKENS, 2))
    pair_logits = noise(splits[2], (TOKENS, 2), 1.5, 6.0, ((0, 4),), jnp.float32)
    gate_weight = noise(splits[3], (EXPERTS, D, FF), D ** -0.5, 0.109375, ((0, 4), (2, 8)))
    up_weight = noise(splits[4], (EXPERTS, D, FF), D ** -0.5, 0.109375, ((0, 4), (2, 8)))
    down_weight = noise(splits[5], (EXPERTS, FF, D), FF ** -0.5, 0.0625, ((0, 4), (1, 8)))
    return {"tokens": tokens, "expert_ids": expert_ids, "pair_logits": pair_logits, "gate_weight": gate_weight, "up_weight": up_weight, "down_weight": down_weight}


def reference(tokens, expert_ids, pair_logits, gate_weight, up_weight, down_weight):
    first = jax.nn.sigmoid(pair_logits[:, 0] - pair_logits[:, 1])
    mix = jnp.stack([first, 1.0 - first], axis=1).reshape(-1)
    flat = expert_ids.reshape(-1).astype(jnp.int32)
    blocks = flat.reshape(N_EXPERT, 2 * TOK_E)
    labels = jnp.arange(EXPERTS, dtype=jnp.int32)
    onehot = (blocks[:, :, None] == labels[None, None, :]).astype(jnp.int32)
    before = jnp.cumsum(onehot, axis=1) - onehot
    slot = jnp.sum(before * onehot, axis=2).reshape(-1).astype(jnp.int32)
    pair_block = (jnp.arange(2 * TOKENS, dtype=jnp.int32) // (2 * TOK_E)).astype(jnp.int32)
    dest = (pair_block * CAP + slot).astype(jnp.int32)
    count = N_EXPERT * CAP
    doubled = jnp.repeat(tokens, 2, axis=0)
    group = FF // N_SPLIT

    def one_expert(total, index):
        hit = flat == index
        target = jnp.where(hit, dest, count).astype(jnp.int32)
        rows = jnp.zeros((count + 1, D), tokens.dtype).at[target].set(doubled)[:count]
        gate = jnp.dot(rows, gate_weight[index], preferred_element_type=jnp.float32)
        up = jnp.dot(rows, up_weight[index], preferred_element_type=jnp.float32)
        hidden = (jax.nn.silu(gate) * up).astype(jnp.bfloat16)
        hid = hidden.reshape(count, N_SPLIT, group).astype(jnp.float32)
        down = down_weight[index].reshape(N_SPLIT, group, D).astype(jnp.float32)
        parts = jnp.einsum("rsf,sfd->srd", hid, down).astype(jnp.bfloat16)
        parts = lax.optimization_barrier(parts).astype(jnp.float32)
        result = jnp.sum(parts, axis=0)
        picked = result[jnp.minimum(target, count - 1)]
        weight = jnp.where(hit, mix, 0.0)
        contrib = (picked * weight[:, None]).reshape(TOKENS, 2, D).sum(axis=1)
        return total + contrib, None

    total, _ = lax.scan(one_expert, jnp.zeros((TOKENS, D), jnp.float32), labels)
    return total.astype(jnp.bfloat16)
```

```python
import jax
import jax.numpy as jnp
from jax import lax
from jax.experimental import pallas as pl
from jax.experimental.pallas import tpu as pltpu
from jax.sharding import PartitionSpec as P

BOTH = ("expert", "split")
HIDDEN_TILE = 512
SCALE = 4


def pair_mix(pair_logits):
    first = jax.nn.sigmoid(pair_logits[:, 0] - pair_logits[:, 1])
    return jnp.stack([first, 1.0 - first], axis=1)


def dispatched(tokens, expert_ids, pair_logits, w_gate, w_up, w_down, capacity):
    experts = lax.axis_size("expert")
    tok_rows, narrow = tokens.shape
    flat = expert_ids.reshape(-1)
    labels = jnp.arange(experts, dtype=jnp.int32)
    onehot = (flat[:, None] == labels[None, :]).astype(jnp.int32)
    before = jnp.cumsum(onehot, axis=0) - onehot
    slot = jnp.sum(before * onehot, axis=1)
    dest = flat * capacity + slot
    mix = pair_mix(pair_logits).reshape(-1)
    select = (jnp.arange(experts * capacity, dtype=jnp.int32)[:, None] == dest[None, :]).astype(
        jnp.bfloat16
    )
    doubled = jnp.repeat(tokens, 2, axis=0)
    packed = jnp.dot(select, doubled, preferred_element_type=jnp.float32).astype(jnp.bfloat16)
    sending = packed.reshape(experts, capacity, narrow)
    arrived = lax.all_to_all(sending, "expert", split_axis=0, concat_axis=0, tiled=True).reshape(
        experts * capacity, narrow
    )
    piece = lax.all_gather(arrived, "split", axis=1, tiled=True)
    gate = jnp.dot(piece, w_gate, preferred_element_type=jnp.float32)
    up_part = jnp.dot(piece, w_up, preferred_element_type=jnp.float32)
    hidden = (jax.nn.silu(gate) * up_part).astype(jnp.bfloat16)
    terms = jnp.dot(hidden, w_down, preferred_element_type=jnp.float32)
    result = lax.psum_scatter(
        terms.astype(jnp.bfloat16), "split", scatter_dimension=1, tiled=True
    ).astype(jnp.float32)
    narrow = result.shape[1]
    returned = lax.all_to_all(
        result.reshape(experts, capacity, narrow).astype(jnp.bfloat16),
        "expert",
        split_axis=0,
        concat_axis=0,
        tiled=True,
    ).astype(jnp.float32)
    returned = returned.reshape(experts * capacity, narrow)
    picked = returned[dest] * mix[:, None]
    mixed = picked.reshape(tok_rows, 2, narrow).sum(axis=1)
    return mixed.astype(jnp.bfloat16)


def send(value, x=0, c=0, z=0, y=0):
    experts, splits = lax.axis_size("expert"), lax.axis_size("split")
    flip_expert, flip_split = x * 2 + c, z * 2 + y
    pairs = [
        (e * splits + s, (e ^ flip_expert) * splits + (s ^ flip_split))
        for e in range(experts)
        for s in range(splits)
    ]
    return lax.ppermute(value, BOTH, pairs)


def after(value, *earlier):
    return lax.optimization_barrier((value, earlier))[0]


def relayed(over_x, over_y):
    half = over_y[0].shape[1] // 2
    first = jnp.concatenate([v[:, :half] for v in over_y])
    last = jnp.concatenate([v[:, half : 2 * half] for v in over_x])
    return send(first, x=1), send(last, y=1)


def swapped(*blocks):
    return [(v, send(v, c=1)) for v in blocks]


def summed(terms, y, x, rows=slice(None)):
    return total(*[term[y, :, rows] for term in terms[x]])


def diagonal(terms):
    half = terms[0][0].shape[2] // 2
    first = summed(terms, 1, 1, slice(0, half)).astype(jnp.bfloat16)
    last = summed(terms, 1, 1, slice(half, 2 * half)).astype(jnp.bfloat16)
    return send(first, x=1), send(last, y=1)


def plane_sums(terms, first, last):
    half = terms[0][0].shape[2] // 2
    first, last = first.astype(jnp.float32), last.astype(jnp.float32)
    to_x = summed(terms, 0, 1) + jnp.pad(last, ((0, 0), (half, 0), (0, 0)))
    to_y = summed(terms, 1, 0) + jnp.pad(first, ((0, 0), (0, half), (0, 0)))
    return to_x.astype(jnp.bfloat16), to_y.astype(jnp.bfloat16)


def total(*terms):
    result = terms[0].astype(jnp.float32)
    for term in terms[1:]:
        result = result + term.astype(jnp.float32)
    return result


def pieces(x, pair):
    blocks, over_x, over_y, first, last = pair
    size = blocks[1][0][0].shape[1]
    arrays, found = [], []
    for z in range(2):
        for c in range(2):
            parts = [(blocks[z], 0, 0), (over_y[z], 0, 1)]
            if x:
                parts = [(over_x[z], 0, 0), (first[z], 0, 1), (last[z], size // 2, 1)]
            for (array, index), row, y in parts:
                array = array[c]
                if not any(array is v for v in arrays):
                    arrays.append(array)
                place = [i for i, v in enumerate(arrays) if v is array][0]
                found.append((place, index, z, c * size + row, y, min(size, array.shape[1])))
    return arrays, found


def fill(place, arrays, found, z_places, rows, sems):
    my_y = place[place.shape[0] - 1]
    copies = []
    for i, (which, index, z, row, y, count) in enumerate(found):
        source = arrays[which].at[index, pl.ds(0, count)]
        column = ((place[z_places[z]] & 1) * 2 + (my_y ^ y)) * source.shape[1]
        columns = pl.ds(pl.multiple_of(column, 128), source.shape[1])
        target = rows.at[pl.ds(row, count), columns]
        copies.append(pltpu.make_async_copy(source, target, sems.at[i]))
    return copies


def all_of(copies):
    for copy in copies:
        copy.start()
    for copy in copies:
        copy.wait()


def weights_kernel(place, *refs, z):
    w_gate, w_up, gate, up, sems = refs[-5:]
    depth = gate.shape[0]
    quarter = depth // 4
    base = pl.multiple_of((place[z] // 2) * depth, depth)
    all_of(
        [
            pltpu.make_async_copy(
                weight.at[pl.ds(base + q * quarter, quarter)],
                result.at[pl.ds(q * quarter, quarter)],
                sems.at[i, q],
            )
            for q in range(4)
            for i, (weight, result) in enumerate(((w_gate, gate), (w_up, up)))
        ]
    )


def first_kernel(place, *refs, found, z_places):
    arrays, (w_gate, w_up, gate, up, rows, sems) = refs[:-6], refs[-6:]
    all_of(fill(place, arrays, found, z_places, rows, sems))
    for weight, result in ((w_gate, gate), (w_up, up)):
        for t in range(result.shape[0]):
            tile = slice(t * HIDDEN_TILE, (t + 1) * HIDDEN_TILE)
            result[t] = jnp.dot(rows[...], weight[:, tile], preferred_element_type=jnp.float32)


def share_column(place, blocks, tails, sems, size):
    experts = place[place.shape[0] - 2]
    expert = place[place.shape[0] - 3]
    copies = []
    for c, block in enumerate(blocks):
        tail = pl.ds(size, tails.shape[1])
        copies.append(pltpu.make_async_copy(block.at[0, tail], tails.at[c], sems.at[c]))
    all_of(copies)
    column = []
    for c in range(2):
        row = lax.broadcasted_iota(jnp.int32, tails.shape[1:], 0)
        mine = (row == expert) | (row == expert + experts)
        shares = jnp.where(mine, tails[c].astype(jnp.float32), 0.0)
        shares = jnp.sum(shares, axis=0, keepdims=True)[:, :size]
        column.append(jnp.broadcast_to(shares, (128, size)).T)
    return jnp.concatenate(column)[:, :1]


def second_kernel(place, *refs, found, z_places, pairs):
    arrays, refs = refs[:-18], refs[-18:]
    w_gate, w_up, gate, up, w_down = refs[:5]
    results = refs[7:9], refs[9:11]
    rows, downs, hidden, tails, sems, d_sems, t_sems = refs[11:]
    my_y = place[place.shape[0] - 1]
    size, span = results[0][0].shape[2], downs.shape[2]
    copies = fill(place, arrays, found, z_places, rows, sems)
    downs_in = []
    for k, pair in enumerate(pairs):
        columns = pl.ds(pl.multiple_of((place[pair[0]] // 2) * span, span), span)
        downs_in.append(pltpu.make_async_copy(w_down.at[:, columns], downs.at[k], d_sems.at[k]))
    for copy in copies + downs_in:
        copy.start()
    share = 0.5 * share_column(place, refs[5:7], tails, t_sems, size)
    for copy in copies:
        copy.wait()
    for t in range(gate.shape[0]):
        tile = slice(t * HIDDEN_TILE, (t + 1) * HIDDEN_TILE)
        g = gate[t] + jnp.dot(rows[...], w_gate[:, tile], preferred_element_type=jnp.float32)
        u = up[t] + jnp.dot(rows[...], w_up[:, tile], preferred_element_type=jnp.float32)
        value = (g + g * jnp.tanh(0.5 * g)) * u * share
        hidden[:, tile] = value.astype(jnp.bfloat16)
    narrow = results[0][0].shape[3]
    for k, pair in enumerate(pairs):
        downs_in[k].wait()
        terms = jnp.dot(hidden[...], downs[k], preferred_element_type=jnp.float32)
        terms = terms.astype(jnp.bfloat16)
        for r, result in enumerate(results[k]):
            for z in range(2):
                n = (place[pair[0]] & 1) ^ z
                for y in range(2):
                    start = (z * 2 + y) * narrow
                    piece = terms[r * size : (r + 1) * size, start : start + narrow]
                    result[my_y ^ y, n] = piece


def cost(flops, bytes_accessed, transcendentals):
    return pl.CostEstimate(
        flops=flops // SCALE,
        bytes_accessed=bytes_accessed // SCALE,
        transcendentals=transcendentals // SCALE,
    )


def in_hbm(value):
    return pltpu.with_memory_space_constraint(value, pltpu.HBM)


def in_vmem(value):
    return pltpu.with_memory_space_constraint(value, pltpu.VMEM)


ANY = pl.BlockSpec(memory_space=pl.ANY)
SCALARS = pl.BlockSpec(memory_space=pltpu.SMEM)
VMEM = pl.BlockSpec(memory_space=pltpu.VMEM)
SEMS = pltpu.SemaphoreType.DMA


def params(mebibytes):
    return pltpu.CompilerParams(vmem_limit_bytes=mebibytes * 1024 * 1024)


def pair_weights(place, z, w_gate, w_up, narrow, *earlier):
    width, depth = w_gate.shape[1], 4 * narrow
    return pl.pallas_call(
        lambda *refs: weights_kernel(*refs, z=z),
        in_specs=[SCALARS] + [ANY] * (len(earlier) + 2),
        out_specs=[VMEM] * 2,
        scratch_shapes=[SEMS((2, 4))],
        out_shape=[pltpu.VMEM((depth, width), jnp.bfloat16)] * 2,
        compiler_params=params(2),
        cost_estimate=cost(flops=0, bytes_accessed=8 * depth * width, transcendentals=0),
        name="pair_weights",
    )(place, *earlier, w_gate, w_up)


def first_part(place, x, pair, z_places, weights):
    arrays, found = pieces(x, pair)
    size, narrow = pair[0][1][0][0].shape[1:]
    depth, width = weights[0].shape
    rows = 2 * size
    sums = (width // HIDDEN_TILE, rows, HIDDEN_TILE)
    return pl.pallas_call(
        lambda *refs: first_kernel(*refs, found=found, z_places=z_places),
        in_specs=[SCALARS] + [ANY] * len(arrays) + [VMEM, VMEM],
        out_specs=[VMEM, VMEM],
        scratch_shapes=[pltpu.VMEM((rows, depth), jnp.bfloat16), SEMS((len(found),))],
        out_shape=[pltpu.VMEM(sums, jnp.float32)] * 2,
        compiler_params=params(4),
        cost_estimate=cost(
            flops=4 * rows * depth * width,
            bytes_accessed=4 * depth * width + 2 * rows * depth + 8 * rows * width,
            transcendentals=0,
        ),
        name="first_part",
    )(place, *arrays, *[in_vmem(v) for v in weights])


def second_part(place, x, pair, z_places, weights, sums, shares, w_down, pairs):
    arrays, found = pieces(x, pair)
    size, narrow = pair[0][1][0][0].shape[1:]
    depth, width = weights[0].shape
    rows, tail = 2 * size, shares[0].shape[1] - size
    return pl.pallas_call(
        lambda *refs: second_kernel(*refs, found=found, z_places=z_places, pairs=pairs),
        in_specs=[SCALARS] + [ANY] * len(arrays) + [VMEM] * 4 + [ANY] * 3,
        out_specs=[VMEM] * 4,
        scratch_shapes=[
            pltpu.VMEM((rows, depth), jnp.bfloat16),
            pltpu.VMEM((2, width, depth), jnp.bfloat16),
            pltpu.VMEM((rows, width), jnp.bfloat16),
            pltpu.VMEM((2, tail, narrow), jnp.bfloat16),
            SEMS((len(found),)),
            SEMS((2,)),
            SEMS((2,)),
        ],
        out_shape=[pltpu.VMEM((2, 2, size, narrow), jnp.bfloat16)] * 4,
        compiler_params=params(13),
        cost_estimate=cost(
            flops=4 * rows * depth * width + 4 * rows * width * depth,
            bytes_accessed=8 * depth * width + 6 * rows * depth + 8 * rows * width,
            transcendentals=rows * width,
        ),
        name="second_part",
    )(place, *arrays, *[in_vmem(v) for v in (*weights, *sums)], w_down, *shares)


def shares_of(expert_ids, pair_logits):
    mix = pair_mix(pair_logits)
    labels = jnp.arange(lax.axis_size("expert"), dtype=jnp.int32)
    named = expert_ids[None, :, :] == labels[:, None, None]
    return jnp.sum(jnp.where(named, mix[None], 0.0), axis=2)


def share_rows(shares, narrow):
    high = lax.reduce_precision(shares, 8, 7)
    rows = jnp.concatenate([high, shares - high]).astype(jnp.bfloat16)
    return jnp.pad(rows, ((0, -rows.shape[0] % 16), (0, narrow - rows.shape[1])))


def every_row(tokens, expert_ids, pair_logits, w_gate, w_up, w_down):
    expert, split = lax.axis_index("expert"), lax.axis_index("split")
    size, narrow = tokens.shape
    place = [(split // 2) ^ z for z in range(4)]
    place = jnp.stack(place + [expert, lax.axis_size("expert"), split % 2]).astype(jnp.int32)
    w_gate, w_up, w_down = in_hbm(w_gate), in_hbm(w_up), in_hbm(w_down)

    w_gate, w_up, w_down = in_hbm(w_gate), in_hbm(w_up), in_hbm(w_down)
    z0 = tokens[None]
    z1 = send(z0, z=1)
    own = shares_of(expert_ids, pair_logits)
    block = jnp.concatenate([tokens, share_rows(own, narrow)])[None]
    sent = after(z0, own)
    x0, y0, z2 = send(block, x=1), send(sent, y=1), send(sent, z=2)
    x1, y1 = send(z1, x=1), send(z1, y=1)
    sz0, sz1, sx0, sx1, sy0, sy1 = swapped(block, z1, x0, x1, y0, y1)
    near_weights = pair_weights(place, 0, w_gate, w_up, narrow, x0)
    far_weights = pair_weights(place, 2, w_gate, w_up, narrow, x0)
    (x1_, y1_), z2, near_weights, far_weights = after(
        ((x1, y1), z2, near_weights, far_weights)
    )
    first, last = relayed([x0, x1_], [y0, y1_])
    z3 = send(z2, z=1)
    x2, y2 = send(z2, x=1), send(z2, y=1)
    near = [[(sz0, 0), (sz1, 0)], [(sx0, 0), (sx1, 0)], [(sy0, 0), (sy1, 0)], None, None]
    sums_0 = first_part(place, 0, near, (0, 1), near_weights)

    z3, sums_0 = after((z3, sums_0))
    (first, last, x2, y2), sums_0 = after(((first, last, x2, y2), sums_0))
    x3, y3 = send(z3, x=1), send(z3, y=1)
    both_of = lambda v: [(v, 0), (v, 1)]
    near[3:] = [both_of(v) for v in swapped(first, last)]
    sz2, sz3, sx2, sy2 = swapped(z2, z3, x2, y2)
    sums_1 = first_part(place, 1, near, (0, 1), near_weights)
    (x3, y3), sums_1 = after(((x3, y3), sums_1))
    first, last = relayed([x2, x3], [y2, y3])
    sx3, sy3 = swapped(x3, y3)
    far = [[(sz2, 0), (sz3, 0)], [(sx2, 0), (sx3, 0)], [(sy2, 0), (sy3, 0)], None, None]
    pairs = (3, 2), (1, 0)
    parts_0 = second_part(place, 0, far, (2, 3), far_weights, sums_0, sz0, w_down, pairs)
    (first, last), parts_0 = after(((first, last), parts_0))
    far[3:] = [both_of(v) for v in swapped(first, last)]
    far_0, near_0 = [(parts_0[i], send(parts_0[i + 1], c=1)) for i in (0, 2)]
    to_z = total(*[v[:, :1] for v in near_0]).astype(jnp.bfloat16)
    passed_0 = send(to_z, z=1)
    sums_1 = after(sums_1, to_z)
    parts_1 = second_part(place, 1, far, (2, 3), far_weights, sums_1, sx0, w_down, pairs)
    passed_0, parts_1 = after((passed_0, parts_1))
    far_1, near_1 = [(parts_1[i], send(parts_1[i + 1], c=1)) for i in (0, 2)]

    far = far_0, far_1
    to_x, to_y = plane_sums(far, *diagonal(far))
    passed_1 = send(total(*[v[:, :1] for v in near_1]).astype(jnp.bfloat16), z=1)
    from_3 = send(to_x[:1], x=1), send(to_y[:1], y=1)
    to_x, to_y = after((to_x, to_y), *from_3)
    from_2 = send(to_x[1:], x=1), send(to_y[1:], y=1)
    here = summed(far, 0, 0)
    to_2 = send(total(here[:1], *from_3).astype(jnp.bfloat16), z=1)
    to_0 = send(total(here[1:], *from_2, to_2).astype(jnp.bfloat16), z=2)
    last_block = lambda terms, passed: [v[:, 1:] for v in terms] + [passed]
    near = last_block(near_0, passed_0), last_block(near_1, passed_1)
    to_x, to_y = plane_sums(near, *diagonal(near))
    from_0 = send(to_x, x=1), send(to_y, y=1)
    return total(summed(near, 0, 0), *from_0, to_0)[0].astype(jnp.bfloat16)


def body(tokens, expert_ids, pair_logits, gate_weight, up_weight, down_weight):
    capacity = 4 * tokens.shape[0] // lax.axis_size("expert")
    arrays = (tokens, expert_ids, pair_logits, gate_weight[0], up_weight[0], down_weight[0])
    splits = lax.axis_size("split")
    if capacity == tokens.shape[0] and splits == 8 and tokens.shape[0] <= tokens.shape[1]:
        return every_row(*arrays)
    return dispatched(*arrays, capacity)


def solution(mesh):
    in_specs = (
        P("expert", "split"),
        P("expert", None),
        P("expert", None),
        P("expert", None, "split"),
        P("expert", None, "split"),
        P("expert", "split", None),
    )
    out_specs = P("expert", "split")
    return jax.shard_map(body, mesh=mesh, in_specs=in_specs, out_specs=out_specs, check_vma=False)
```

```python
import jax
import jax.numpy as jnp
from jax import lax
from jax.experimental import pallas as pl
from jax.experimental.pallas import tpu as pltpu
from jax.sharding import PartitionSpec as P

BOTH = ("expert", "split")
HIDDEN_TILE = 512
SCALE = 4


def pair_mix(pair_logits):
    first = jax.nn.sigmoid(pair_logits[:, 0] - pair_logits[:, 1])
    return jnp.stack([first, 1.0 - first], axis=1)


def dispatched(tokens, expert_ids, pair_logits, w_gate, w_up, w_down, capacity):
    experts = lax.axis_size("expert")
    tok_rows, narrow = tokens.shape
    flat = expert_ids.reshape(-1)
    labels = jnp.arange(experts, dtype=jnp.int32)
    onehot = (flat[:, None] == labels[None, :]).astype(jnp.int32)
    before = jnp.cumsum(onehot, axis=0) - onehot
    slot = jnp.sum(before * onehot, axis=1)
    dest = flat * capacity + slot
    mix = pair_mix(pair_logits).reshape(-1)
    select = (jnp.arange(experts * capacity, dtype=jnp.int32)[:, None] == dest[None, :]).astype(
        jnp.bfloat16
    )
    doubled = jnp.repeat(tokens, 2, axis=0)
    packed = jnp.dot(select, doubled, preferred_element_type=jnp.float32).astype(jnp.bfloat16)
    sending = packed.reshape(experts, capacity, narrow)
    arrived = lax.all_to_all(sending, "expert", split_axis=0, concat_axis=0, tiled=True).reshape(
        experts * capacity, narrow
    )
    piece = lax.all_gather(arrived, "split", axis=1, tiled=True)
    gate = jnp.dot(piece, w_gate, preferred_element_type=jnp.float32)
    up_part = jnp.dot(piece, w_up, preferred_element_type=jnp.float32)
    hidden = (jax.nn.silu(gate) * up_part).astype(jnp.bfloat16)
    terms = jnp.dot(hidden, w_down, preferred_element_type=jnp.float32)
    result = lax.psum_scatter(
        terms.astype(jnp.bfloat16), "split", scatter_dimension=1, tiled=True
    ).astype(jnp.float32)
    narrow = result.shape[1]
    returned = lax.all_to_all(
        result.reshape(experts, capacity, narrow).astype(jnp.bfloat16),
        "expert",
        split_axis=0,
        concat_axis=0,
        tiled=True,
    ).astype(jnp.float32)
    returned = returned.reshape(experts * capacity, narrow)
    picked = returned[dest] * mix[:, None]
    mixed = picked.reshape(tok_rows, 2, narrow).sum(axis=1)
    return mixed.astype(jnp.bfloat16)


def send(value, x=0, c=0, z=0, y=0):
    experts, splits = lax.axis_size("expert"), lax.axis_size("split")
    flip_expert, flip_split = x * 2 + c, z * 2 + y
    pairs = [
        (e * splits + s, (e ^ flip_expert) * splits + (s ^ flip_split))
        for e in range(experts)
        for s in range(splits)
    ]
    return lax.ppermute(value, BOTH, pairs)


def after(value, *earlier):
    return lax.optimization_barrier((value, earlier))[0]


def relayed(over_x, over_y):
    half = over_y[0].shape[1] // 2
    first = jnp.concatenate([v[:, :half] for v in over_y])
    last = jnp.concatenate([v[:, half : 2 * half] for v in over_x])
    return send(first, x=1), send(last, y=1)


def swapped(*blocks):
    return [(v, send(v, c=1)) for v in blocks]


def summed(terms, y, x, rows=slice(None)):
    return total(*[term[y, :, rows] for term in terms[x]])


def diagonal(terms):
    half = terms[0][0].shape[2] // 2
    first = summed(terms, 1, 1, slice(0, half)).astype(jnp.bfloat16)
    last = summed(terms, 1, 1, slice(half, 2 * half)).astype(jnp.bfloat16)
    return send(first, x=1), send(last, y=1)


def plane_sums(terms, first, last):
    half = terms[0][0].shape[2] // 2
    first, last = first.astype(jnp.float32), last.astype(jnp.float32)
    to_x = summed(terms, 0, 1) + jnp.pad(last, ((0, 0), (half, 0), (0, 0)))
    to_y = summed(terms, 1, 0) + jnp.pad(first, ((0, 0), (0, half), (0, 0)))
    return to_x.astype(jnp.bfloat16), to_y.astype(jnp.bfloat16)


def total(*terms):
    result = terms[0].astype(jnp.float32)
    for term in terms[1:]:
        result = result + term.astype(jnp.float32)
    return result


def pieces(x, pair):
    blocks, over_x, over_y, first, last = pair
    size = blocks[1][0][0].shape[1]
    arrays, found = [], []
    for z in range(2):
        for c in range(2):
            parts = [(blocks[z], 0, 0), (over_y[z], 0, 1)]
            if x:
                parts = [(over_x[z], 0, 0), (first[z], 0, 1), (last[z], size // 2, 1)]
            for (array, index), row, y in parts:
                array = array[c]
                if not any(array is v for v in arrays):
                    arrays.append(array)
                place = [i for i, v in enumerate(arrays) if v is array][0]
                found.append((place, index, z, c * size + row, y, min(size, array.shape[1])))
    return arrays, found


def fill(place, arrays, found, z_places, rows, sems):
    my_y = place[place.shape[0] - 1]
    copies = []
    for i, (which, index, z, row, y, count) in enumerate(found):
        source = arrays[which].at[index, pl.ds(0, count)]
        column = ((place[z_places[z]] & 1) * 2 + (my_y ^ y)) * source.shape[1]
        columns = pl.ds(pl.multiple_of(column, 128), source.shape[1])
        target = rows.at[pl.ds(row, count), columns]
        copies.append(pltpu.make_async_copy(source, target, sems.at[i]))
    return copies


def all_of(copies):
    for copy in copies:
        copy.start()
    for copy in copies:
        copy.wait()


def weight_copies(place, z, weight, result, sems):
    depth = result.shape[0]
    quarter = depth // 4
    base = pl.multiple_of((place[z] // 2) * depth, depth)
    return [
        pltpu.make_async_copy(
            weight.at[pl.ds(base + q * quarter, quarter)],
            result.at[pl.ds(q * quarter, quarter)],
            sems.at[q],
        )
        for q in range(4)
    ]


def weights_kernel(place, *refs, z):
    w_gate, w_up, gate, up, gate_sems, up_sems = refs[-6:]
    all_of(
        weight_copies(place, z, w_gate, gate, gate_sems)
        + weight_copies(place, z, w_up, up, up_sems)
    )


def first_kernel(place, *refs, found, z_places, following):
    arrays, refs = refs[:-9], refs[-9:]
    w_gate, w_up, later, gate, up, later_rows, rows, sems, later_sems = refs
    later = weight_copies(place, following, later, later_rows, later_sems)
    copies = fill(place, arrays, found, z_places, rows, sems)
    for copy in copies + later:
        copy.start()
    for copy in copies:
        copy.wait()
    for weight, result in ((w_gate, gate), (w_up, up)):
        for t in range(result.shape[0]):
            tile = slice(t * HIDDEN_TILE, (t + 1) * HIDDEN_TILE)
            result[t] = jnp.dot(rows[...], weight[:, tile], preferred_element_type=jnp.float32)
    for copy in later:
        copy.wait()


def share_column(place, blocks, tails, sems, size):
    experts = place[place.shape[0] - 2]
    expert = place[place.shape[0] - 3]
    copies = []
    for c, block in enumerate(blocks):
        tail = pl.ds(size, tails.shape[1])
        copies.append(pltpu.make_async_copy(block.at[0, tail], tails.at[c], sems.at[c]))
    all_of(copies)
    column = []
    for c in range(2):
        row = lax.broadcasted_iota(jnp.int32, tails.shape[1:], 0)
        mine = (row == expert) | (row == expert + experts)
        shares = jnp.where(mine, tails[c].astype(jnp.float32), 0.0)
        shares = jnp.sum(shares, axis=0, keepdims=True)[:, :size]
        column.append(jnp.broadcast_to(shares, (128, size)).T)
    return jnp.concatenate(column)[:, :1]


def down_copy(place, pair, w_down, tile, sem):
    span = tile.shape[1]
    columns = pl.ds(pl.multiple_of((place[pair[0]] // 2) * span, span), span)
    return pltpu.make_async_copy(w_down.at[:, columns], tile, sem)


def down_products(place, pair, hidden, tile, results):
    my_y = place[place.shape[0] - 1]
    size, narrow = results[0].shape[2:]
    terms = jnp.dot(hidden[...], tile[...], preferred_element_type=jnp.float32)
    terms = terms.astype(jnp.bfloat16)
    for r, result in enumerate(results):
        for z in range(2):
            n = (place[pair[0]] & 1) ^ z
            for y in range(2):
                start = (z * 2 + y) * narrow
                piece = terms[r * size : (r + 1) * size, start : start + narrow]
                result[my_y ^ y, n] = piece


def second_kernel(place, *refs, x, found, z_places, pairs):
    count = 17 if x else 19
    arrays, refs = refs[:-count], refs[-count:]
    w_gate, w_up, gate, up, w_down = refs[:5]
    shares, out = refs[5:7], refs[7:11]
    rows, tails, sems, t_sems, d_sems, first_tile = refs[11:17]
    hidden, second_tile = out[2:] if x else refs[17:]
    copies = fill(place, arrays, found, z_places, rows, sems)
    downs_in = [
        down_copy(place, pair, w_down, tile, d_sems.at[k])
        for k, (pair, tile) in enumerate(zip(pairs, (first_tile, second_tile)))
    ]
    for copy in copies + downs_in:
        copy.start()
    share = 0.5 * share_column(place, shares, tails, t_sems, out[0].shape[2])
    for copy in copies:
        copy.wait()
    for t in range(gate.shape[0]):
        tile = slice(t * HIDDEN_TILE, (t + 1) * HIDDEN_TILE)
        g = gate[t] + jnp.dot(rows[...], w_gate[:, tile], preferred_element_type=jnp.float32)
        u = up[t] + jnp.dot(rows[...], w_up[:, tile], preferred_element_type=jnp.float32)
        value = (g + g * jnp.tanh(0.5 * g)) * u * share
        hidden[:, tile] = value.astype(jnp.bfloat16)
    downs_in[0].wait()
    down_products(place, pairs[0], hidden, first_tile, out[:2])
    downs_in[1].wait()
    if x == 0:
        down_products(place, pairs[1], hidden, second_tile, out[2:])


def third_kernel(place, hidden, tile, own, sibling, pair):
    down_products(place, pair, hidden, tile, (own, sibling))


def cost(flops, bytes_accessed, transcendentals):
    return pl.CostEstimate(
        flops=flops // SCALE,
        bytes_accessed=bytes_accessed // SCALE,
        transcendentals=transcendentals // SCALE,
    )


def in_hbm(value):
    return pltpu.with_memory_space_constraint(value, pltpu.HBM)


def in_vmem(value):
    return pltpu.with_memory_space_constraint(value, pltpu.VMEM)


ANY = pl.BlockSpec(memory_space=pl.ANY)
SCALARS = pl.BlockSpec(memory_space=pltpu.SMEM)
VMEM = pl.BlockSpec(memory_space=pltpu.VMEM)
SEMS = pltpu.SemaphoreType.DMA


def params(mebibytes):
    return pltpu.CompilerParams(vmem_limit_bytes=mebibytes * 1024 * 1024)


def pair_weights(place, z, w_gate, w_up, narrow, *earlier):
    width, depth = w_gate.shape[1], 4 * narrow
    return pl.pallas_call(
        lambda *refs: weights_kernel(*refs, z=z),
        in_specs=[SCALARS] + [ANY] * (len(earlier) + 2),
        out_specs=[VMEM] * 2,
        scratch_shapes=[SEMS((4,)), SEMS((4,))],
        out_shape=[pltpu.VMEM((depth, width), jnp.bfloat16)] * 2,
        compiler_params=params(2),
        cost_estimate=cost(flops=0, bytes_accessed=8 * depth * width, transcendentals=0),
        name="pair_weights",
    )(place, *earlier, w_gate, w_up)


def first_part(place, x, pair, z_places, weights, following, later):
    arrays, found = pieces(x, pair)
    size, narrow = pair[0][1][0][0].shape[1:]
    depth, width = weights[0].shape
    rows = 2 * size
    sums = pltpu.VMEM((width // HIDDEN_TILE, rows, HIDDEN_TILE), jnp.float32)
    return pl.pallas_call(
        lambda *refs: first_kernel(*refs, found=found, z_places=z_places, following=following),
        in_specs=[SCALARS] + [ANY] * len(arrays) + [VMEM, VMEM, ANY],
        out_specs=[VMEM] * 3,
        scratch_shapes=[
            pltpu.VMEM((rows, depth), jnp.bfloat16),
            SEMS((len(found),)),
            SEMS((4,)),
        ],
        out_shape=[sums, sums, pltpu.VMEM((depth, width), jnp.bfloat16)],
        compiler_params=params(4),
        cost_estimate=cost(
            flops=4 * rows * depth * width,
            bytes_accessed=4 * depth * width + 2 * rows * depth + 8 * rows * width,
            transcendentals=0,
        ),
        name="first_part",
    )(place, *arrays, *[in_vmem(v) for v in weights], later)


def second_part(place, x, pair, z_places, weights, sums, shares, w_down, pairs):
    arrays, found = pieces(x, pair)
    size, narrow = pair[0][1][0][0].shape[1:]
    depth, width = weights[0].shape
    rows, tail = 2 * size, shares[0].shape[1] - size
    part = pltpu.VMEM((2, 2, size, narrow), jnp.bfloat16)
    hidden, tile = [pltpu.VMEM(v, jnp.bfloat16) for v in ((rows, width), (width, depth))]
    return pl.pallas_call(
        lambda *refs: second_kernel(
            *refs, x=x, found=found, z_places=z_places, pairs=pairs
        ),
        in_specs=[SCALARS] + [ANY] * len(arrays) + [VMEM] * 4 + [ANY] * 3,
        out_specs=[VMEM] * 4,
        scratch_shapes=[
            pltpu.VMEM((rows, depth), jnp.bfloat16),
            pltpu.VMEM((2, tail, narrow), jnp.bfloat16),
            SEMS((len(found),)),
            SEMS((2,)),
            SEMS((2,)),
            tile,
        ]
        + ([] if x else [hidden, tile]),
        out_shape=[part, part] + ([hidden, tile] if x else [part, part]),
        compiler_params=params(9 if x else 13),
        cost_estimate=cost(
            flops=4 * rows * depth * width + 4 * rows * width * depth,
            bytes_accessed=8 * depth * width + 6 * rows * depth + 8 * rows * width,
            transcendentals=rows * width,
        ),
        name="second_part",
    )(place, *arrays, *[in_vmem(v) for v in (*weights, *sums)], w_down, *shares)


def third_part(place, hidden, tile, pair, size):
    rows, width = hidden.shape
    narrow = tile.shape[1] // 4
    return pl.pallas_call(
        lambda *refs: third_kernel(*refs, pair=pair),
        in_specs=[SCALARS, VMEM, VMEM],
        out_specs=[VMEM] * 2,
        out_shape=[pltpu.VMEM((2, 2, size, narrow), jnp.bfloat16)] * 2,
        compiler_params=params(8),
        cost_estimate=cost(
            flops=2 * rows * width * tile.shape[1],
            bytes_accessed=2 * width * (rows + tile.shape[1]) + 2 * rows * tile.shape[1],
            transcendentals=0,
        ),
        name="third_part",
    )(place, in_vmem(hidden), in_vmem(tile))


def shares_of(expert_ids, pair_logits):
    mix = pair_mix(pair_logits)
    labels = jnp.arange(lax.axis_size("expert"), dtype=jnp.int32)
    named = expert_ids[None, :, :] == labels[:, None, None]
    return jnp.sum(jnp.where(named, mix[None], 0.0), axis=2)


def share_rows(shares, narrow):
    high = lax.reduce_precision(shares, 8, 7)
    rows = jnp.concatenate([high, shares - high]).astype(jnp.bfloat16)
    return jnp.pad(rows, ((0, -rows.shape[0] % 16), (0, narrow - rows.shape[1])))


def every_row(tokens, expert_ids, pair_logits, w_gate, w_up, w_down):
    expert, split = lax.axis_index("expert"), lax.axis_index("split")
    size, narrow = tokens.shape
    place = [(split // 2) ^ z for z in range(4)]
    place = jnp.stack(place + [expert, lax.axis_size("expert"), split % 2]).astype(jnp.int32)
    w_gate, w_up, w_down = in_hbm(w_gate), in_hbm(w_up), in_hbm(w_down)

    w_gate, w_up, w_down = in_hbm(w_gate), in_hbm(w_up), in_hbm(w_down)
    z0 = tokens[None]
    z1 = send(z0, z=1)
    own = shares_of(expert_ids, pair_logits)
    block = jnp.concatenate([tokens, share_rows(own, narrow)])[None]
    sent = after(z0, own)
    x0, y0, z2 = send(block, x=1), send(sent, y=1), send(sent, z=2)
    x1, y1 = send(z1, x=1), send(z1, y=1)
    sz0, sz1, sx0, sx1, sy0, sy1 = swapped(block, z1, x0, x1, y0, y1)
    near_weights = pair_weights(place, 0, w_gate, w_up, narrow, x0)
    (x1_, y1_), z2, near_weights = after(((x1, y1), z2, near_weights))
    first, last = relayed([x0, x1_], [y0, y1_])
    z3 = send(z2, z=1)
    x2, y2 = send(z2, x=1), send(z2, y=1)
    near = [[(sz0, 0), (sz1, 0)], [(sx0, 0), (sx1, 0)], [(sy0, 0), (sy1, 0)], None, None]
    *sums_0, far_gate = first_part(place, 0, near, (0, 1), near_weights, 2, w_gate)

    z3, sums_0 = after((z3, sums_0))
    (first, last, x2, y2), sums_0 = after(((first, last, x2, y2), sums_0))
    x3, y3 = send(z3, x=1), send(z3, y=1)
    both_of = lambda v: [(v, 0), (v, 1)]
    near[3:] = [both_of(v) for v in swapped(first, last)]
    sz2, sz3, sx2, sy2 = swapped(z2, z3, x2, y2)
    *sums_1, far_up = first_part(place, 1, near, (0, 1), near_weights, 2, w_up)
    far_weights = far_gate, far_up
    (x3, y3), sums_1 = after(((x3, y3), sums_1))
    first, last = relayed([x2, x3], [y2, y3])
    sx3, sy3 = swapped(x3, y3)
    far = [[(sz2, 0), (sz3, 0)], [(sx2, 0), (sx3, 0)], [(sy2, 0), (sy3, 0)], None, None]
    pairs = (3, 2), (1, 0)
    parts_0 = second_part(place, 0, far, (2, 3), far_weights, sums_0, sz0, w_down, pairs)
    (first, last, sx2, sx3), parts_0 = after(((first, last, sx2, sx3), parts_0))
    far[1] = [(sx2, 0), (sx3, 0)]
    far[3:] = [both_of(v) for v in swapped(first, last)]
    near_0 = parts_0[2], send(parts_0[3], c=1)
    near_0, parts_0 = after((near_0, parts_0), far[3:])
    far_0 = parts_0[0], send(parts_0[1], c=1)
    to_z = total(*[v[:, :1] for v in near_0]).astype(jnp.bfloat16)
    passed_0 = send(to_z, z=1)
    sums_1 = after(sums_1, to_z)
    *parts_1, hidden, tile = second_part(
        place, 1, far, (2, 3), far_weights, sums_1, sx0, w_down, pairs
    )
    passed_0, far_0, parts_1 = after((passed_0, far_0, parts_1))
    other_1 = send(parts_1[1], c=1)
    last_1 = third_part(place, after(hidden, far_0), tile, pairs[1], size)
    other_1, last_1 = after((other_1, last_1))
    far_1, near_1 = (parts_1[0], other_1), (last_1[0], send(last_1[1], c=1))

    far = far_0, far_1
    corner = diagonal(far)
    to_z = total(*[v[:, :1] for v in near_1]).astype(jnp.bfloat16)
    passed_1 = send(to_z, z=1)
    to_x, to_y = plane_sums(far, *after(corner, to_z))
    from_3 = send(to_x[:1], x=1), send(to_y[:1], y=1)
    here = summed(far, 0, 0)
    to_2 = total(here[:1], *from_3).astype(jnp.bfloat16)
    to_x, to_y = after((to_x, to_y), to_2)
    to_2 = send(to_2, z=1)
    from_2 = send(to_x[1:], x=1), send(to_y[1:], y=1)
    last_block = lambda terms, passed: [v[:, 1:] for v in terms] + [passed]
    near = last_block(near_0, passed_0), last_block(near_1, passed_1)
    corner = diagonal(near)
    from_2, corner = after((from_2, corner))
    to_0 = send(total(here[1:], *from_2, to_2).astype(jnp.bfloat16), z=2)
    to_x, to_y = plane_sums(near, *after(corner, to_2))
    from_0 = send(to_x, x=1), send(to_y, y=1)
    return total(summed(near, 0, 0), *from_0, to_0)[0].astype(jnp.bfloat16)


def body(tokens, expert_ids, pair_logits, gate_weight, up_weight, down_weight):
    capacity = 4 * tokens.shape[0] // lax.axis_size("expert")
    arrays = (tokens, expert_ids, pair_logits, gate_weight[0], up_weight[0], down_weight[0])
    splits = lax.axis_size("split")
    if capacity == tokens.shape[0] and splits == 8 and tokens.shape[0] <= tokens.shape[1]:
        return every_row(*arrays)
    return dispatched(*arrays, capacity)


def solution(mesh):
    in_specs = (
        P("expert", "split"),
        P("expert", None),
        P("expert", None),
        P("expert", None, "split"),
        P("expert", None, "split"),
        P("expert", "split", None),
    )
    out_specs = P("expert", "split")
    return jax.shard_map(body, mesh=mesh, in_specs=in_specs, out_specs=out_specs, check_vma=False)
```

```python
import jax
import jax.numpy as jnp
from jax import lax
from jax.experimental import pallas as pl
from jax.experimental.pallas import tpu as pltpu
from jax.sharding import PartitionSpec as P

BOTH = ("expert", "split")
HIDDEN_TILE = 512
SCALE = 4


def pair_mix(pair_logits):
    first = jax.nn.sigmoid(pair_logits[:, 0] - pair_logits[:, 1])
    return jnp.stack([first, 1.0 - first], axis=1)


def dispatched(tokens, expert_ids, pair_logits, w_gate, w_up, w_down, capacity):
    experts = lax.axis_size("expert")
    tok_rows, narrow = tokens.shape
    flat = expert_ids.reshape(-1)
    labels = jnp.arange(experts, dtype=jnp.int32)
    onehot = (flat[:, None] == labels[None, :]).astype(jnp.int32)
    before = jnp.cumsum(onehot, axis=0) - onehot
    slot = jnp.sum(before * onehot, axis=1)
    dest = flat * capacity + slot
    mix = pair_mix(pair_logits).reshape(-1)
    select = (jnp.arange(experts * capacity, dtype=jnp.int32)[:, None] == dest[None, :]).astype(
        jnp.bfloat16
    )
    doubled = jnp.repeat(tokens, 2, axis=0)
    packed = jnp.dot(select, doubled, preferred_element_type=jnp.float32).astype(jnp.bfloat16)
    sending = packed.reshape(experts, capacity, narrow)
    arrived = lax.all_to_all(sending, "expert", split_axis=0, concat_axis=0, tiled=True).reshape(
        experts * capacity, narrow
    )
    piece = lax.all_gather(arrived, "split", axis=1, tiled=True)
    gate = jnp.dot(piece, w_gate, preferred_element_type=jnp.float32)
    up_part = jnp.dot(piece, w_up, preferred_element_type=jnp.float32)
    hidden = (jax.nn.silu(gate) * up_part).astype(jnp.bfloat16)
    terms = jnp.dot(hidden, w_down, preferred_element_type=jnp.float32)
    result = lax.psum_scatter(
        terms.astype(jnp.bfloat16), "split", scatter_dimension=1, tiled=True
    ).astype(jnp.float32)
    narrow = result.shape[1]
    returned = lax.all_to_all(
        result.reshape(experts, capacity, narrow).astype(jnp.bfloat16),
        "expert",
        split_axis=0,
        concat_axis=0,
        tiled=True,
    ).astype(jnp.float32)
    returned = returned.reshape(experts * capacity, narrow)
    picked = returned[dest] * mix[:, None]
    mixed = picked.reshape(tok_rows, 2, narrow).sum(axis=1)
    return mixed.astype(jnp.bfloat16)


def send(value, x=0, c=0, z=0, y=0):
    experts, splits = lax.axis_size("expert"), lax.axis_size("split")
    flip_expert, flip_split = x * 2 + c, z * 2 + y
    pairs = [
        (e * splits + s, (e ^ flip_expert) * splits + (s ^ flip_split))
        for e in range(experts)
        for s in range(splits)
    ]
    return lax.ppermute(value, BOTH, pairs)


def after(value, *earlier):
    return lax.optimization_barrier((value, earlier))[0]


def relayed(over_x, over_y):
    half = over_y[0].shape[1] // 2
    first = jnp.concatenate([v[:, :half] for v in over_y])
    last = jnp.concatenate([v[:, half : 2 * half] for v in over_x])
    return send(first, x=1), send(last, y=1)


def swapped(*blocks):
    return [(v, send(v, c=1)) for v in blocks]


def summed(terms, y, x, rows=slice(None)):
    return total(*[term[y, :, rows] for term in terms[x]])


def diagonal(terms):
    half = terms[0][0].shape[2] // 2
    first = summed(terms, 1, 1, slice(0, half)).astype(jnp.bfloat16)
    last = summed(terms, 1, 1, slice(half, 2 * half)).astype(jnp.bfloat16)
    return send(first, x=1), send(last, y=1)


def plane_sums(terms, first, last):
    half = terms[0][0].shape[2] // 2
    first, last = first.astype(jnp.float32), last.astype(jnp.float32)
    to_x = summed(terms, 0, 1) + jnp.pad(last, ((0, 0), (half, 0), (0, 0)))
    to_y = summed(terms, 1, 0) + jnp.pad(first, ((0, 0), (0, half), (0, 0)))
    return to_x.astype(jnp.bfloat16), to_y.astype(jnp.bfloat16)


def total(*terms):
    result = terms[0].astype(jnp.float32)
    for term in terms[1:]:
        result = result + term.astype(jnp.float32)
    return result


def pieces(x, pair):
    blocks, over_x, over_y, first, last = pair
    size = blocks[1][0][0].shape[1]
    arrays, found = [], []
    for z in range(2):
        for c in range(2):
            parts = [(blocks[z], 0, 0), (over_y[z], 0, 1)]
            if x:
                parts = [(over_x[z], 0, 0), (first[z], 0, 1), (last[z], size // 2, 1)]
            for (array, index), row, y in parts:
                array = array[c]
                if not any(array is v for v in arrays):
                    arrays.append(array)
                place = [i for i, v in enumerate(arrays) if v is array][0]
                found.append((place, index, z, c * size + row, y, min(size, array.shape[1])))
    return arrays, found


def fill(place, arrays, found, z_places, rows, sems):
    my_y = place[place.shape[0] - 1]
    copies = []
    for i, (which, index, z, row, y, count) in enumerate(found):
        source = arrays[which].at[index, pl.ds(0, count)]
        column = ((place[z_places[z]] & 1) * 2 + (my_y ^ y)) * source.shape[1]
        columns = pl.ds(pl.multiple_of(column, 128), source.shape[1])
        target = rows.at[pl.ds(row, count), columns]
        copies.append(pltpu.make_async_copy(source, target, sems.at[i]))
    return copies


def all_of(copies):
    for copy in copies:
        copy.start()
    for copy in copies:
        copy.wait()


def weight_copies(place, z, weight, result, sems):
    depth = result.shape[0]
    quarter = depth // 4
    base = pl.multiple_of((place[z] // 2) * depth, depth)
    return [
        pltpu.make_async_copy(
            weight.at[pl.ds(base + q * quarter, quarter)],
            result.at[pl.ds(q * quarter, quarter)],
            sems.at[q],
        )
        for q in range(4)
    ]


def weights_kernel(place, *refs, z):
    w_gate, w_up, gate, up, gate_sems, up_sems = refs[-6:]
    all_of(
        weight_copies(place, z, w_gate, gate, gate_sems)
        + weight_copies(place, z, w_up, up, up_sems)
    )


def first_kernel(place, *refs, found, z_places, following):
    arrays, refs = refs[:-9], refs[-9:]
    w_gate, w_up, later, gate, up, later_rows, rows, sems, later_sems = refs
    later = weight_copies(place, following, later, later_rows, later_sems)
    copies = fill(place, arrays, found, z_places, rows, sems)
    for copy in copies + later:
        copy.start()
    for copy in copies:
        copy.wait()
    for weight, result in ((w_gate, gate), (w_up, up)):
        for t in range(result.shape[0]):
            tile = slice(t * HIDDEN_TILE, (t + 1) * HIDDEN_TILE)
            result[t] = jnp.dot(rows[...], weight[:, tile], preferred_element_type=jnp.float32)
    for copy in later:
        copy.wait()


def share_column(place, blocks, tails, sems, size):
    experts = place[place.shape[0] - 2]
    expert = place[place.shape[0] - 3]
    copies = []
    for c, block in enumerate(blocks):
        tail = pl.ds(size, tails.shape[1])
        copies.append(pltpu.make_async_copy(block.at[0, tail], tails.at[c], sems.at[c]))
    all_of(copies)
    column = []
    for c in range(2):
        row = lax.broadcasted_iota(jnp.int32, tails.shape[1:], 0)
        mine = (row == expert) | (row == expert + experts)
        shares = jnp.where(mine, tails[c].astype(jnp.float32), 0.0)
        shares = jnp.sum(shares, axis=0, keepdims=True)[:, :size]
        column.append(jnp.broadcast_to(shares, (128, size)).T)
    return jnp.concatenate(column)[:, :1]


def down_copy(place, pair, w_down, tile, sem):
    span = tile.shape[1]
    columns = pl.ds(pl.multiple_of((place[pair[0]] // 2) * span, span), span)
    return pltpu.make_async_copy(w_down.at[:, columns], tile, sem)


def down_products(place, pair, hidden, tile, results):
    my_y = place[place.shape[0] - 1]
    size, narrow = results[0].shape[2:]
    terms = jnp.dot(hidden[...], tile[...], preferred_element_type=jnp.float32)
    terms = terms.astype(jnp.bfloat16)
    for r, result in enumerate(results):
        for z in range(2):
            n = (place[pair[0]] & 1) ^ z
            for y in range(2):
                start = (z * 2 + y) * narrow
                piece = terms[r * size : (r + 1) * size, start : start + narrow]
                result[my_y ^ y, n] = piece


def second_kernel(place, *refs, x, found, z_places, pairs):
    count = 17 if x else 19
    arrays, refs = refs[:-count], refs[-count:]
    w_gate, w_up, gate, up, w_down = refs[:5]
    shares, out = refs[5:7], refs[7:11]
    rows, tails, sems, t_sems, d_sems, first_tile = refs[11:17]
    hidden, second_tile = out[2:] if x else refs[17:]
    copies = fill(place, arrays, found, z_places, rows, sems)
    downs_in = [
        down_copy(place, pair, w_down, tile, d_sems.at[k])
        for k, (pair, tile) in enumerate(zip(pairs, (first_tile, second_tile)))
    ]
    for copy in copies + downs_in:
        copy.start()
    share = 0.5 * share_column(place, shares, tails, t_sems, out[0].shape[2])
    for copy in copies:
        copy.wait()
    for t in range(gate.shape[0]):
        tile = slice(t * HIDDEN_TILE, (t + 1) * HIDDEN_TILE)
        g = gate[t] + jnp.dot(rows[...], w_gate[:, tile], preferred_element_type=jnp.float32)
        u = up[t] + jnp.dot(rows[...], w_up[:, tile], preferred_element_type=jnp.float32)
        value = (g + g * jnp.tanh(0.5 * g)) * u * share
        hidden[:, tile] = value.astype(jnp.bfloat16)
    downs_in[0].wait()
    down_products(place, pairs[0], hidden, first_tile, out[:2])
    downs_in[1].wait()
    if x == 0:
        down_products(place, pairs[1], hidden, second_tile, out[2:])


def third_kernel(place, hidden, tile, own, sibling, pair):
    down_products(place, pair, hidden, tile, (own, sibling))


def cost(flops, bytes_accessed, transcendentals):
    return pl.CostEstimate(
        flops=flops // SCALE,
        bytes_accessed=bytes_accessed // SCALE,
        transcendentals=transcendentals // SCALE,
    )


def in_hbm(value):
    return pltpu.with_memory_space_constraint(value, pltpu.HBM)


def in_vmem(value):
    return pltpu.with_memory_space_constraint(value, pltpu.VMEM)


ANY = pl.BlockSpec(memory_space=pl.ANY)
SCALARS = pl.BlockSpec(memory_space=pltpu.SMEM)
VMEM = pl.BlockSpec(memory_space=pltpu.VMEM)
SEMS = pltpu.SemaphoreType.DMA


def params(mebibytes):
    return pltpu.CompilerParams(vmem_limit_bytes=mebibytes * 1024 * 1024)


def pair_weights(place, z, w_gate, w_up, narrow, *earlier):
    width, depth = w_gate.shape[1], 4 * narrow
    return pl.pallas_call(
        lambda *refs: weights_kernel(*refs, z=z),
        in_specs=[SCALARS] + [ANY] * (len(earlier) + 2),
        out_specs=[VMEM] * 2,
        scratch_shapes=[SEMS((4,)), SEMS((4,))],
        out_shape=[pltpu.VMEM((depth, width), jnp.bfloat16)] * 2,
        compiler_params=params(2),
        cost_estimate=cost(flops=0, bytes_accessed=8 * depth * width, transcendentals=0),
        name="pair_weights",
    )(place, *earlier, w_gate, w_up)


def first_part(place, x, pair, z_places, weights, following, later):
    arrays, found = pieces(x, pair)
    size, narrow = pair[0][1][0][0].shape[1:]
    depth, width = weights[0].shape
    rows = 2 * size
    sums = pltpu.VMEM((width // HIDDEN_TILE, rows, HIDDEN_TILE), jnp.float32)
    return pl.pallas_call(
        lambda *refs: first_kernel(*refs, found=found, z_places=z_places, following=following),
        in_specs=[SCALARS] + [ANY] * len(arrays) + [VMEM, VMEM, ANY],
        out_specs=[VMEM] * 3,
        scratch_shapes=[
            pltpu.VMEM((rows, depth), jnp.bfloat16),
            SEMS((len(found),)),
            SEMS((4,)),
        ],
        out_shape=[sums, sums, pltpu.VMEM((depth, width), jnp.bfloat16)],
        compiler_params=params(4),
        cost_estimate=cost(
            flops=4 * rows * depth * width,
            bytes_accessed=4 * depth * width + 2 * rows * depth + 8 * rows * width,
            transcendentals=0,
        ),
        name="first_part",
    )(place, *arrays, *[in_vmem(v) for v in weights], later)


def second_part(place, x, pair, z_places, weights, sums, shares, w_down, pairs):
    arrays, found = pieces(x, pair)
    size, narrow = pair[0][1][0][0].shape[1:]
    depth, width = weights[0].shape
    rows, tail = 2 * size, shares[0].shape[1] - size
    part = pltpu.VMEM((2, 2, size, narrow), jnp.bfloat16)
    hidden, tile = [pltpu.VMEM(v, jnp.bfloat16) for v in ((rows, width), (width, depth))]
    return pl.pallas_call(
        lambda *refs: second_kernel(
            *refs, x=x, found=found, z_places=z_places, pairs=pairs
        ),
        in_specs=[SCALARS] + [ANY] * len(arrays) + [VMEM] * 4 + [ANY] * 3,
        out_specs=[VMEM] * 4,
        scratch_shapes=[
            pltpu.VMEM((rows, depth), jnp.bfloat16),
            pltpu.VMEM((2, tail, narrow), jnp.bfloat16),
            SEMS((len(found),)),
            SEMS((2,)),
            SEMS((2,)),
            tile,
        ]
        + ([] if x else [hidden, tile]),
        out_shape=[part, part] + ([hidden, tile] if x else [part, part]),
        compiler_params=params(9 if x else 13),
        cost_estimate=cost(
            flops=4 * rows * depth * width + 4 * rows * width * depth,
            bytes_accessed=8 * depth * width + 6 * rows * depth + 8 * rows * width,
            transcendentals=rows * width,
        ),
        name="second_part",
    )(place, *arrays, *[in_vmem(v) for v in (*weights, *sums)], w_down, *shares)


def third_part(place, hidden, tile, pair, size):
    rows, width = hidden.shape
    narrow = tile.shape[1] // 4
    return pl.pallas_call(
        lambda *refs: third_kernel(*refs, pair=pair),
        in_specs=[SCALARS, VMEM, VMEM],
        out_specs=[VMEM] * 2,
        out_shape=[pltpu.VMEM((2, 2, size, narrow), jnp.bfloat16)] * 2,
        compiler_params=params(8),
        cost_estimate=cost(
            flops=2 * rows * width * tile.shape[1],
            bytes_accessed=2 * width * (rows + tile.shape[1]) + 2 * rows * tile.shape[1],
            transcendentals=0,
        ),
        name="third_part",
    )(place, in_vmem(hidden), in_vmem(tile))


def shares_of(expert_ids, pair_logits):
    mix = pair_mix(pair_logits)
    labels = jnp.arange(lax.axis_size("expert"), dtype=jnp.int32)
    named = expert_ids[None, :, :] == labels[:, None, None]
    return jnp.sum(jnp.where(named, mix[None], 0.0), axis=2)


def share_rows(shares, narrow):
    high = lax.reduce_precision(shares, 8, 7)
    rows = jnp.concatenate([high, shares - high]).astype(jnp.bfloat16)
    return jnp.pad(rows, ((0, -rows.shape[0] % 16), (0, narrow - rows.shape[1])))


def every_row(tokens, expert_ids, pair_logits, w_gate, w_up, w_down):
    expert, split = lax.axis_index("expert"), lax.axis_index("split")
    size, narrow = tokens.shape
    place = [(split // 2) ^ z for z in range(4)]
    place = jnp.stack(place + [expert, lax.axis_size("expert"), split % 2]).astype(jnp.int32)
    w_gate, w_up, w_down = in_hbm(w_gate), in_hbm(w_up), in_hbm(w_down)

    w_gate, w_up, w_down = in_hbm(w_gate), in_hbm(w_up), in_hbm(w_down)
    z0 = tokens[None]
    z1 = send(z0, z=1)
    own = shares_of(expert_ids, pair_logits)
    block = jnp.concatenate([tokens, share_rows(own, narrow)])[None]
    sent = after(z0, own)
    x0, y0, z2 = send(block, x=1), send(sent, y=1), send(z0, z=2)
    x1, y1 = send(z1, x=1), send(z1, y=1)
    sz0, sz1, sx0, sx1, sy0, sy1 = swapped(block, z1, x0, x1, y0, y1)
    near_weights = pair_weights(place, 0, w_gate, w_up, narrow, x0)
    (x1_, y1_), z2, near_weights = after(((x1, y1), z2, near_weights))
    first, last = relayed([x0, x1_], [y0, y1_])
    z3 = send(z2, z=1)
    x2, y2 = send(z2, x=1), send(z2, y=1)
    near = [[(sz0, 0), (sz1, 0)], [(sx0, 0), (sx1, 0)], [(sy0, 0), (sy1, 0)], None, None]
    *sums_0, far_gate = first_part(place, 0, near, (0, 1), near_weights, 2, w_gate)

    z3, sums_0 = after((z3, sums_0))
    (first, last, x2, y2), sums_0 = after(((first, last, x2, y2), sums_0))
    x3, y3 = send(z3, x=1), send(z3, y=1)
    both_of = lambda v: [(v, 0), (v, 1)]
    near[3:] = [both_of(v) for v in swapped(first, last)]
    sz2, sz3, sx2, sy2 = swapped(z2, z3, x2, y2)
    *sums_1, far_up = first_part(place, 1, near, (0, 1), near_weights, 2, w_up)
    far_weights = far_gate, far_up
    (x3, y3), sums_1 = after(((x3, y3), sums_1))
    first, last = relayed([x2, x3], [y2, y3])
    sx3, sy3 = swapped(x3, y3)
    far = [[(sz2, 0), (sz3, 0)], [(sx2, 0), (sx3, 0)], [(sy2, 0), (sy3, 0)], None, None]
    pairs = (3, 2), (1, 0)
    parts_0 = second_part(place, 0, far, (2, 3), far_weights, sums_0, sz0, w_down, pairs)
    (first, last, sx2, sx3), parts_0 = after(((first, last, sx2, sx3), parts_0))
    far[1] = [(sx2, 0), (sx3, 0)]
    far[3:] = [both_of(v) for v in swapped(first, last)]
    near_0 = parts_0[2], send(parts_0[3], c=1)
    near_0, parts_0 = after((near_0, parts_0), far[3:])
    far_0 = parts_0[0], send(parts_0[1], c=1)
    to_z = total(*[v[:, :1] for v in near_0]).astype(jnp.bfloat16)
    passed_0 = send(to_z, z=1)
    *parts_1, hidden, tile = second_part(
        place, 1, far, (2, 3), far_weights, sums_1, sx0, w_down, pairs
    )
    far_0, parts_1 = after((far_0, parts_1))
    other_1 = send(parts_1[1], c=1)
    last_1 = third_part(place, after(hidden, far_0), tile, pairs[1], size)
    other_1, last_1 = after((other_1, last_1))
    far_1, near_1 = (parts_1[0], other_1), (last_1[0], send(last_1[1], c=1))

    far = far_0, far_1
    corner = diagonal(far)
    to_z = total(*[v[:, :1] for v in near_1]).astype(jnp.bfloat16)
    passed_1 = send(to_z, z=1)
    to_x, to_y = plane_sums(far, *after(corner, to_z))
    from_3 = send(to_x[:1], x=1), send(to_y[:1], y=1)
    here = summed(far, 0, 0)
    to_2 = total(here[:1], *from_3).astype(jnp.bfloat16)
    to_x, to_y = after((to_x, to_y), to_2)
    to_2 = send(to_2, z=1)
    from_2 = send(to_x[1:], x=1), send(to_y[1:], y=1)
    last_block = lambda terms, passed: [v[:, 1:] for v in terms] + [passed]
    near = last_block(near_0, passed_0), last_block(near_1, passed_1)
    corner = diagonal(near)
    to_0 = total(here[1:], *from_2, to_2).astype(jnp.bfloat16)
    to_x, to_y = plane_sums(near, *after(corner, to_0))
    to_0 = send(to_0, z=2)
    from_0 = send(to_x, x=1), send(to_y, y=1)
    return total(summed(near, 0, 0), *from_0, to_0)[0].astype(jnp.bfloat16)


def body(tokens, expert_ids, pair_logits, gate_weight, up_weight, down_weight):
    capacity = 4 * tokens.shape[0] // lax.axis_size("expert")
    arrays = (tokens, expert_ids, pair_logits, gate_weight[0], up_weight[0], down_weight[0])
    splits = lax.axis_size("split")
    if capacity == tokens.shape[0] and splits == 8 and tokens.shape[0] <= tokens.shape[1]:
        return every_row(*arrays)
    return dispatched(*arrays, capacity)


def solution(mesh):
    in_specs = (
        P("expert", "split"),
        P("expert", None),
        P("expert", None),
        P("expert", None, "split"),
        P("expert", None, "split"),
        P("expert", "split", None),
    )
    out_specs = P("expert", "split")
    return jax.shard_map(body, mesh=mesh, in_specs=in_specs, out_specs=out_specs, check_vma=False)
```

```python
import jax
import jax.numpy as jnp
from jax import lax
from jax.experimental import pallas as pl
from jax.experimental.pallas import tpu as pltpu
from jax.sharding import PartitionSpec as P

BOTH = ("expert", "split")
HIDDEN_TILE = 512
SCALE = 4


def pair_mix(pair_logits):
    first = jax.nn.sigmoid(pair_logits[:, 0] - pair_logits[:, 1])
    return jnp.stack([first, 1.0 - first], axis=1)


def dispatched(tokens, expert_ids, pair_logits, w_gate, w_up, w_down, capacity):
    experts = lax.axis_size("expert")
    tok_rows, narrow = tokens.shape
    flat = expert_ids.reshape(-1)
    labels = jnp.arange(experts, dtype=jnp.int32)
    onehot = (flat[:, None] == labels[None, :]).astype(jnp.int32)
    before = jnp.cumsum(onehot, axis=0) - onehot
    slot = jnp.sum(before * onehot, axis=1)
    dest = flat * capacity + slot
    mix = pair_mix(pair_logits).reshape(-1)
    select = (jnp.arange(experts * capacity, dtype=jnp.int32)[:, None] == dest[None, :]).astype(
        jnp.bfloat16
    )
    doubled = jnp.repeat(tokens, 2, axis=0)
    packed = jnp.dot(select, doubled, preferred_element_type=jnp.float32).astype(jnp.bfloat16)
    sending = packed.reshape(experts, capacity, narrow)
    arrived = lax.all_to_all(sending, "expert", split_axis=0, concat_axis=0, tiled=True).reshape(
        experts * capacity, narrow
    )
    piece = lax.all_gather(arrived, "split", axis=1, tiled=True)
    gate = jnp.dot(piece, w_gate, preferred_element_type=jnp.float32)
    up_part = jnp.dot(piece, w_up, preferred_element_type=jnp.float32)
    hidden = (jax.nn.silu(gate) * up_part).astype(jnp.bfloat16)
    terms = jnp.dot(hidden, w_down, preferred_element_type=jnp.float32)
    result = lax.psum_scatter(
        terms.astype(jnp.bfloat16), "split", scatter_dimension=1, tiled=True
    ).astype(jnp.float32)
    narrow = result.shape[1]
    returned = lax.all_to_all(
        result.reshape(experts, capacity, narrow).astype(jnp.bfloat16),
        "expert",
        split_axis=0,
        concat_axis=0,
        tiled=True,
    ).astype(jnp.float32)
    returned = returned.reshape(experts * capacity, narrow)
    picked = returned[dest] * mix[:, None]
    mixed = picked.reshape(tok_rows, 2, narrow).sum(axis=1)
    return mixed.astype(jnp.bfloat16)


def send(value, x=0, c=0, z=0, y=0):
    experts, splits = lax.axis_size("expert"), lax.axis_size("split")
    flip_expert, flip_split = x * 2 + c, z * 2 + y
    pairs = [
        (e * splits + s, (e ^ flip_expert) * splits + (s ^ flip_split))
        for e in range(experts)
        for s in range(splits)
    ]
    return lax.ppermute(value, BOTH, pairs)


def after(value, *earlier):
    return lax.optimization_barrier((value, earlier))[0]


def relayed(over_x, over_y):
    half = over_y[0].shape[1] // 2
    first = jnp.concatenate([v[:, :half] for v in over_y])
    last = jnp.concatenate([v[:, half : 2 * half] for v in over_x])
    return send(first, x=1), send(last, y=1)


def swapped(*blocks):
    return [(v, send(v, c=1)) for v in blocks]


def summed(terms, y, x, rows=slice(None)):
    return total(*[term[y, :, rows] for term in terms[x]])


def diagonal(terms):
    half = terms[0][0].shape[2] // 2
    first = summed(terms, 1, 1, slice(0, half)).astype(jnp.bfloat16)
    last = summed(terms, 1, 1, slice(half, 2 * half)).astype(jnp.bfloat16)
    return first, last


def across(halves):
    return send(halves[0], x=1), send(halves[1], y=1)


def plane_sums(terms, first, last):
    half = terms[0][0].shape[2] // 2
    first, last = first.astype(jnp.float32), last.astype(jnp.float32)
    to_x = summed(terms, 0, 1) + jnp.pad(last, ((0, 0), (half, 0), (0, 0)))
    to_y = summed(terms, 1, 0) + jnp.pad(first, ((0, 0), (0, half), (0, 0)))
    return to_x.astype(jnp.bfloat16), to_y.astype(jnp.bfloat16)


def total(*terms):
    result = terms[0].astype(jnp.float32)
    for term in terms[1:]:
        result = result + term.astype(jnp.float32)
    return result


def pieces(x, pair):
    blocks, over_x, over_y, first, last = pair
    size = blocks[0][0][0].shape[1]
    arrays, found = [], []
    for z in range(2):
        for c in range(2):
            parts = [(blocks[z], 0, 0), (over_y[z], 0, 1)]
            if x:
                parts = [(over_x[z], 0, 0), (first[z], 0, 1), (last[z], size // 2, 1)]
            for (array, index), row, y in parts:
                array = array[c]
                if not any(array is v for v in arrays):
                    arrays.append(array)
                place = [i for i, v in enumerate(arrays) if v is array][0]
                found.append((place, index, z, c * size + row, y, min(size, array.shape[1])))
    return arrays, found


def fill(place, arrays, found, z_places, rows, sems):
    my_y = place[place.shape[0] - 1]
    copies = []
    for i, (which, index, z, row, y, count) in enumerate(found):
        source = arrays[which].at[index, pl.ds(0, count)]
        column = ((place[z_places[z]] & 1) * 2 + (my_y ^ y)) * source.shape[1]
        columns = pl.ds(pl.multiple_of(column, 128), source.shape[1])
        target = rows.at[pl.ds(row, count), columns]
        copies.append(pltpu.make_async_copy(source, target, sems.at[i]))
    return copies


def all_of(copies):
    for copy in copies:
        copy.start()
    for copy in copies:
        copy.wait()


def weight_copies(place, z, weight, result, sems):
    depth = result.shape[0]
    quarter = depth // 4
    base = pl.multiple_of((place[z] // 2) * depth, depth)
    return [
        pltpu.make_async_copy(
            weight.at[pl.ds(base + q * quarter, quarter)],
            result.at[pl.ds(q * quarter, quarter)],
            sems.at[q],
        )
        for q in range(4)
    ]


def weights_kernel(place, *refs, z):
    w_gate, w_up, gate, up, gate_sems, up_sems = refs[-6:]
    all_of(
        weight_copies(place, z, w_gate, gate, gate_sems)
        + weight_copies(place, z, w_up, up, up_sems)
    )


def first_kernel(place, *refs, found, z_places, following):
    arrays, refs = refs[:-9], refs[-9:]
    w_gate, w_up, later, gate, up, later_rows, rows, sems, later_sems = refs
    later = weight_copies(place, following, later, later_rows, later_sems)
    copies = fill(place, arrays, found, z_places, rows, sems)
    for copy in copies + later:
        copy.start()
    for copy in copies:
        copy.wait()
    for weight, result in ((w_gate, gate), (w_up, up)):
        for t in range(result.shape[0]):
            tile = slice(t * HIDDEN_TILE, (t + 1) * HIDDEN_TILE)
            result[t] = jnp.dot(rows[...], weight[:, tile], preferred_element_type=jnp.float32)
    for copy in later:
        copy.wait()


def share_column(place, blocks, tails, sems, size):
    experts = place[place.shape[0] - 2]
    expert = place[place.shape[0] - 3]
    copies = []
    for c, block in enumerate(blocks):
        tail = pl.ds(size, tails.shape[1])
        copies.append(pltpu.make_async_copy(block.at[0, tail], tails.at[c], sems.at[c]))
    all_of(copies)
    column = []
    for c in range(2):
        row = lax.broadcasted_iota(jnp.int32, tails.shape[1:], 0)
        mine = (row == expert) | (row == expert + experts)
        shares = jnp.where(mine, tails[c].astype(jnp.float32), 0.0)
        shares = jnp.sum(shares, axis=0, keepdims=True)[:, :size]
        column.append(jnp.broadcast_to(shares, (128, size)).T)
    return jnp.concatenate(column)[:, :1]


def down_copy(place, pair, w_down, tile, sem):
    span = tile.shape[1]
    columns = pl.ds(pl.multiple_of((place[pair[0]] // 2) * span, span), span)
    return pltpu.make_async_copy(w_down.at[:, columns], tile, sem)


def down_products(place, pair, hidden, tile, results):
    my_y = place[place.shape[0] - 1]
    size, narrow = results[0].shape[2:]
    terms = jnp.dot(hidden[...], tile[...], preferred_element_type=jnp.float32)
    terms = terms.astype(jnp.bfloat16)
    for r, result in enumerate(results):
        for z in range(2):
            n = (place[pair[0]] & 1) ^ z
            for y in range(2):
                start = (z * 2 + y) * narrow
                piece = terms[r * size : (r + 1) * size, start : start + narrow]
                result[my_y ^ y, n] = piece


def second_kernel(place, *refs, x, found, z_places, pairs):
    count = 17 if x else 19
    arrays, refs = refs[:-count], refs[-count:]
    w_gate, w_up, gate, up, w_down = refs[:5]
    shares, out = refs[5:7], refs[7:11]
    rows, tails, sems, t_sems, d_sems, first_tile = refs[11:17]
    hidden, second_tile = out[2:] if x else refs[17:]
    copies = fill(place, arrays, found, z_places, rows, sems)
    downs_in = [
        down_copy(place, pair, w_down, tile, d_sems.at[k])
        for k, (pair, tile) in enumerate(zip(pairs, (first_tile, second_tile)))
    ]
    for copy in copies + downs_in:
        copy.start()
    share = 0.5 * share_column(place, shares, tails, t_sems, out[0].shape[2])
    for copy in copies:
        copy.wait()
    for t in range(gate.shape[0]):
        tile = slice(t * HIDDEN_TILE, (t + 1) * HIDDEN_TILE)
        g = gate[t] + jnp.dot(rows[...], w_gate[:, tile], preferred_element_type=jnp.float32)
        u = up[t] + jnp.dot(rows[...], w_up[:, tile], preferred_element_type=jnp.float32)
        value = (g + g * jnp.tanh(0.5 * g)) * u * share
        hidden[:, tile] = value.astype(jnp.bfloat16)
    downs_in[0].wait()
    down_products(place, pairs[0], hidden, first_tile, out[:2])
    downs_in[1].wait()
    if x == 0:
        down_products(place, pairs[1], hidden, second_tile, out[2:])


def third_kernel(place, hidden, tile, own, sibling, pair):
    down_products(place, pair, hidden, tile, (own, sibling))


def cost(flops, bytes_accessed, transcendentals):
    return pl.CostEstimate(
        flops=flops // SCALE,
        bytes_accessed=bytes_accessed // SCALE,
        transcendentals=transcendentals // SCALE,
    )


def in_hbm(value):
    return pltpu.with_memory_space_constraint(value, pltpu.HBM)


def in_vmem(value):
    return pltpu.with_memory_space_constraint(value, pltpu.VMEM)


ANY = pl.BlockSpec(memory_space=pl.ANY)
SCALARS = pl.BlockSpec(memory_space=pltpu.SMEM)
VMEM = pl.BlockSpec(memory_space=pltpu.VMEM)
SEMS = pltpu.SemaphoreType.DMA


def params(mebibytes):
    return pltpu.CompilerParams(vmem_limit_bytes=mebibytes * 1024 * 1024)


def pair_weights(place, z, w_gate, w_up, narrow, *earlier):
    width, depth = w_gate.shape[1], 4 * narrow
    return pl.pallas_call(
        lambda *refs: weights_kernel(*refs, z=z),
        in_specs=[SCALARS] + [ANY] * (len(earlier) + 2),
        out_specs=[VMEM] * 2,
        scratch_shapes=[SEMS((4,)), SEMS((4,))],
        out_shape=[pltpu.VMEM((depth, width), jnp.bfloat16)] * 2,
        compiler_params=params(2),
        cost_estimate=cost(flops=0, bytes_accessed=8 * depth * width, transcendentals=0),
        name="pair_weights",
    )(place, *earlier, w_gate, w_up)


def first_part(place, x, pair, z_places, weights, following, later):
    arrays, found = pieces(x, pair)
    size, narrow = pair[0][0][0][0].shape[1:]
    depth, width = weights[0].shape
    rows = 2 * size
    sums = pltpu.VMEM((width // HIDDEN_TILE, rows, HIDDEN_TILE), jnp.float32)
    return pl.pallas_call(
        lambda *refs: first_kernel(*refs, found=found, z_places=z_places, following=following),
        in_specs=[SCALARS] + [ANY] * len(arrays) + [VMEM, VMEM, ANY],
        out_specs=[VMEM] * 3,
        scratch_shapes=[
            pltpu.VMEM((rows, depth), jnp.bfloat16),
            SEMS((len(found),)),
            SEMS((4,)),
        ],
        out_shape=[sums, sums, pltpu.VMEM((depth, width), jnp.bfloat16)],
        compiler_params=params(4),
        cost_estimate=cost(
            flops=4 * rows * depth * width,
            bytes_accessed=4 * depth * width + 2 * rows * depth + 8 * rows * width,
            transcendentals=0,
        ),
        name="first_part",
    )(place, *arrays, *[in_vmem(v) for v in weights], later)


def second_part(place, x, pair, z_places, weights, sums, shares, w_down, pairs):
    arrays, found = pieces(x, pair)
    size, narrow = pair[0][0][0][0].shape[1:]
    depth, width = weights[0].shape
    rows, tail = 2 * size, shares[0].shape[1] - size
    part = pltpu.VMEM((2, 2, size, narrow), jnp.bfloat16)
    hidden, tile = [pltpu.VMEM(v, jnp.bfloat16) for v in ((rows, width), (width, depth))]
    return pl.pallas_call(
        lambda *refs: second_kernel(
            *refs, x=x, found=found, z_places=z_places, pairs=pairs
        ),
        in_specs=[SCALARS] + [ANY] * len(arrays) + [VMEM] * 4 + [ANY] * 3,
        out_specs=[VMEM] * 4,
        scratch_shapes=[
            pltpu.VMEM((rows, depth), jnp.bfloat16),
            pltpu.VMEM((2, tail, narrow), jnp.bfloat16),
            SEMS((len(found),)),
            SEMS((2,)),
            SEMS((2,)),
            tile,
        ]
        + ([] if x else [hidden, tile]),
        out_shape=[part, part] + ([hidden, tile] if x else [part, part]),
        compiler_params=params(9 if x else 13),
        cost_estimate=cost(
            flops=4 * rows * depth * width + 4 * rows * width * depth,
            bytes_accessed=8 * depth * width + 6 * rows * depth + 8 * rows * width,
            transcendentals=rows * width,
        ),
        name="second_part",
    )(place, *arrays, *[in_vmem(v) for v in (*weights, *sums)], w_down, *shares)


def third_part(place, hidden, tile, pair, size):
    rows, width = hidden.shape
    narrow = tile.shape[1] // 4
    return pl.pallas_call(
        lambda *refs: third_kernel(*refs, pair=pair),
        in_specs=[SCALARS, VMEM, VMEM],
        out_specs=[VMEM] * 2,
        out_shape=[pltpu.VMEM((2, 2, size, narrow), jnp.bfloat16)] * 2,
        compiler_params=params(8),
        cost_estimate=cost(
            flops=2 * rows * width * tile.shape[1],
            bytes_accessed=2 * width * (rows + tile.shape[1]) + 2 * rows * tile.shape[1],
            transcendentals=0,
        ),
        name="third_part",
    )(place, in_vmem(hidden), in_vmem(tile))


def shares_of(expert_ids, pair_logits):
    mix = pair_mix(pair_logits)
    labels = jnp.arange(lax.axis_size("expert"), dtype=jnp.int32)
    named = expert_ids[None, :, :] == labels[:, None, None]
    return jnp.sum(jnp.where(named, mix[None], 0.0), axis=2)


def share_rows(shares, narrow):
    high = lax.reduce_precision(shares, 8, 7)
    rows = jnp.concatenate([high, shares - high]).astype(jnp.bfloat16)
    return jnp.pad(rows, ((0, -rows.shape[0] % 16), (0, narrow - rows.shape[1])))


def every_row(tokens, expert_ids, pair_logits, w_gate, w_up, w_down):
    expert, split = lax.axis_index("expert"), lax.axis_index("split")
    size, narrow = tokens.shape
    place = [(split // 2) ^ z for z in range(4)]
    place = jnp.stack(place + [expert, lax.axis_size("expert"), split % 2]).astype(jnp.int32)
    w_gate, w_up, w_down = in_hbm(w_gate), in_hbm(w_up), in_hbm(w_down)

    w_gate, w_up, w_down = in_hbm(w_gate), in_hbm(w_up), in_hbm(w_down)
    z0 = tokens[None]
    z1 = send(z0, z=1)
    x0, y0, z2 = send(z0, x=1), send(z0, y=1), send(z0, z=2)
    x1, y1 = send(z1, x=1), send(z1, y=1)
    sz0, sz1, sx0, sx1, sy0, sy1 = swapped(z0, z1, x0, x1, y0, y1)
    near_weights = pair_weights(place, 0, w_gate, w_up, narrow, x0)
    tail = share_rows(shares_of(expert_ids, after(pair_logits, x0)), narrow)[None]
    (x1_, y1_), z2, near_weights, tail = after(((x1, y1), z2, near_weights, tail))
    first, last = relayed([x0, x1_], [y0, y1_])
    z3 = send(z2, z=1)
    x2, y2 = send(z2, x=1), send(z2, y=1)
    near = [[(sz0, 0), (sz1, 0)], [(sx0, 0), (sx1, 0)], [(sy0, 0), (sy1, 0)], None, None]
    *sums_0, far_gate = first_part(place, 0, near, (0, 1), near_weights, 2, w_gate)

    z3, sums_0 = after((z3, sums_0))
    (first, last, x2, y2), sums_0 = after(((first, last, x2, y2), sums_0))
    block = jnp.concatenate([z3, tail], axis=1)
    x3, y3 = send(block, x=1), send(z3, y=1)
    both_of = lambda v: [(v, 0), (v, 1)]
    near[3:] = [both_of(v) for v in swapped(first, last)]
    sz2, sz3, sx2, sy2 = swapped(z2, block, x2, y2)
    *sums_1, far_up = first_part(place, 1, near, (0, 1), near_weights, 2, w_up)
    far_weights = far_gate, far_up
    (x3, y3), sums_1 = after(((x3, y3), sums_1))
    first, last = relayed([x2, x3], [y2, y3])
    sx3, sy3 = swapped(x3, y3)
    far = [[(sz2, 0), (sz3, 0)], [(sx2, 0), (sx3, 0)], [(sy2, 0), (sy3, 0)], None, None]
    pairs = (3, 2), (1, 0)
    parts_0 = second_part(place, 0, far, (2, 3), far_weights, sums_0, sz3, w_down, pairs)
    (first, last, sx2, sx3), parts_0 = after(((first, last, sx2, sx3), parts_0))
    far[1] = [(sx2, 0), (sx3, 0)]
    far[3:] = [both_of(v) for v in swapped(first, last)]
    near_0 = parts_0[2], send(parts_0[3], c=1)
    near_0, parts_0 = after((near_0, parts_0), far[3:])
    far_0 = parts_0[0], send(parts_0[1], c=1)
    to_z = total(*[v[:, :1] for v in near_0]).astype(jnp.bfloat16)
    *parts_1, hidden, tile = second_part(
        place, 1, far, (2, 3), far_weights, sums_1, sx3, w_down, pairs
    )
    far_0, parts_1 = after((far_0, parts_1))
    far_0, parts_1 = after((far_0, parts_1))
    other_1 = send(parts_1[1], c=1)
    last_1 = third_part(place, after(hidden, far_0), tile, pairs[1], size)
    other_1, last_1 = after((other_1, last_1))
    far = far_0, (parts_1[0], other_1)
    near_1 = last_1[0], send(last_1[1], c=1)

    passed_0 = send(to_z, z=1)
    to_z = total(*[v[:, :1] for v in near_1]).astype(jnp.bfloat16)
    passed_1 = send(to_z, z=1)
    block_3, block_2 = [[[v[:, i : i + 1] for v in terms] for terms in far] for i in range(2)]
    corner_3 = across(diagonal(block_3))
    halves = after(diagonal(block_2), to_z)
    to_x, to_y = plane_sums(block_3, *after(corner_3, halves))
    corner_2 = across(halves)
    from_3 = send(to_x, x=1), send(to_y, y=1)
    from_3, passed_0 = after((from_3, passed_0))
    to_2 = total(summed(block_3, 0, 0), *from_3).astype(jnp.bfloat16)
    to_x, to_y = plane_sums(block_2, *after(corner_2, to_2))
    to_2 = send(to_2, z=1)
    from_2 = send(to_x, x=1), send(to_y, y=1)
    last_block = lambda terms, passed: [v[:, 1:] for v in terms] + [passed]
    near = last_block(near_0, passed_0), last_block(near_1, passed_1)
    corner = across(diagonal(near))
    from_2, passed_1 = after((from_2, passed_1))
    to_0 = total(summed(block_2, 0, 0), *from_2, to_2).astype(jnp.bfloat16)
    to_x, to_y = plane_sums(near, *after(corner, to_0))
    to_0 = send(to_0, z=2)
    from_0 = send(to_x, x=1), send(to_y, y=1)
    return total(summed(near, 0, 0), *from_0, to_0)[0].astype(jnp.bfloat16)


def body(tokens, expert_ids, pair_logits, gate_weight, up_weight, down_weight):
    capacity = 4 * tokens.shape[0] // lax.axis_size("expert")
    arrays = (tokens, expert_ids, pair_logits, gate_weight[0], up_weight[0], down_weight[0])
    splits = lax.axis_size("split")
    if capacity == tokens.shape[0] and splits == 8 and tokens.shape[0] <= tokens.shape[1]:
        return every_row(*arrays)
    return dispatched(*arrays, capacity)


def solution(mesh):
    in_specs = (
        P("expert", "split"),
        P("expert", None),
        P("expert", None),
        P("expert", None, "split"),
        P("expert", None, "split"),
        P("expert", "split", None),
    )
    out_specs = P("expert", "split")
    return jax.shard_map(body, mesh=mesh, in_specs=in_specs, out_specs=out_specs, check_vma=False)
```

```python
import jax
import jax.numpy as jnp
from jax import lax
from jax.experimental import pallas as pl
from jax.experimental.pallas import tpu as pltpu
from jax.sharding import PartitionSpec as P

BOTH = ("expert", "split")
HIDDEN_TILE = 512
SCALE = 4


def pair_mix(pair_logits):
    first = jax.nn.sigmoid(pair_logits[:, 0] - pair_logits[:, 1])
    return jnp.stack([first, 1.0 - first], axis=1)


def dispatched(tokens, expert_ids, pair_logits, w_gate, w_up, w_down, capacity):
    experts = lax.axis_size("expert")
    tok_rows, narrow = tokens.shape
    flat = expert_ids.reshape(-1)
    labels = jnp.arange(experts, dtype=jnp.int32)
    onehot = (flat[:, None] == labels[None, :]).astype(jnp.int32)
    before = jnp.cumsum(onehot, axis=0) - onehot
    slot = jnp.sum(before * onehot, axis=1)
    dest = flat * capacity + slot
    mix = pair_mix(pair_logits).reshape(-1)
    select = (jnp.arange(experts * capacity, dtype=jnp.int32)[:, None] == dest[None, :]).astype(
        jnp.bfloat16
    )
    doubled = jnp.repeat(tokens, 2, axis=0)
    packed = jnp.dot(select, doubled, preferred_element_type=jnp.float32).astype(jnp.bfloat16)
    sending = packed.reshape(experts, capacity, narrow)
    arrived = lax.all_to_all(sending, "expert", split_axis=0, concat_axis=0, tiled=True).reshape(
        experts * capacity, narrow
    )
    piece = lax.all_gather(arrived, "split", axis=1, tiled=True)
    gate = jnp.dot(piece, w_gate, preferred_element_type=jnp.float32)
    up_part = jnp.dot(piece, w_up, preferred_element_type=jnp.float32)
    hidden = (jax.nn.silu(gate) * up_part).astype(jnp.bfloat16)
    terms = jnp.dot(hidden, w_down, preferred_element_type=jnp.float32)
    result = lax.psum_scatter(
        terms.astype(jnp.bfloat16), "split", scatter_dimension=1, tiled=True
    ).astype(jnp.float32)
    narrow = result.shape[1]
    returned = lax.all_to_all(
        result.reshape(experts, capacity, narrow).astype(jnp.bfloat16),
        "expert",
        split_axis=0,
        concat_axis=0,
        tiled=True,
    ).astype(jnp.float32)
    returned = returned.reshape(experts * capacity, narrow)
    picked = returned[dest] * mix[:, None]
    mixed = picked.reshape(tok_rows, 2, narrow).sum(axis=1)
    return mixed.astype(jnp.bfloat16)


def send(value, x=0, c=0, z=0, y=0):
    experts, splits = lax.axis_size("expert"), lax.axis_size("split")
    flip_expert, flip_split = x * 2 + c, z * 2 + y
    pairs = [
        (e * splits + s, (e ^ flip_expert) * splits + (s ^ flip_split))
        for e in range(experts)
        for s in range(splits)
    ]
    return lax.ppermute(value, BOTH, pairs)


def after(value, *earlier):
    return lax.optimization_barrier((value, earlier))[0]


def relayed(over_x, over_y):
    half = over_y[0].shape[1] // 2
    first = jnp.concatenate([v[:, :half] for v in over_y])
    last = jnp.concatenate([v[:, half : 2 * half] for v in over_x])
    return send(first, x=1), send(last, y=1)


def swapped(*blocks):
    return [(v, send(v, c=1)) for v in blocks]


def summed(terms, y, x, rows=slice(None)):
    return total(*[term[y, :, rows] for term in terms[x]])


def diagonal(terms):
    half = terms[0][0].shape[2] // 2
    first = summed(terms, 1, 1, slice(0, half)).astype(jnp.bfloat16)
    last = summed(terms, 1, 1, slice(half, 2 * half)).astype(jnp.bfloat16)
    return send(first, x=1), send(last, y=1)


def plane_sums(terms, first, last):
    half = terms[0][0].shape[2] // 2
    first, last = first.astype(jnp.float32), last.astype(jnp.float32)
    to_x = summed(terms, 0, 1) + jnp.pad(last, ((0, 0), (half, 0), (0, 0)))
    to_y = summed(terms, 1, 0) + jnp.pad(first, ((0, 0), (0, half), (0, 0)))
    return to_x.astype(jnp.bfloat16), to_y.astype(jnp.bfloat16)


def total(*terms):
    result = terms[0].astype(jnp.float32)
    for term in terms[1:]:
        result = result + term.astype(jnp.float32)
    return result


def pieces(x, pair):
    blocks, over_x, over_y, first, last = pair
    size = blocks[1][0][0].shape[1]
    arrays, found = [], []
    for z in range(2):
        for c in range(2):
            parts = [(blocks[z], 0, 0), (over_y[z], 0, 1)]
            if x:
                parts = [(over_x[z], 0, 0), (first[z], 0, 1), (last[z], size // 2, 1)]
            for (array, index), row, y in parts:
                array = array[c]
                if not any(array is v for v in arrays):
                    arrays.append(array)
                place = [i for i, v in enumerate(arrays) if v is array][0]
                found.append((place, index, z, c * size + row, y, min(size, array.shape[1])))
    return arrays, found


def fill(place, arrays, found, z_places, rows):
    my_y = place[place.shape[0] - 1]
    for which, index, z, row, y, count in found:
        narrow = arrays[which].shape[2]
        column = ((place[z_places[z]] & 1) * 2 + (my_y ^ y)) * narrow
        columns = pl.ds(pl.multiple_of(column, 128), narrow)
        rows[row : row + count, columns] = arrays[which][index, :count]


def all_of(copies):
    for copy in copies:
        copy.start()
    for copy in copies:
        copy.wait()


def weight_copies(place, z, weight, result, sems):
    depth = result.shape[0]
    quarter = depth // 4
    base = pl.multiple_of((place[z] // 2) * depth, depth)
    return [
        pltpu.make_async_copy(
            weight.at[pl.ds(base + q * quarter, quarter)],
            result.at[pl.ds(q * quarter, quarter)],
            sems.at[q],
        )
        for q in range(4)
    ]


def weights_kernel(place, *refs, z):
    w_gate, w_up, gate, up, gate_sems, up_sems = refs[-6:]
    all_of(
        weight_copies(place, z, w_gate, gate, gate_sems)
        + weight_copies(place, z, w_up, up, up_sems)
    )


def first_kernel(place, *refs, found, z_places, following):
    arrays, refs = refs[:-8], refs[-8:]
    w_gate, w_up, later, gate, up, later_rows, rows, later_sems = refs
    later = weight_copies(place, following, later, later_rows, later_sems)
    for copy in later:
        copy.start()
    fill(place, arrays, found, z_places, rows)
    for weight, result in ((w_gate, gate), (w_up, up)):
        for t in range(result.shape[0]):
            tile = slice(t * HIDDEN_TILE, (t + 1) * HIDDEN_TILE)
            result[t] = jnp.dot(rows[...], weight[:, tile], preferred_element_type=jnp.float32)
    for copy in later:
        copy.wait()


def share_column(place, blocks, tails, sems, size):
    experts = place[place.shape[0] - 2]
    expert = place[place.shape[0] - 3]
    copies = []
    for c, block in enumerate(blocks):
        tail = pl.ds(size, tails.shape[1])
        copies.append(pltpu.make_async_copy(block.at[0, tail], tails.at[c], sems.at[c]))
    all_of(copies)
    column = []
    for c in range(2):
        row = lax.broadcasted_iota(jnp.int32, tails.shape[1:], 0)
        mine = (row == expert) | (row == expert + experts)
        shares = jnp.where(mine, tails[c].astype(jnp.float32), 0.0)
        shares = jnp.sum(shares, axis=0, keepdims=True)[:, :size]
        column.append(jnp.broadcast_to(shares, (128, size)).T)
    return jnp.concatenate(column)[:, :1]


def down_copy(place, pair, w_down, tile, sem):
    span = tile.shape[1]
    columns = pl.ds(pl.multiple_of((place[pair[0]] // 2) * span, span), span)
    return pltpu.make_async_copy(w_down.at[:, columns], tile, sem)


def down_products(place, pair, hidden, tile, results):
    my_y = place[place.shape[0] - 1]
    size, narrow = results[0].shape[2:]
    terms = jnp.dot(hidden[...], tile[...], preferred_element_type=jnp.float32)
    terms = terms.astype(jnp.bfloat16)
    for r, result in enumerate(results):
        for z in range(2):
            n = (place[pair[0]] & 1) ^ z
            for y in range(2):
                start = (z * 2 + y) * narrow
                piece = terms[r * size : (r + 1) * size, start : start + narrow]
                result[my_y ^ y, n] = piece


def second_kernel(place, *refs, x, found, z_places, pairs):
    count = 16 if x else 18
    arrays, refs = refs[:-count], refs[-count:]
    w_gate, w_up, gate, up, w_down = refs[:5]
    shares, out = refs[5:7], refs[7:11]
    rows, tails, t_sems, d_sems, first_tile = refs[11:16]
    hidden, second_tile = out[2:] if x else refs[16:]
    downs_in = [
        down_copy(place, pair, w_down, tile, d_sems.at[k])
        for k, (pair, tile) in enumerate(zip(pairs, (first_tile, second_tile)))
    ]
    for copy in downs_in:
        copy.start()
    fill(place, arrays, found, z_places, rows)
    share = 0.5 * share_column(place, shares, tails, t_sems, out[0].shape[2])
    for t in range(gate.shape[0]):
        tile = slice(t * HIDDEN_TILE, (t + 1) * HIDDEN_TILE)
        g = gate[t] + jnp.dot(rows[...], w_gate[:, tile], preferred_element_type=jnp.float32)
        u = up[t] + jnp.dot(rows[...], w_up[:, tile], preferred_element_type=jnp.float32)
        value = (g + g * jnp.tanh(0.5 * g)) * u * share
        hidden[:, tile] = value.astype(jnp.bfloat16)
    downs_in[0].wait()
    down_products(place, pairs[0], hidden, first_tile, out[:2])
    downs_in[1].wait()
    if x == 0:
        down_products(place, pairs[1], hidden, second_tile, out[2:])


def third_kernel(place, hidden, tile, own, sibling, pair):
    down_products(place, pair, hidden, tile, (own, sibling))


def cost(flops, bytes_accessed, transcendentals):
    return pl.CostEstimate(
        flops=flops // SCALE,
        bytes_accessed=bytes_accessed // SCALE,
        transcendentals=transcendentals // SCALE,
    )


def in_hbm(value):
    return pltpu.with_memory_space_constraint(value, pltpu.HBM)


def in_vmem(value):
    return pltpu.with_memory_space_constraint(value, pltpu.VMEM)


ANY = pl.BlockSpec(memory_space=pl.ANY)
SCALARS = pl.BlockSpec(memory_space=pltpu.SMEM)
VMEM = pl.BlockSpec(memory_space=pltpu.VMEM)
SEMS = pltpu.SemaphoreType.DMA


def params(mebibytes):
    return pltpu.CompilerParams(vmem_limit_bytes=mebibytes * 1024 * 1024)


def pair_weights(place, z, w_gate, w_up, narrow, *earlier):
    width, depth = w_gate.shape[1], 4 * narrow
    return pl.pallas_call(
        lambda *refs: weights_kernel(*refs, z=z),
        in_specs=[SCALARS] + [ANY] * (len(earlier) + 2),
        out_specs=[VMEM] * 2,
        scratch_shapes=[SEMS((4,)), SEMS((4,))],
        out_shape=[pltpu.VMEM((depth, width), jnp.bfloat16)] * 2,
        compiler_params=params(2),
        cost_estimate=cost(flops=0, bytes_accessed=8 * depth * width, transcendentals=0),
        name="pair_weights",
    )(place, *earlier, w_gate, w_up)


def first_part(place, x, pair, z_places, weights, following, later):
    arrays, found = pieces(x, pair)
    size, narrow = pair[0][1][0][0].shape[1:]
    depth, width = weights[0].shape
    rows = 2 * size
    sums = pltpu.VMEM((width // HIDDEN_TILE, rows, HIDDEN_TILE), jnp.float32)
    return pl.pallas_call(
        lambda *refs: first_kernel(*refs, found=found, z_places=z_places, following=following),
        in_specs=[SCALARS] + [VMEM] * (len(arrays) + 2) + [ANY],
        out_specs=[VMEM] * 3,
        scratch_shapes=[
            pltpu.VMEM((rows, depth), jnp.bfloat16),
            SEMS((4,)),
        ],
        out_shape=[sums, sums, pltpu.VMEM((depth, width), jnp.bfloat16)],
        compiler_params=params(4),
        cost_estimate=cost(
            flops=4 * rows * depth * width,
            bytes_accessed=4 * depth * width + 2 * rows * depth + 8 * rows * width,
            transcendentals=0,
        ),
        name="first_part",
    )(place, *[in_vmem(v) for v in (*arrays, *weights)], later)


def second_part(place, x, pair, z_places, weights, sums, shares, w_down, pairs):
    arrays, found = pieces(x, pair)
    size, narrow = pair[0][1][0][0].shape[1:]
    depth, width = weights[0].shape
    rows, tail = 2 * size, shares[0].shape[1] - size
    part = pltpu.VMEM((2, 2, size, narrow), jnp.bfloat16)
    hidden, tile = [pltpu.VMEM(v, jnp.bfloat16) for v in ((rows, width), (width, depth))]
    return pl.pallas_call(
        lambda *refs: second_kernel(
            *refs, x=x, found=found, z_places=z_places, pairs=pairs
        ),
        in_specs=[SCALARS] + [VMEM] * (len(arrays) + 4) + [ANY] * 3,
        out_specs=[VMEM] * 4,
        scratch_shapes=[
            pltpu.VMEM((rows, depth), jnp.bfloat16),
            pltpu.VMEM((2, tail, narrow), jnp.bfloat16),
            SEMS((2,)),
            SEMS((2,)),
            tile,
        ]
        + ([] if x else [hidden, tile]),
        out_shape=[part, part] + ([hidden, tile] if x else [part, part]),
        compiler_params=params(9 if x else 13),
        cost_estimate=cost(
            flops=4 * rows * depth * width + 4 * rows * width * depth,
            bytes_accessed=8 * depth * width + 6 * rows * depth + 8 * rows * width,
            transcendentals=rows * width,
        ),
        name="second_part",
    )(place, *[in_vmem(v) for v in (*arrays, *weights, *sums)], w_down, *shares)


def third_part(place, hidden, tile, pair, size):
    rows, width = hidden.shape
    narrow = tile.shape[1] // 4
    return pl.pallas_call(
        lambda *refs: third_kernel(*refs, pair=pair),
        in_specs=[SCALARS, VMEM, VMEM],
        out_specs=[VMEM] * 2,
        out_shape=[pltpu.VMEM((2, 2, size, narrow), jnp.bfloat16)] * 2,
        compiler_params=params(8),
        cost_estimate=cost(
            flops=2 * rows * width * tile.shape[1],
            bytes_accessed=2 * width * (rows + tile.shape[1]) + 2 * rows * tile.shape[1],
            transcendentals=0,
        ),
        name="third_part",
    )(place, in_vmem(hidden), in_vmem(tile))


def shares_of(expert_ids, pair_logits):
    mix = pair_mix(pair_logits)
    labels = jnp.arange(lax.axis_size("expert"), dtype=jnp.int32)
    named = expert_ids[None, :, :] == labels[:, None, None]
    return jnp.sum(jnp.where(named, mix[None], 0.0), axis=2)


def share_rows(shares, narrow):
    high = lax.reduce_precision(shares, 8, 7)
    rows = jnp.concatenate([high, shares - high]).astype(jnp.bfloat16)
    return jnp.pad(rows, ((0, -rows.shape[0] % 16), (0, narrow - rows.shape[1])))


def every_row(tokens, expert_ids, pair_logits, w_gate, w_up, w_down):
    expert, split = lax.axis_index("expert"), lax.axis_index("split")
    size, narrow = tokens.shape
    place = [(split // 2) ^ z for z in range(4)]
    place = jnp.stack(place + [expert, lax.axis_size("expert"), split % 2]).astype(jnp.int32)
    w_gate, w_up, w_down = in_hbm(w_gate), in_hbm(w_up), in_hbm(w_down)

    w_gate, w_up, w_down = in_hbm(w_gate), in_hbm(w_up), in_hbm(w_down)
    z0 = tokens[None]
    z1 = send(z0, z=1)
    own = shares_of(expert_ids, pair_logits)
    block = jnp.concatenate([tokens, share_rows(own, narrow)])[None]
    sent = after(z0, own)
    x0, y0, z2 = send(block, x=1), send(sent, y=1), send(z0, z=2)
    x1, y1 = send(z1, x=1), send(z1, y=1)
    sz0, sz1, sx0, sx1, sy0, sy1 = swapped(block, z1, x0, x1, y0, y1)
    near_weights = pair_weights(place, 0, w_gate, w_up, narrow, x0)
    (x1_, y1_), z2, near_weights = after(((x1, y1), z2, near_weights))
    first, last = relayed([x0, x1_], [y0, y1_])
    z3 = send(z2, z=1)
    x2, y2 = send(z2, x=1), send(z2, y=1)
    near = [[(sz0, 0), (sz1, 0)], [(sx0, 0), (sx1, 0)], [(sy0, 0), (sy1, 0)], None, None]
    *sums_0, far_gate = first_part(place, 0, near, (0, 1), near_weights, 2, w_gate)

    z3, sums_0 = after((z3, sums_0))
    (first, last, x2, y2), sums_0 = after(((first, last, x2, y2), sums_0))
    x3, y3 = send(z3, x=1), send(z3, y=1)
    both_of = lambda v: [(v, 0), (v, 1)]
    near[3:] = [both_of(v) for v in swapped(first, last)]
    sz2, sz3, sx2, sy2 = swapped(z2, z3, x2, y2)
    *sums_1, far_up = first_part(place, 1, near, (0, 1), near_weights, 2, w_up)
    far_weights = far_gate, far_up
    (x3, y3), sums_1 = after(((x3, y3), sums_1))
    first, last = relayed([x2, x3], [y2, y3])
    sx3, sy3 = swapped(x3, y3)
    far = [[(sz2, 0), (sz3, 0)], [(sx2, 0), (sx3, 0)], [(sy2, 0), (sy3, 0)], None, None]
    pairs = (3, 2), (1, 0)
    parts_0 = second_part(place, 0, far, (2, 3), far_weights, sums_0, sz0, w_down, pairs)
    (first, last, sx2, sx3), parts_0 = after(((first, last, sx2, sx3), parts_0))
    far[1] = [(sx2, 0), (sx3, 0)]
    far[3:] = [both_of(v) for v in swapped(first, last)]
    near_0 = parts_0[2], send(parts_0[3], c=1)
    near_0, parts_0 = after((near_0, parts_0), far[3:])
    far_0 = parts_0[0], send(parts_0[1], c=1)
    to_z = total(*[v[:, :1] for v in near_0]).astype(jnp.bfloat16)
    passed_0 = send(to_z, z=1)
    *parts_1, hidden, tile = second_part(
        place, 1, far, (2, 3), far_weights, sums_1, sx0, w_down, pairs
    )
    far_0, parts_1 = after((far_0, parts_1))
    other_1 = send(parts_1[1], c=1)
    last_1 = third_part(place, after(hidden, far_0), tile, pairs[1], size)
    other_1, last_1 = after((other_1, last_1))
    far_1, near_1 = (parts_1[0], other_1), (last_1[0], send(last_1[1], c=1))

    far = far_0, far_1
    corner = diagonal(far)
    to_z = total(*[v[:, :1] for v in near_1]).astype(jnp.bfloat16)
    passed_1 = send(to_z, z=1)
    to_x, to_y = plane_sums(far, *after(corner, to_z))
    from_3 = send(to_x[:1], x=1), send(to_y[:1], y=1)
    here = summed(far, 0, 0)
    to_2 = total(here[:1], *from_3).astype(jnp.bfloat16)
    to_x, to_y = after((to_x, to_y), to_2)
    to_2 = send(to_2, z=1)
    from_2 = send(to_x[1:], x=1), send(to_y[1:], y=1)
    last_block = lambda terms, passed: [v[:, 1:] for v in terms] + [passed]
    near = last_block(near_0, passed_0), last_block(near_1, passed_1)
    corner = diagonal(near)
    to_0 = total(here[1:], *from_2, to_2).astype(jnp.bfloat16)
    to_x, to_y = plane_sums(near, *after(corner, to_0))
    to_0 = send(to_0, z=2)
    from_0 = send(to_x, x=1), send(to_y, y=1)
    return total(summed(near, 0, 0), *from_0, to_0)[0].astype(jnp.bfloat16)


def body(tokens, expert_ids, pair_logits, gate_weight, up_weight, down_weight):
    capacity = 4 * tokens.shape[0] // lax.axis_size("expert")
    arrays = (tokens, expert_ids, pair_logits, gate_weight[0], up_weight[0], down_weight[0])
    splits = lax.axis_size("split")
    if capacity == tokens.shape[0] and splits == 8 and tokens.shape[0] <= tokens.shape[1]:
        return every_row(*arrays)
    return dispatched(*arrays, capacity)


def solution(mesh):
    in_specs = (
        P("expert", "split"),
        P("expert", None),
        P("expert", None),
        P("expert", None, "split"),
        P("expert", None, "split"),
        P("expert", "split", None),
    )
    out_specs = P("expert", "split")
    return jax.shard_map(body, mesh=mesh, in_specs=in_specs, out_specs=out_specs, check_vma=False)
```

```python
import jax
import jax.numpy as jnp
from jax import lax
from jax.experimental import pallas as pl
from jax.experimental.pallas import tpu as pltpu
from jax.sharding import PartitionSpec as P

BOTH = ("expert", "split")
HIDDEN_TILE = 512
SCALE = 4


def pair_mix(pair_logits):
    first = jax.nn.sigmoid(pair_logits[:, 0] - pair_logits[:, 1])
    return jnp.stack([first, 1.0 - first], axis=1)


def dispatched(tokens, expert_ids, pair_logits, w_gate, w_up, w_down, capacity):
    experts = lax.axis_size("expert")
    tok_rows, narrow = tokens.shape
    flat = expert_ids.reshape(-1)
    labels = jnp.arange(experts, dtype=jnp.int32)
    onehot = (flat[:, None] == labels[None, :]).astype(jnp.int32)
    before = jnp.cumsum(onehot, axis=0) - onehot
    slot = jnp.sum(before * onehot, axis=1)
    dest = flat * capacity + slot
    mix = pair_mix(pair_logits).reshape(-1)
    select = (jnp.arange(experts * capacity, dtype=jnp.int32)[:, None] == dest[None, :]).astype(
        jnp.bfloat16
    )
    doubled = jnp.repeat(tokens, 2, axis=0)
    packed = jnp.dot(select, doubled, preferred_element_type=jnp.float32).astype(jnp.bfloat16)
    sending = packed.reshape(experts, capacity, narrow)
    arrived = lax.all_to_all(sending, "expert", split_axis=0, concat_axis=0, tiled=True).reshape(
        experts * capacity, narrow
    )
    piece = lax.all_gather(arrived, "split", axis=1, tiled=True)
    gate = jnp.dot(piece, w_gate, preferred_element_type=jnp.float32)
    up_part = jnp.dot(piece, w_up, preferred_element_type=jnp.float32)
    hidden = (jax.nn.silu(gate) * up_part).astype(jnp.bfloat16)
    terms = jnp.dot(hidden, w_down, preferred_element_type=jnp.float32)
    result = lax.psum_scatter(
        terms.astype(jnp.bfloat16), "split", scatter_dimension=1, tiled=True
    ).astype(jnp.float32)
    narrow = result.shape[1]
    returned = lax.all_to_all(
        result.reshape(experts, capacity, narrow).astype(jnp.bfloat16),
        "expert",
        split_axis=0,
        concat_axis=0,
        tiled=True,
    ).astype(jnp.float32)
    returned = returned.reshape(experts * capacity, narrow)
    picked = returned[dest] * mix[:, None]
    mixed = picked.reshape(tok_rows, 2, narrow).sum(axis=1)
    return mixed.astype(jnp.bfloat16)


def send(value, x=0, c=0, z=0, y=0):
    experts, splits = lax.axis_size("expert"), lax.axis_size("split")
    flip_expert, flip_split = x * 2 + c, z * 2 + y
    pairs = [
        (e * splits + s, (e ^ flip_expert) * splits + (s ^ flip_split))
        for e in range(experts)
        for s in range(splits)
    ]
    return lax.ppermute(value, BOTH, pairs)


def after(value, *earlier):
    return lax.optimization_barrier((value, earlier))[0]


def relayed(over_x, over_y):
    half = over_y[0].shape[1] // 2
    first = jnp.concatenate([v[:, :half] for v in over_y])
    last = jnp.concatenate([v[:, half : 2 * half] for v in over_x])
    return send(first, x=1), send(last, y=1)


def swapped(*blocks):
    return [(v, send(v, c=1)) for v in blocks]


def summed(terms, y, x, rows=slice(None)):
    return total(*[term[y, :, rows] for term in terms[x]])


def diagonal(terms):
    half = terms[0][0].shape[2] // 2
    first = summed(terms, 1, 1, slice(0, half)).astype(jnp.bfloat16)
    last = summed(terms, 1, 1, slice(half, 2 * half)).astype(jnp.bfloat16)
    return send(first, x=1), send(last, y=1)


def plane_sums(terms, first, last):
    half = terms[0][0].shape[2] // 2
    first, last = first.astype(jnp.float32), last.astype(jnp.float32)
    to_x = summed(terms, 0, 1) + jnp.pad(last, ((0, 0), (half, 0), (0, 0)))
    to_y = summed(terms, 1, 0) + jnp.pad(first, ((0, 0), (0, half), (0, 0)))
    return to_x.astype(jnp.bfloat16), to_y.astype(jnp.bfloat16)


def total(*terms):
    result = terms[0].astype(jnp.float32)
    for term in terms[1:]:
        result = result + term.astype(jnp.float32)
    return result


def pieces(x, pair):
    blocks, over_x, over_y, first, last = pair
    size = blocks[0][0][0].shape[1]
    arrays, found = [], []
    for z in range(2):
        for c in range(2):
            parts = [(blocks[z], 0, 0), (over_y[z], 0, 1)]
            if x:
                parts = [(over_x[z], 0, 0), (first[z], 0, 1), (last[z], size // 2, 1)]
            for (array, index), row, y in parts:
                array = array[c]
                if not any(array is v for v in arrays):
                    arrays.append(array)
                place = [i for i, v in enumerate(arrays) if v is array][0]
                found.append((place, index, z, c * size + row, y, min(size, array.shape[1])))
    return arrays, found


def fill(place, arrays, found, z_places, rows, sems):
    my_y = place[place.shape[0] - 1]
    copies = []
    for i, (which, index, z, row, y, count) in enumerate(found):
        source = arrays[which].at[index, pl.ds(0, count)]
        column = ((place[z_places[z]] & 1) * 2 + (my_y ^ y)) * source.shape[1]
        columns = pl.ds(pl.multiple_of(column, 128), source.shape[1])
        target = rows.at[pl.ds(row, count), columns]
        copies.append(pltpu.make_async_copy(source, target, sems.at[i]))
    return copies


def all_of(copies):
    for copy in copies:
        copy.start()
    for copy in copies:
        copy.wait()


def weight_copies(place, z, weight, result, sems):
    depth = result.shape[0]
    quarter = depth // 4
    base = pl.multiple_of((place[z] // 2) * depth, depth)
    return [
        pltpu.make_async_copy(
            weight.at[pl.ds(base + q * quarter, quarter)],
            result.at[pl.ds(q * quarter, quarter)],
            sems.at[q],
        )
        for q in range(4)
    ]


def weights_kernel(place, *refs, z):
    w_gate, w_up, gate, up, gate_sems, up_sems = refs[-6:]
    all_of(
        weight_copies(place, z, w_gate, gate, gate_sems)
        + weight_copies(place, z, w_up, up, up_sems)
    )


def first_kernel(place, *refs, found, z_places, following):
    arrays, refs = refs[:-9], refs[-9:]
    w_gate, w_up, later, gate, up, later_rows, rows, sems, later_sems = refs
    later = weight_copies(place, following, later, later_rows, later_sems)
    copies = fill(place, arrays, found, z_places, rows, sems)
    for copy in copies + later:
        copy.start()
    for copy in copies:
        copy.wait()
    for weight, result in ((w_gate, gate), (w_up, up)):
        for t in range(result.shape[0]):
            tile = slice(t * HIDDEN_TILE, (t + 1) * HIDDEN_TILE)
            result[t] = jnp.dot(rows[...], weight[:, tile], preferred_element_type=jnp.float32)
    for copy in later:
        copy.wait()


def share_column(place, blocks, tails, sems, size):
    experts = place[place.shape[0] - 2]
    expert = place[place.shape[0] - 3]
    copies = []
    for c, block in enumerate(blocks):
        tail = pl.ds(size, tails.shape[1])
        copies.append(pltpu.make_async_copy(block.at[0, tail], tails.at[c], sems.at[c]))
    all_of(copies)
    column = []
    for c in range(2):
        row = lax.broadcasted_iota(jnp.int32, tails.shape[1:], 0)
        mine = (row == expert) | (row == expert + experts)
        shares = jnp.where(mine, tails[c].astype(jnp.float32), 0.0)
        shares = jnp.sum(shares, axis=0, keepdims=True)[:, :size]
        column.append(jnp.broadcast_to(shares, (128, size)).T)
    return jnp.concatenate(column)[:, :1]


def down_copy(place, pair, w_down, tile, sem):
    span = tile.shape[1]
    columns = pl.ds(pl.multiple_of((place[pair[0]] // 2) * span, span), span)
    return pltpu.make_async_copy(w_down.at[:, columns], tile, sem)


def down_products(place, pair, hidden, tile, results):
    my_y = place[place.shape[0] - 1]
    size, narrow = results[0].shape[2:]
    terms = jnp.dot(hidden[...], tile[...], preferred_element_type=jnp.float32)
    terms = terms.astype(jnp.bfloat16)
    for r, result in enumerate(results):
        for z in range(2):
            n = (place[pair[0]] & 1) ^ z
            for y in range(2):
                start = (z * 2 + y) * narrow
                piece = terms[r * size : (r + 1) * size, start : start + narrow]
                result[my_y ^ y, n] = piece


def second_kernel(place, *refs, x, found, z_places, pairs):
    count = 16 if x else 17
    arrays, refs = refs[:-count], refs[-count:]
    w_gate, w_up, gate, up, w_down = refs[:5]
    shares, results, hidden = refs[5:7], refs[7:9], refs[9]
    rows, tails, sems, t_sems, d_sems, tile = refs[-6:]
    copies = fill(place, arrays, found, z_places, rows, sems)
    downs_in = [down_copy(place, pairs[0], w_down, tile, d_sems.at[0])]
    if x == 0:
        downs_in.append(down_copy(place, pairs[1], w_down, refs[10], d_sems.at[1]))
    for copy in copies + downs_in:
        copy.start()
    share = 0.5 * share_column(place, shares, tails, t_sems, results[0].shape[2])
    for copy in copies:
        copy.wait()
    for t in range(gate.shape[0]):
        span = slice(t * HIDDEN_TILE, (t + 1) * HIDDEN_TILE)
        g = gate[t] + jnp.dot(rows[...], w_gate[:, span], preferred_element_type=jnp.float32)
        u = up[t] + jnp.dot(rows[...], w_up[:, span], preferred_element_type=jnp.float32)
        value = (g + g * jnp.tanh(0.5 * g)) * u * share
        hidden[:, span] = value.astype(jnp.bfloat16)
    downs_in[0].wait()
    down_products(place, pairs[0], hidden, tile, results)
    for copy in downs_in[1:]:
        copy.wait()


def third_kernel(place, hidden, tile, own, sibling, pair):
    down_products(place, pair, hidden, tile, (own, sibling))


def cost(flops, bytes_accessed, transcendentals):
    return pl.CostEstimate(
        flops=flops // SCALE,
        bytes_accessed=bytes_accessed // SCALE,
        transcendentals=transcendentals // SCALE,
    )


def in_hbm(value):
    return pltpu.with_memory_space_constraint(value, pltpu.HBM)


def in_vmem(value):
    return pltpu.with_memory_space_constraint(value, pltpu.VMEM)


ANY = pl.BlockSpec(memory_space=pl.ANY)
SCALARS = pl.BlockSpec(memory_space=pltpu.SMEM)
VMEM = pl.BlockSpec(memory_space=pltpu.VMEM)
SEMS = pltpu.SemaphoreType.DMA


def params(mebibytes):
    return pltpu.CompilerParams(vmem_limit_bytes=mebibytes * 1024 * 1024)


def pair_weights(place, z, w_gate, w_up, narrow, *earlier):
    width, depth = w_gate.shape[1], 4 * narrow
    return pl.pallas_call(
        lambda *refs: weights_kernel(*refs, z=z),
        in_specs=[SCALARS] + [ANY] * (len(earlier) + 2),
        out_specs=[VMEM] * 2,
        scratch_shapes=[SEMS((4,)), SEMS((4,))],
        out_shape=[pltpu.VMEM((depth, width), jnp.bfloat16)] * 2,
        compiler_params=params(2),
        cost_estimate=cost(flops=0, bytes_accessed=8 * depth * width, transcendentals=0),
        name="pair_weights",
    )(place, *earlier, w_gate, w_up)


def first_part(place, x, pair, z_places, weights, following, later):
    arrays, found = pieces(x, pair)
    size, narrow = pair[0][0][0][0].shape[1:]
    depth, width = weights[0].shape
    rows = 2 * size
    sums = pltpu.VMEM((width // HIDDEN_TILE, rows, HIDDEN_TILE), jnp.float32)
    return pl.pallas_call(
        lambda *refs: first_kernel(*refs, found=found, z_places=z_places, following=following),
        in_specs=[SCALARS] + [ANY] * len(arrays) + [VMEM, VMEM, ANY],
        out_specs=[VMEM] * 3,
        scratch_shapes=[
            pltpu.VMEM((rows, depth), jnp.bfloat16),
            SEMS((len(found),)),
            SEMS((4,)),
        ],
        out_shape=[sums, sums, pltpu.VMEM((depth, width), jnp.bfloat16)],
        compiler_params=params(4),
        cost_estimate=cost(
            flops=4 * rows * depth * width,
            bytes_accessed=4 * depth * width + 2 * rows * depth + 8 * rows * width,
            transcendentals=0,
        ),
        name="first_part",
    )(place, *arrays, *[in_vmem(v) for v in weights], later)


def second_part(place, x, pair, z_places, weights, sums, shares, w_down, pairs):
    arrays, found = pieces(x, pair)
    size, narrow = pair[0][0][0][0].shape[1:]
    depth, width = weights[0].shape
    rows, tail = 2 * size, shares[0].shape[1] - size
    part = pltpu.VMEM((2, 2, size, narrow), jnp.bfloat16)
    hidden, tile = [pltpu.VMEM(v, jnp.bfloat16) for v in ((rows, width), (width, depth))]
    return pl.pallas_call(
        lambda *refs: second_kernel(
            *refs, x=x, found=found, z_places=z_places, pairs=pairs
        ),
        in_specs=[SCALARS] + [ANY] * len(arrays) + [VMEM] * 4 + [ANY] * 3,
        out_specs=[VMEM] * (3 if x else 4),
        scratch_shapes=[
            pltpu.VMEM((rows, depth), jnp.bfloat16),
            pltpu.VMEM((2, tail, narrow), jnp.bfloat16),
            SEMS((len(found),)),
            SEMS((2,)),
            SEMS((2,)),
            tile,
        ],
        out_shape=[part, part, hidden] + ([] if x else [tile]),
        compiler_params=params(9),
        cost_estimate=cost(
            flops=4 * rows * depth * width + 4 * rows * width * depth,
            bytes_accessed=8 * depth * width + 6 * rows * depth + 8 * rows * width,
            transcendentals=rows * width,
        ),
        name="second_part",
    )(place, *arrays, *[in_vmem(v) for v in (*weights, *sums)], w_down, *shares)


def third_part(place, hidden, tile, pair, size):
    rows, width = hidden.shape
    narrow = tile.shape[1] // 4
    return pl.pallas_call(
        lambda *refs: third_kernel(*refs, pair=pair),
        in_specs=[SCALARS, VMEM, VMEM],
        out_specs=[VMEM] * 2,
        out_shape=[pltpu.VMEM((2, 2, size, narrow), jnp.bfloat16)] * 2,
        compiler_params=params(8),
        cost_estimate=cost(
            flops=2 * rows * width * tile.shape[1],
            bytes_accessed=2 * width * (rows + tile.shape[1]) + 2 * rows * tile.shape[1],
            transcendentals=0,
        ),
        name="third_part",
    )(place, in_vmem(hidden), in_vmem(tile))


def shares_of(expert_ids, pair_logits):
    mix = pair_mix(pair_logits)
    labels = jnp.arange(lax.axis_size("expert"), dtype=jnp.int32)
    named = expert_ids[None, :, :] == labels[:, None, None]
    return jnp.sum(jnp.where(named, mix[None], 0.0), axis=2)


def share_rows(shares, narrow):
    high = lax.reduce_precision(shares, 8, 7)
    rows = jnp.concatenate([high, shares - high]).astype(jnp.bfloat16)
    return jnp.pad(rows, ((0, -rows.shape[0] % 16), (0, narrow - rows.shape[1])))


def every_row(tokens, expert_ids, pair_logits, w_gate, w_up, w_down):
    expert, split = lax.axis_index("expert"), lax.axis_index("split")
    size, narrow = tokens.shape
    place = [(split // 2) ^ z for z in range(4)]
    place = jnp.stack(place + [expert, lax.axis_size("expert"), split % 2]).astype(jnp.int32)
    w_gate, w_up, w_down = in_hbm(w_gate), in_hbm(w_up), in_hbm(w_down)

    w_gate, w_up, w_down = in_hbm(w_gate), in_hbm(w_up), in_hbm(w_down)
    z0 = tokens[None]
    z1 = send(z0, z=1)
    own = shares_of(expert_ids, pair_logits)
    sent = after(z0, own)
    x0, y0, z2 = send(sent, x=1), send(sent, y=1), send(sent, z=2)
    tail = share_rows(own, narrow)[None]
    x1, y1 = send(z1, x=1), send(z1, y=1)
    sz0, sz1, sx0, sx1, sy0, sy1 = swapped(z0, z1, x0, x1, y0, y1)
    near_weights = pair_weights(place, 0, w_gate, w_up, narrow, x0)
    (x1_, y1_), z2, near_weights, tail = after(((x1, y1), z2, near_weights, tail))
    first, last = relayed([x0, x1_], [y0, y1_])
    z3 = send(z2, z=1)
    x2, y2 = send(z2, x=1), send(z2, y=1)
    near = [[(sz0, 0), (sz1, 0)], [(sx0, 0), (sx1, 0)], [(sy0, 0), (sy1, 0)], None, None]
    *sums_0, far_gate = first_part(place, 0, near, (0, 1), near_weights, 2, w_gate)

    z3, sums_0 = after((z3, sums_0))
    (first, last, x2, y2), sums_0 = after(((first, last, x2, y2), sums_0))
    block = jnp.concatenate([z3, tail], axis=1)
    x3, y3 = send(block, x=1), send(z3, y=1)
    both_of = lambda v: [(v, 0), (v, 1)]
    near[3:] = [both_of(v) for v in swapped(first, last)]
    sz2, sz3, sx2, sy2 = swapped(z2, block, x2, y2)
    *sums_1, far_up = first_part(place, 1, near, (0, 1), near_weights, 2, w_up)
    far_weights = far_gate, far_up
    (x3, y3), sums_1 = after(((x3, y3), sums_1))
    first, last = relayed([x2, x3], [y2, y3])
    sx3, sy3 = swapped(x3, y3)
    far = [[(sz2, 0), (sz3, 0)], [(sx2, 0), (sx3, 0)], [(sy2, 0), (sy3, 0)], None, None]
    pairs = (3, 2), (1, 0)
    *parts_0, hidden, tile = second_part(
        place, 0, far, (2, 3), far_weights, sums_0, sz3, w_down, pairs
    )
    (first, last, sx2, sx3), parts_0 = after(((first, last, sx2, sx3), parts_0))
    far[1] = [(sx2, 0), (sx3, 0)]
    corners = swapped(first, last)
    last_0 = third_part(place, hidden, tile, pairs[1], size)
    corners, last_0 = after((corners, last_0))
    far[3:] = [both_of(v) for v in corners]
    far_0 = parts_0[0], send(parts_0[1], c=1)
    near_0 = last_0[0], send(last_0[1], c=1)
    *parts_1, hidden = second_part(
        place, 1, far, (2, 3), far_weights, sums_1, sx3, w_down, pairs
    )
    far_0, near_0, parts_1 = after((far_0, near_0, parts_1))
    to_z = total(*[v[:, :1] for v in near_0]).astype(jnp.bfloat16)
    passed_0 = send(to_z, z=1)
    other_1 = send(parts_1[1], c=1)
    last_1 = third_part(place, after(hidden, far_0), tile, pairs[1], size)
    other_1, last_1 = after((other_1, last_1))
    far_1, near_1 = (parts_1[0], other_1), (last_1[0], send(last_1[1], c=1))

    far = far_0, far_1
    corner = diagonal(far)
    to_z = total(*[v[:, :1] for v in near_1]).astype(jnp.bfloat16)
    passed_1 = send(to_z, z=1)
    to_x, to_y = plane_sums(far, *after(corner, to_z))
    from_3 = send(to_x[:1], x=1), send(to_y[:1], y=1)
    here = summed(far, 0, 0)
    to_2 = total(here[:1], *from_3).astype(jnp.bfloat16)
    to_x, to_y = after((to_x, to_y), to_2)
    to_2 = send(to_2, z=1)
    from_2 = send(to_x[1:], x=1), send(to_y[1:], y=1)
    last_block = lambda terms, passed: [v[:, 1:] for v in terms] + [passed]
    near = last_block(near_0, passed_0), last_block(near_1, passed_1)
    corner = diagonal(near)
    to_0 = total(here[1:], *from_2, to_2).astype(jnp.bfloat16)
    to_x, to_y = plane_sums(near, *after(corner, to_0))
    to_0 = send(to_0, z=2)
    from_0 = send(to_x, x=1), send(to_y, y=1)
    return total(summed(near, 0, 0), *from_0, to_0)[0].astype(jnp.bfloat16)


def body(tokens, expert_ids, pair_logits, gate_weight, up_weight, down_weight):
    capacity = 4 * tokens.shape[0] // lax.axis_size("expert")
    arrays = (tokens, expert_ids, pair_logits, gate_weight[0], up_weight[0], down_weight[0])
    splits = lax.axis_size("split")
    if capacity == tokens.shape[0] and splits == 8 and tokens.shape[0] <= tokens.shape[1]:
        return every_row(*arrays)
    return dispatched(*arrays, capacity)


def solution(mesh):
    in_specs = (
        P("expert", "split"),
        P("expert", None),
        P("expert", None),
        P("expert", None, "split"),
        P("expert", None, "split"),
        P("expert", "split", None),
    )
    out_specs = P("expert", "split")
    return jax.shard_map(body, mesh=mesh, in_specs=in_specs, out_specs=out_specs, check_vma=False)
```

```python
import jax
import jax.numpy as jnp
from jax import lax
from jax.experimental import pallas as pl
from jax.experimental.pallas import tpu as pltpu
from jax.sharding import PartitionSpec as P

BOTH = ("expert", "split")
HIDDEN_TILE = 512
SCALE = 4


def pair_mix(pair_logits):
    first = jax.nn.sigmoid(pair_logits[:, 0] - pair_logits[:, 1])
    return jnp.stack([first, 1.0 - first], axis=1)


def dispatched(tokens, expert_ids, pair_logits, w_gate, w_up, w_down, capacity):
    experts = lax.axis_size("expert")
    tok_rows, narrow = tokens.shape
    flat = expert_ids.reshape(-1)
    labels = jnp.arange(experts, dtype=jnp.int32)
    onehot = (flat[:, None] == labels[None, :]).astype(jnp.int32)
    before = jnp.cumsum(onehot, axis=0) - onehot
    slot = jnp.sum(before * onehot, axis=1)
    dest = flat * capacity + slot
    mix = pair_mix(pair_logits).reshape(-1)
    select = (jnp.arange(experts * capacity, dtype=jnp.int32)[:, None] == dest[None, :]).astype(
        jnp.bfloat16
    )
    doubled = jnp.repeat(tokens, 2, axis=0)
    packed = jnp.dot(select, doubled, preferred_element_type=jnp.float32).astype(jnp.bfloat16)
    sending = packed.reshape(experts, capacity, narrow)
    arrived = lax.all_to_all(sending, "expert", split_axis=0, concat_axis=0, tiled=True).reshape(
        experts * capacity, narrow
    )
    piece = lax.all_gather(arrived, "split", axis=1, tiled=True)
    gate = jnp.dot(piece, w_gate, preferred_element_type=jnp.float32)
    up_part = jnp.dot(piece, w_up, preferred_element_type=jnp.float32)
    hidden = (jax.nn.silu(gate) * up_part).astype(jnp.bfloat16)
    terms = jnp.dot(hidden, w_down, preferred_element_type=jnp.float32)
    result = lax.psum_scatter(
        terms.astype(jnp.bfloat16), "split", scatter_dimension=1, tiled=True
    ).astype(jnp.float32)
    narrow = result.shape[1]
    returned = lax.all_to_all(
        result.reshape(experts, capacity, narrow).astype(jnp.bfloat16),
        "expert",
        split_axis=0,
        concat_axis=0,
        tiled=True,
    ).astype(jnp.float32)
    returned = returned.reshape(experts * capacity, narrow)
    picked = returned[dest] * mix[:, None]
    mixed = picked.reshape(tok_rows, 2, narrow).sum(axis=1)
    return mixed.astype(jnp.bfloat16)


def send(value, x=0, c=0, z=0, y=0):
    experts, splits = lax.axis_size("expert"), lax.axis_size("split")
    flip_expert, flip_split = x * 2 + c, z * 2 + y
    pairs = [
        (e * splits + s, (e ^ flip_expert) * splits + (s ^ flip_split))
        for e in range(experts)
        for s in range(splits)
    ]
    return lax.ppermute(value, BOTH, pairs)


def after(value, *earlier):
    return lax.optimization_barrier((value, earlier))[0]


def relayed(over_x, over_y):
    half = over_y[0].shape[1] // 2
    first = jnp.concatenate([v[:, :half] for v in over_y])
    last = jnp.concatenate([v[:, half : 2 * half] for v in over_x])
    return send(first, x=1), send(last, y=1)


def swapped(*blocks):
    return [(v, send(v, c=1)) for v in blocks]


def summed(terms, y, x, rows=slice(None)):
    return total(*[term[y, :, rows] for term in terms[x]])


def diagonal(terms):
    half = terms[0][0].shape[2] // 2
    first = summed(terms, 1, 1, slice(0, half)).astype(jnp.bfloat16)
    last = summed(terms, 1, 1, slice(half, 2 * half)).astype(jnp.bfloat16)
    return send(first, x=1), send(last, y=1)


def plane_sums(terms, first, last):
    half = terms[0][0].shape[2] // 2
    first, last = first.astype(jnp.float32), last.astype(jnp.float32)
    to_x = summed(terms, 0, 1) + jnp.pad(last, ((0, 0), (half, 0), (0, 0)))
    to_y = summed(terms, 1, 0) + jnp.pad(first, ((0, 0), (0, half), (0, 0)))
    return to_x.astype(jnp.bfloat16), to_y.astype(jnp.bfloat16)


def total(*terms):
    result = terms[0].astype(jnp.float32)
    for term in terms[1:]:
        result = result + term.astype(jnp.float32)
    return result


def pieces(x, pair):
    blocks, over_x, over_y, first, last = pair
    size = blocks[1][0][0].shape[1]
    arrays, found = [], []
    for z in range(2):
        for c in range(2):
            parts = [(blocks[z], 0, 0), (over_y[z], 0, 1)]
            if x:
                parts = [(over_x[z], 0, 0), (first[z], 0, 1), (last[z], size // 2, 1)]
            for (array, index), row, y in parts:
                array = array[c]
                if not any(array is v for v in arrays):
                    arrays.append(array)
                place = [i for i, v in enumerate(arrays) if v is array][0]
                found.append((place, index, z, c * size + row, y, min(size, array.shape[1])))
    return arrays, found


def fill(place, arrays, found, z_places, rows, sems):
    my_y = place[place.shape[0] - 1]
    copies = []
    for i, (which, index, z, row, y, count) in enumerate(found):
        source = arrays[which].at[index, pl.ds(0, count)]
        column = ((place[z_places[z]] & 1) * 2 + (my_y ^ y)) * source.shape[1]
        columns = pl.ds(pl.multiple_of(column, 128), source.shape[1])
        target = rows.at[pl.ds(row, count), columns]
        copies.append(pltpu.make_async_copy(source, target, sems.at[i]))
    return copies


def all_of(copies):
    for copy in copies:
        copy.start()
    for copy in copies:
        copy.wait()


def weight_copies(place, z, weight, result, sems):
    depth = result.shape[0]
    quarter = depth // 4
    base = pl.multiple_of((place[z] // 2) * depth, depth)
    return [
        pltpu.make_async_copy(
            weight.at[pl.ds(base + q * quarter, quarter)],
            result.at[pl.ds(q * quarter, quarter)],
            sems.at[q],
        )
        for q in range(4)
    ]


def weights_kernel(place, *refs, z):
    w_gate, w_up, gate, up, gate_sems, up_sems = refs[-6:]
    all_of(
        weight_copies(place, z, w_gate, gate, gate_sems)
        + weight_copies(place, z, w_up, up, up_sems)
    )


def first_kernel(place, *refs, found, z_places, following):
    arrays, refs = refs[:-9], refs[-9:]
    w_gate, w_up, later, gate, up, later_rows, rows, sems, later_sems = refs
    later = weight_copies(place, following, later, later_rows, later_sems)
    copies = fill(place, arrays, found, z_places, rows, sems)
    for copy in copies + later:
        copy.start()
    for copy in copies:
        copy.wait()
    for weight, result in ((w_gate, gate), (w_up, up)):
        for t in range(result.shape[0]):
            tile = slice(t * HIDDEN_TILE, (t + 1) * HIDDEN_TILE)
            result[t] = jnp.dot(rows[...], weight[:, tile], preferred_element_type=jnp.float32)
    for copy in later:
        copy.wait()


def share_column(place, blocks, tails, sems, size):
    experts = place[place.shape[0] - 2]
    expert = place[place.shape[0] - 3]
    copies = []
    for c, block in enumerate(blocks):
        tail = pl.ds(size, tails.shape[1])
        copies.append(pltpu.make_async_copy(block.at[0, tail], tails.at[c], sems.at[c]))
    all_of(copies)
    column = []
    for c in range(2):
        row = lax.broadcasted_iota(jnp.int32, tails.shape[1:], 0)
        mine = (row == expert) | (row == expert + experts)
        shares = jnp.where(mine, tails[c].astype(jnp.float32), 0.0)
        shares = jnp.sum(shares, axis=0, keepdims=True)[:, :size]
        column.append(jnp.broadcast_to(shares, (128, size)).T)
    return jnp.concatenate(column)[:, :1]


def down_copy(place, pair, w_down, tile, sem):
    span = tile.shape[1]
    columns = pl.ds(pl.multiple_of((place[pair[0]] // 2) * span, span), span)
    return pltpu.make_async_copy(w_down.at[:, columns], tile, sem)


def down_products(place, pair, hidden, tile, results):
    my_y = place[place.shape[0] - 1]
    size, narrow = results[0].shape[2:]
    terms = jnp.dot(hidden[...], tile[...], preferred_element_type=jnp.float32)
    terms = terms.astype(jnp.bfloat16)
    for r, result in enumerate(results):
        for z in range(2):
            n = (place[pair[0]] & 1) ^ z
            for y in range(2):
                start = (z * 2 + y) * narrow
                piece = terms[r * size : (r + 1) * size, start : start + narrow]
                result[my_y ^ y, n] = piece


def second_kernel(place, *refs, x, found, z_places, pairs):
    count = 16 if x else 17
    arrays, refs = refs[:-count], refs[-count:]
    w_gate, w_up, gate, up, w_down = refs[:5]
    shares, results, hidden = refs[5:7], refs[7:9], refs[9]
    rows, tails, sems, t_sems, d_sems, tile = refs[-6:]
    copies = fill(place, arrays, found, z_places, rows, sems)
    downs_in = [down_copy(place, pairs[0], w_down, tile, d_sems.at[0])]
    if x == 0:
        downs_in.append(down_copy(place, pairs[1], w_down, refs[10], d_sems.at[1]))
    for copy in copies + downs_in:
        copy.start()
    share = 0.5 * share_column(place, shares, tails, t_sems, results[0].shape[2])
    for copy in copies:
        copy.wait()
    for t in range(gate.shape[0]):
        span = slice(t * HIDDEN_TILE, (t + 1) * HIDDEN_TILE)
        g = gate[t] + jnp.dot(rows[...], w_gate[:, span], preferred_element_type=jnp.float32)
        u = up[t] + jnp.dot(rows[...], w_up[:, span], preferred_element_type=jnp.float32)
        value = (g + g * jnp.tanh(0.5 * g)) * u * share
        hidden[:, span] = value.astype(jnp.bfloat16)
    downs_in[0].wait()
    down_products(place, pairs[0], hidden, tile, results)
    for copy in downs_in[1:]:
        copy.wait()


def third_kernel(place, hidden, tile, own, sibling, pair):
    down_products(place, pair, hidden, tile, (own, sibling))


def cost(flops, bytes_accessed, transcendentals):
    return pl.CostEstimate(
        flops=flops // SCALE,
        bytes_accessed=bytes_accessed // SCALE,
        transcendentals=transcendentals // SCALE,
    )


def in_hbm(value):
    return pltpu.with_memory_space_constraint(value, pltpu.HBM)


def in_vmem(value):
    return pltpu.with_memory_space_constraint(value, pltpu.VMEM)


ANY = pl.BlockSpec(memory_space=pl.ANY)
SCALARS = pl.BlockSpec(memory_space=pltpu.SMEM)
VMEM = pl.BlockSpec(memory_space=pltpu.VMEM)
SEMS = pltpu.SemaphoreType.DMA


def params(mebibytes):
    return pltpu.CompilerParams(vmem_limit_bytes=mebibytes * 1024 * 1024)


def pair_weights(place, z, w_gate, w_up, narrow, *earlier):
    width, depth = w_gate.shape[1], 4 * narrow
    return pl.pallas_call(
        lambda *refs: weights_kernel(*refs, z=z),
        in_specs=[SCALARS] + [ANY] * (len(earlier) + 2),
        out_specs=[VMEM] * 2,
        scratch_shapes=[SEMS((4,)), SEMS((4,))],
        out_shape=[pltpu.VMEM((depth, width), jnp.bfloat16)] * 2,
        compiler_params=params(2),
        cost_estimate=cost(flops=0, bytes_accessed=8 * depth * width, transcendentals=0),
        name="pair_weights",
    )(place, *earlier, w_gate, w_up)


def first_part(place, x, pair, z_places, weights, following, later):
    arrays, found = pieces(x, pair)
    size, narrow = pair[0][1][0][0].shape[1:]
    depth, width = weights[0].shape
    rows = 2 * size
    sums = pltpu.VMEM((width // HIDDEN_TILE, rows, HIDDEN_TILE), jnp.float32)
    return pl.pallas_call(
        lambda *refs: first_kernel(*refs, found=found, z_places=z_places, following=following),
        in_specs=[SCALARS] + [ANY] * len(arrays) + [VMEM, VMEM, ANY],
        out_specs=[VMEM] * 3,
        scratch_shapes=[
            pltpu.VMEM((rows, depth), jnp.bfloat16),
            SEMS((len(found),)),
            SEMS((4,)),
        ],
        out_shape=[sums, sums, pltpu.VMEM((depth, width), jnp.bfloat16)],
        compiler_params=params(4),
        cost_estimate=cost(
            flops=4 * rows * depth * width,
            bytes_accessed=4 * depth * width + 2 * rows * depth + 8 * rows * width,
            transcendentals=0,
        ),
        name="first_part",
    )(place, *arrays, *[in_vmem(v) for v in weights], later)


def second_part(place, x, pair, z_places, weights, sums, shares, w_down, pairs):
    arrays, found = pieces(x, pair)
    size, narrow = pair[0][1][0][0].shape[1:]
    depth, width = weights[0].shape
    rows, tail = 2 * size, shares[0].shape[1] - size
    part = pltpu.VMEM((2, 2, size, narrow), jnp.bfloat16)
    hidden, tile = [pltpu.VMEM(v, jnp.bfloat16) for v in ((rows, width), (width, depth))]
    return pl.pallas_call(
        lambda *refs: second_kernel(
            *refs, x=x, found=found, z_places=z_places, pairs=pairs
        ),
        in_specs=[SCALARS] + [ANY] * len(arrays) + [VMEM] * 4 + [ANY] * 3,
        out_specs=[VMEM] * (3 if x else 4),
        scratch_shapes=[
            pltpu.VMEM((rows, depth), jnp.bfloat16),
            pltpu.VMEM((2, tail, narrow), jnp.bfloat16),
            SEMS((len(found),)),
            SEMS((2,)),
            SEMS((2,)),
            tile,
        ],
        out_shape=[part, part, hidden] + ([] if x else [tile]),
        compiler_params=params(9),
        cost_estimate=cost(
            flops=4 * rows * depth * width + 4 * rows * width * depth,
            bytes_accessed=8 * depth * width + 6 * rows * depth + 8 * rows * width,
            transcendentals=rows * width,
        ),
        name="second_part",
    )(place, *arrays, *[in_vmem(v) for v in (*weights, *sums)], w_down, *shares)


def third_part(place, hidden, tile, pair, size):
    rows, width = hidden.shape
    narrow = tile.shape[1] // 4
    return pl.pallas_call(
        lambda *refs: third_kernel(*refs, pair=pair),
        in_specs=[SCALARS, VMEM, VMEM],
        out_specs=[VMEM] * 2,
        out_shape=[pltpu.VMEM((2, 2, size, narrow), jnp.bfloat16)] * 2,
        compiler_params=params(8),
        cost_estimate=cost(
            flops=2 * rows * width * tile.shape[1],
            bytes_accessed=2 * width * (rows + tile.shape[1]) + 2 * rows * tile.shape[1],
            transcendentals=0,
        ),
        name="third_part",
    )(place, in_vmem(hidden), in_vmem(tile))


def shares_of(expert_ids, pair_logits):
    mix = pair_mix(pair_logits)
    labels = jnp.arange(lax.axis_size("expert"), dtype=jnp.int32)
    named = expert_ids[None, :, :] == labels[:, None, None]
    return jnp.sum(jnp.where(named, mix[None], 0.0), axis=2)


def share_rows(shares, narrow):
    high = lax.reduce_precision(shares, 8, 7)
    rows = jnp.concatenate([high, shares - high]).astype(jnp.bfloat16)
    return jnp.pad(rows, ((0, -rows.shape[0] % 16), (0, narrow - rows.shape[1])))


def every_row(tokens, expert_ids, pair_logits, w_gate, w_up, w_down):
    expert, split = lax.axis_index("expert"), lax.axis_index("split")
    size, narrow = tokens.shape
    place = [(split // 2) ^ z for z in range(4)]
    place = jnp.stack(place + [expert, lax.axis_size("expert"), split % 2]).astype(jnp.int32)
    w_gate, w_up, w_down = in_hbm(w_gate), in_hbm(w_up), in_hbm(w_down)

    w_gate, w_up, w_down = in_hbm(w_gate), in_hbm(w_up), in_hbm(w_down)
    z0 = tokens[None]
    z1 = send(z0, z=1)
    own = shares_of(expert_ids, pair_logits)
    block = jnp.concatenate([tokens, share_rows(own, narrow)])[None]
    sent = after(z0, own)
    x0, y0, z2 = send(block, x=1), send(sent, y=1), send(sent, z=2)
    x1, y1 = send(z1, x=1), send(z1, y=1)
    sz0, sz1, sx0, sx1, sy0, sy1 = swapped(block, z1, x0, x1, y0, y1)
    near_weights = pair_weights(place, 0, w_gate, w_up, narrow, x0)
    (x1_, y1_), z2, near_weights = after(((x1, y1), z2, near_weights))
    first, last = relayed([x0, x1_], [y0, y1_])
    z3 = send(z2, z=1)
    x2, y2 = send(z2, x=1), send(z2, y=1)
    near = [[(sz0, 0), (sz1, 0)], [(sx0, 0), (sx1, 0)], [(sy0, 0), (sy1, 0)], None, None]
    *sums_0, far_gate = first_part(place, 0, near, (0, 1), near_weights, 2, w_gate)

    z3, sums_0 = after((z3, sums_0))
    (first, last, x2, y2), sums_0 = after(((first, last, x2, y2), sums_0))
    x3, y3 = send(z3, x=1), send(z3, y=1)
    both_of = lambda v: [(v, 0), (v, 1)]
    near[3:] = [both_of(v) for v in swapped(first, last)]
    sz2, sz3, sx2, sy2 = swapped(z2, z3, x2, y2)
    *sums_1, far_up = first_part(place, 1, near, (0, 1), near_weights, 2, w_up)
    far_weights = far_gate, far_up
    (x3, y3), sums_1 = after(((x3, y3), sums_1))
    first, last = relayed([x2, x3], [y2, y3])
    sx3, sy3 = swapped(x3, y3)
    far = [[(sz2, 0), (sz3, 0)], [(sx2, 0), (sx3, 0)], [(sy2, 0), (sy3, 0)], None, None]
    pairs = (3, 2), (1, 0)
    *parts_0, hidden, tile = second_part(
        place, 0, far, (2, 3), far_weights, sums_0, sz0, w_down, pairs
    )
    (first, last, sx2, sx3), parts_0 = after(((first, last, sx2, sx3), parts_0))
    far[1] = [(sx2, 0), (sx3, 0)]
    corners = swapped(first, last)
    last_0 = third_part(place, hidden, tile, pairs[1], size)
    corners, last_0 = after((corners, last_0))
    far[3:] = [both_of(v) for v in corners]
    far_0 = parts_0[0], send(parts_0[1], c=1)
    near_0 = last_0[0], send(last_0[1], c=1)
    *parts_1, hidden = second_part(
        place, 1, far, (2, 3), far_weights, sums_1, sx0, w_down, pairs
    )
    far_0, near_0, parts_1 = after((far_0, near_0, parts_1))
    to_z = total(*[v[:, :1] for v in near_0]).astype(jnp.bfloat16)
    passed_0 = send(to_z, z=1)
    other_1 = send(parts_1[1], c=1)
    last_1 = third_part(place, after(hidden, far_0), tile, pairs[1], size)
    other_1, last_1 = after((other_1, last_1))
    far_1, near_1 = (parts_1[0], other_1), (last_1[0], send(last_1[1], c=1))

    far = far_0, far_1
    corner = diagonal(far)
    to_z = total(*[v[:, :1] for v in near_1]).astype(jnp.bfloat16)
    passed_1 = send(to_z, z=1)
    to_x, to_y = plane_sums(far, *after(corner, to_z))
    from_3 = send(to_x[:1], x=1), send(to_y[:1], y=1)
    here = summed(far, 0, 0)
    to_2 = total(here[:1], *from_3).astype(jnp.bfloat16)
    to_x, to_y = after((to_x, to_y), to_2)
    to_2 = send(to_2, z=1)
    from_2 = send(to_x[1:], x=1), send(to_y[1:], y=1)
    last_block = lambda terms, passed: [v[:, 1:] for v in terms] + [passed]
    near = last_block(near_0, passed_0), last_block(near_1, passed_1)
    corner = diagonal(near)
    to_0 = total(here[1:], *from_2, to_2).astype(jnp.bfloat16)
    to_x, to_y = plane_sums(near, *after(corner, to_0))
    to_0 = send(to_0, z=2)
    from_0 = send(to_x, x=1), send(to_y, y=1)
    return total(summed(near, 0, 0), *from_0, to_0)[0].astype(jnp.bfloat16)


def body(tokens, expert_ids, pair_logits, gate_weight, up_weight, down_weight):
    capacity = 4 * tokens.shape[0] // lax.axis_size("expert")
    arrays = (tokens, expert_ids, pair_logits, gate_weight[0], up_weight[0], down_weight[0])
    splits = lax.axis_size("split")
    if capacity == tokens.shape[0] and splits == 8 and tokens.shape[0] <= tokens.shape[1]:
        return every_row(*arrays)
    return dispatched(*arrays, capacity)


def solution(mesh):
    in_specs = (
        P("expert", "split"),
        P("expert", None),
        P("expert", None),
        P("expert", None, "split"),
        P("expert", None, "split"),
        P("expert", "split", None),
    )
    out_specs = P("expert", "split")
    return jax.shard_map(body, mesh=mesh, in_specs=in_specs, out_specs=out_specs, check_vma=False)
```

```python
import jax
import jax.numpy as jnp
from jax import lax
from jax.experimental import pallas as pl
from jax.experimental.pallas import tpu as pltpu
from jax.sharding import PartitionSpec as P

BOTH = ("expert", "split")
HIDDEN_TILE = 1024
SCALE = 4


def pair_mix(pair_logits):
    first = jax.nn.sigmoid(pair_logits[:, 0] - pair_logits[:, 1])
    return jnp.stack([first, 1.0 - first], axis=1)


def dispatched(tokens, expert_ids, pair_logits, w_gate, w_up, w_down, capacity):
    experts = lax.axis_size("expert")
    tok_rows, narrow = tokens.shape
    flat = expert_ids.reshape(-1)
    labels = jnp.arange(experts, dtype=jnp.int32)
    onehot = (flat[:, None] == labels[None, :]).astype(jnp.int32)
    before = jnp.cumsum(onehot, axis=0) - onehot
    slot = jnp.sum(before * onehot, axis=1)
    dest = flat * capacity + slot
    mix = pair_mix(pair_logits).reshape(-1)
    select = (jnp.arange(experts * capacity, dtype=jnp.int32)[:, None] == dest[None, :]).astype(
        jnp.bfloat16
    )
    doubled = jnp.repeat(tokens, 2, axis=0)
    packed = jnp.dot(select, doubled, preferred_element_type=jnp.float32).astype(jnp.bfloat16)
    sending = packed.reshape(experts, capacity, narrow)
    arrived = lax.all_to_all(sending, "expert", split_axis=0, concat_axis=0, tiled=True).reshape(
        experts * capacity, narrow
    )
    piece = lax.all_gather(arrived, "split", axis=1, tiled=True)
    gate = jnp.dot(piece, w_gate, preferred_element_type=jnp.float32)
    up_part = jnp.dot(piece, w_up, preferred_element_type=jnp.float32)
    hidden = (jax.nn.silu(gate) * up_part).astype(jnp.bfloat16)
    terms = jnp.dot(hidden, w_down, preferred_element_type=jnp.float32)
    result = lax.psum_scatter(
        terms.astype(jnp.bfloat16), "split", scatter_dimension=1, tiled=True
    ).astype(jnp.float32)
    narrow = result.shape[1]
    returned = lax.all_to_all(
        result.reshape(experts, capacity, narrow).astype(jnp.bfloat16),
        "expert",
        split_axis=0,
        concat_axis=0,
        tiled=True,
    ).astype(jnp.float32)
    returned = returned.reshape(experts * capacity, narrow)
    picked = returned[dest] * mix[:, None]
    mixed = picked.reshape(tok_rows, 2, narrow).sum(axis=1)
    return mixed.astype(jnp.bfloat16)


def send(value, x=0, c=0, z=0, y=0):
    experts, splits = lax.axis_size("expert"), lax.axis_size("split")
    flip_expert, flip_split = x * 2 + c, z * 2 + y
    pairs = [
        (e * splits + s, (e ^ flip_expert) * splits + (s ^ flip_split))
        for e in range(experts)
        for s in range(splits)
    ]
    return lax.ppermute(value, BOTH, pairs)


def after(value, *earlier):
    return lax.optimization_barrier((value, earlier))[0]


def relayed(over_x, over_y):
    half = over_y[0].shape[1] // 2
    first = jnp.concatenate([v[:, :half] for v in over_y])
    last = jnp.concatenate([v[:, half : 2 * half] for v in over_x])
    return send(first, x=1), send(last, y=1)


def swapped(*blocks):
    return [(v, send(v, c=1)) for v in blocks]


def summed(terms, y, x, rows=slice(None)):
    return total(*[term[y, :, rows] for term in terms[x]])


def diagonal(terms):
    half = terms[0][0].shape[2] // 2
    first = summed(terms, 1, 1, slice(0, half)).astype(jnp.bfloat16)
    last = summed(terms, 1, 1, slice(half, 2 * half)).astype(jnp.bfloat16)
    return send(first, x=1), send(last, y=1)


def plane_sums(terms, first, last):
    half = terms[0][0].shape[2] // 2
    first, last = first.astype(jnp.float32), last.astype(jnp.float32)
    to_x = summed(terms, 0, 1) + jnp.pad(last, ((0, 0), (half, 0), (0, 0)))
    to_y = summed(terms, 1, 0) + jnp.pad(first, ((0, 0), (0, half), (0, 0)))
    return to_x.astype(jnp.bfloat16), to_y.astype(jnp.bfloat16)


def total(*terms):
    result = terms[0].astype(jnp.float32)
    for term in terms[1:]:
        result = result + term.astype(jnp.float32)
    return result


def pieces(x, pair):
    blocks, over_x, over_y, first, last = pair
    size = blocks[1][0][0].shape[1]
    arrays, found = [], []
    for z in range(2):
        for c in range(2):
            parts = [(blocks[z], 0, 0), (over_y[z], 0, 1)]
            if x:
                parts = [(over_x[z], 0, 0), (first[z], 0, 1), (last[z], size // 2, 1)]
            for (array, index), row, y in parts:
                array = array[c]
                if not any(array is v for v in arrays):
                    arrays.append(array)
                place = [i for i, v in enumerate(arrays) if v is array][0]
                found.append((place, index, z, c * size + row, y, min(size, array.shape[1])))
    return arrays, found


def fill(place, arrays, found, z_places, rows, sems):
    my_y = place[place.shape[0] - 1]
    copies = []
    for i, (which, index, z, row, y, count) in enumerate(found):
        source = arrays[which].at[index, pl.ds(0, count)]
        column = ((place[z_places[z]] & 1) * 2 + (my_y ^ y)) * source.shape[1]
        columns = pl.ds(pl.multiple_of(column, 128), source.shape[1])
        target = rows.at[pl.ds(row, count), columns]
        copies.append(pltpu.make_async_copy(source, target, sems.at[i]))
    return copies


def all_of(copies):
    for copy in copies:
        copy.start()
    for copy in copies:
        copy.wait()


def weight_copies(place, z, weight, result, sems):
    depth = result.shape[0]
    quarter = depth // 4
    base = pl.multiple_of((place[z] // 2) * depth, depth)
    return [
        pltpu.make_async_copy(
            weight.at[pl.ds(base + q * quarter, quarter)],
            result.at[pl.ds(q * quarter, quarter)],
            sems.at[q],
        )
        for q in range(4)
    ]


def weights_kernel(place, *refs, z):
    w_gate, w_up, gate, up, gate_sems, up_sems = refs[-6:]
    all_of(
        weight_copies(place, z, w_gate, gate, gate_sems)
        + weight_copies(place, z, w_up, up, up_sems)
    )


def first_kernel(place, *refs, found, z_places, following):
    arrays, refs = refs[:-9], refs[-9:]
    w_gate, w_up, later, gate, up, later_rows, rows, sems, later_sems = refs
    later = weight_copies(place, following, later, later_rows, later_sems)
    copies = fill(place, arrays, found, z_places, rows, sems)
    for copy in copies + later:
        copy.start()
    for copy in copies:
        copy.wait()
    for weight, result in ((w_gate, gate), (w_up, up)):
        for t in range(result.shape[0]):
            tile = slice(t * HIDDEN_TILE, (t + 1) * HIDDEN_TILE)
            result[t] = jnp.dot(rows[...], weight[:, tile], preferred_element_type=jnp.float32)
    for copy in later:
        copy.wait()


def share_column(place, blocks, tails, sems, size):
    experts = place[place.shape[0] - 2]
    expert = place[place.shape[0] - 3]
    copies = []
    for c, block in enumerate(blocks):
        tail = pl.ds(size, tails.shape[1])
        copies.append(pltpu.make_async_copy(block.at[0, tail], tails.at[c], sems.at[c]))
    all_of(copies)
    column = []
    for c in range(2):
        row = lax.broadcasted_iota(jnp.int32, tails.shape[1:], 0)
        mine = (row == expert) | (row == expert + experts)
        shares = jnp.where(mine, tails[c].astype(jnp.float32), 0.0)
        shares = jnp.sum(shares, axis=0, keepdims=True)[:, :size]
        column.append(jnp.broadcast_to(shares, (128, size)).T)
    return jnp.concatenate(column)[:, :1]


def down_copy(place, pair, w_down, tile, sem):
    span = tile.shape[1]
    columns = pl.ds(pl.multiple_of((place[pair[0]] // 2) * span, span), span)
    return pltpu.make_async_copy(w_down.at[:, columns], tile, sem)


def down_products(place, pair, hidden, tile, results):
    my_y = place[place.shape[0] - 1]
    size, narrow = results[0].shape[2:]
    terms = jnp.dot(hidden[...], tile[...], preferred_element_type=jnp.float32)
    terms = terms.astype(jnp.bfloat16)
    for r, result in enumerate(results):
        for z in range(2):
            n = (place[pair[0]] & 1) ^ z
            for y in range(2):
                start = (z * 2 + y) * narrow
                piece = terms[r * size : (r + 1) * size, start : start + narrow]
                result[my_y ^ y, n] = piece


def second_kernel(place, *refs, x, found, z_places, pairs):
    count = 16 if x else 17
    arrays, refs = refs[:-count], refs[-count:]
    w_gate, w_up, gate, up, w_down = refs[:5]
    shares, results, hidden = refs[5:7], refs[7:9], refs[9]
    rows, tails, sems, t_sems, d_sems, tile = refs[-6:]
    copies = fill(place, arrays, found, z_places, rows, sems)
    downs_in = [down_copy(place, pairs[0], w_down, tile, d_sems.at[0])]
    if x == 0:
        downs_in.append(down_copy(place, pairs[1], w_down, refs[10], d_sems.at[1]))
    for copy in copies + downs_in:
        copy.start()
    share = 0.5 * share_column(place, shares, tails, t_sems, results[0].shape[2])
    for copy in copies:
        copy.wait()
    for t in range(gate.shape[0]):
        span = slice(t * HIDDEN_TILE, (t + 1) * HIDDEN_TILE)
        g = gate[t] + jnp.dot(rows[...], w_gate[:, span], preferred_element_type=jnp.float32)
        u = up[t] + jnp.dot(rows[...], w_up[:, span], preferred_element_type=jnp.float32)
        value = (g + g * jnp.tanh(0.5 * g)) * u * share
        hidden[:, span] = value.astype(jnp.bfloat16)
    downs_in[0].wait()
    down_products(place, pairs[0], hidden, tile, results)
    for copy in downs_in[1:]:
        copy.wait()


def third_kernel(place, hidden, tile, own, sibling, pair):
    down_products(place, pair, hidden, tile, (own, sibling))


def cost(flops, bytes_accessed, transcendentals):
    return pl.CostEstimate(
        flops=flops // SCALE,
        bytes_accessed=bytes_accessed // SCALE,
        transcendentals=transcendentals // SCALE,
    )


def in_hbm(value):
    return pltpu.with_memory_space_constraint(value, pltpu.HBM)


def in_vmem(value):
    return pltpu.with_memory_space_constraint(value, pltpu.VMEM)


ANY = pl.BlockSpec(memory_space=pl.ANY)
SCALARS = pl.BlockSpec(memory_space=pltpu.SMEM)
VMEM = pl.BlockSpec(memory_space=pltpu.VMEM)
SEMS = pltpu.SemaphoreType.DMA


def params(mebibytes):
    return pltpu.CompilerParams(vmem_limit_bytes=mebibytes * 1024 * 1024)


def pair_weights(place, z, w_gate, w_up, narrow, *earlier):
    width, depth = w_gate.shape[1], 4 * narrow
    return pl.pallas_call(
        lambda *refs: weights_kernel(*refs, z=z),
        in_specs=[SCALARS] + [ANY] * (len(earlier) + 2),
        out_specs=[VMEM] * 2,
        scratch_shapes=[SEMS((4,)), SEMS((4,))],
        out_shape=[pltpu.VMEM((depth, width), jnp.bfloat16)] * 2,
        compiler_params=params(2),
        cost_estimate=cost(flops=0, bytes_accessed=8 * depth * width, transcendentals=0),
        name="pair_weights",
    )(place, *earlier, w_gate, w_up)


def first_part(place, x, pair, z_places, weights, following, later):
    arrays, found = pieces(x, pair)
    size, narrow = pair[0][1][0][0].shape[1:]
    depth, width = weights[0].shape
    rows = 2 * size
    sums = pltpu.VMEM((width // HIDDEN_TILE, rows, HIDDEN_TILE), jnp.float32)
    return pl.pallas_call(
        lambda *refs: first_kernel(*refs, found=found, z_places=z_places, following=following),
        in_specs=[SCALARS] + [ANY] * len(arrays) + [VMEM, VMEM, ANY],
        out_specs=[VMEM] * 3,
        scratch_shapes=[
            pltpu.VMEM((rows, depth), jnp.bfloat16),
            SEMS((len(found),)),
            SEMS((4,)),
        ],
        out_shape=[sums, sums, pltpu.VMEM((depth, width), jnp.bfloat16)],
        compiler_params=params(4),
        cost_estimate=cost(
            flops=4 * rows * depth * width,
            bytes_accessed=4 * depth * width + 2 * rows * depth + 8 * rows * width,
            transcendentals=0,
        ),
        name="first_part",
    )(place, *arrays, *[in_vmem(v) for v in weights], later)


def second_part(place, x, pair, z_places, weights, sums, shares, w_down, pairs):
    arrays, found = pieces(x, pair)
    size, narrow = pair[0][1][0][0].shape[1:]
    depth, width = weights[0].shape
    rows, tail = 2 * size, shares[0].shape[1] - size
    part = pltpu.VMEM((2, 2, size, narrow), jnp.bfloat16)
    hidden, tile = [pltpu.VMEM(v, jnp.bfloat16) for v in ((rows, width), (width, depth))]
    return pl.pallas_call(
        lambda *refs: second_kernel(
            *refs, x=x, found=found, z_places=z_places, pairs=pairs
        ),
        in_specs=[SCALARS] + [ANY] * len(arrays) + [VMEM] * 4 + [ANY] * 3,
        out_specs=[VMEM] * (3 if x else 4),
        scratch_shapes=[
            pltpu.VMEM((rows, depth), jnp.bfloat16),
            pltpu.VMEM((2, tail, narrow), jnp.bfloat16),
            SEMS((len(found),)),
            SEMS((2,)),
            SEMS((2,)),
            tile,
        ],
        out_shape=[part, part, hidden] + ([] if x else [tile]),
        compiler_params=params(9),
        cost_estimate=cost(
            flops=4 * rows * depth * width + 4 * rows * width * depth,
            bytes_accessed=8 * depth * width + 6 * rows * depth + 8 * rows * width,
            transcendentals=rows * width,
        ),
        name="second_part",
    )(place, *arrays, *[in_vmem(v) for v in (*weights, *sums)], w_down, *shares)


def third_part(place, hidden, tile, pair, size):
    rows, width = hidden.shape
    narrow = tile.shape[1] // 4
    return pl.pallas_call(
        lambda *refs: third_kernel(*refs, pair=pair),
        in_specs=[SCALARS, VMEM, VMEM],
        out_specs=[VMEM] * 2,
        out_shape=[pltpu.VMEM((2, 2, size, narrow), jnp.bfloat16)] * 2,
        compiler_params=params(8),
        cost_estimate=cost(
            flops=2 * rows * width * tile.shape[1],
            bytes_accessed=2 * width * (rows + tile.shape[1]) + 2 * rows * tile.shape[1],
            transcendentals=0,
        ),
        name="third_part",
    )(place, in_vmem(hidden), in_vmem(tile))


def shares_of(expert_ids, pair_logits):
    mix = pair_mix(pair_logits)
    labels = jnp.arange(lax.axis_size("expert"), dtype=jnp.int32)
    named = expert_ids[None, :, :] == labels[:, None, None]
    return jnp.sum(jnp.where(named, mix[None], 0.0), axis=2)


def share_rows(shares, narrow):
    high = lax.reduce_precision(shares, 8, 7)
    rows = jnp.concatenate([high, shares - high]).astype(jnp.bfloat16)
    return jnp.pad(rows, ((0, -rows.shape[0] % 16), (0, narrow - rows.shape[1])))


def every_row(tokens, expert_ids, pair_logits, w_gate, w_up, w_down):
    expert, split = lax.axis_index("expert"), lax.axis_index("split")
    size, narrow = tokens.shape
    place = [(split // 2) ^ z for z in range(4)]
    place = jnp.stack(place + [expert, lax.axis_size("expert"), split % 2]).astype(jnp.int32)
    w_gate, w_up, w_down = in_hbm(w_gate), in_hbm(w_up), in_hbm(w_down)

    w_gate, w_up, w_down = in_hbm(w_gate), in_hbm(w_up), in_hbm(w_down)
    z0 = tokens[None]
    z1 = send(z0, z=1)
    own = shares_of(expert_ids, pair_logits)
    block = jnp.concatenate([tokens, share_rows(own, narrow)])[None]
    sent = after(z0, own)
    x0, y0, z2 = send(block, x=1), send(sent, y=1), send(sent, z=2)
    x1, y1 = send(z1, x=1), send(z1, y=1)
    sz0, sz1, sx0, sx1, sy0, sy1 = swapped(block, z1, x0, x1, y0, y1)
    near_weights = pair_weights(place, 0, w_gate, w_up, narrow, x0)
    (x1_, y1_), z2, near_weights = after(((x1, y1), z2, near_weights))
    first, last = relayed([x0, x1_], [y0, y1_])
    z3 = send(z2, z=1)
    x2, y2 = send(z2, x=1), send(z2, y=1)
    near = [[(sz0, 0), (sz1, 0)], [(sx0, 0), (sx1, 0)], [(sy0, 0), (sy1, 0)], None, None]
    *sums_0, far_gate = first_part(place, 0, near, (0, 1), near_weights, 2, w_gate)

    z3, sums_0 = after((z3, sums_0))
    (first, last, x2, y2), sums_0 = after(((first, last, x2, y2), sums_0))
    x3, y3 = send(z3, x=1), send(z3, y=1)
    both_of = lambda v: [(v, 0), (v, 1)]
    near[3:] = [both_of(v) for v in swapped(first, last)]
    sz2, sz3, sx2, sy2 = swapped(z2, z3, x2, y2)
    *sums_1, far_up = first_part(place, 1, near, (0, 1), near_weights, 2, w_up)
    far_weights = far_gate, far_up
    (x3, y3), sums_1 = after(((x3, y3), sums_1))
    first, last = relayed([x2, x3], [y2, y3])
    sx3, sy3 = swapped(x3, y3)
    far = [[(sz2, 0), (sz3, 0)], [(sx2, 0), (sx3, 0)], [(sy2, 0), (sy3, 0)], None, None]
    pairs = (3, 2), (1, 0)
    *parts_0, hidden, tile = second_part(
        place, 0, far, (2, 3), far_weights, sums_0, sz0, w_down, pairs
    )
    (first, last, sx2, sx3), parts_0 = after(((first, last, sx2, sx3), parts_0))
    far[1] = [(sx2, 0), (sx3, 0)]
    corners = swapped(first, last)
    last_0 = third_part(place, hidden, tile, pairs[1], size)
    corners, last_0 = after((corners, last_0))
    far[3:] = [both_of(v) for v in corners]
    far_0 = parts_0[0], send(parts_0[1], c=1)
    near_0 = last_0[0], send(last_0[1], c=1)
    *parts_1, hidden = second_part(
        place, 1, far, (2, 3), far_weights, sums_1, sx0, w_down, pairs
    )
    far_0, near_0, parts_1 = after((far_0, near_0, parts_1))
    to_z = total(*[v[:, :1] for v in near_0]).astype(jnp.bfloat16)
    passed_0 = send(to_z, z=1)
    other_1 = send(parts_1[1], c=1)
    last_1 = third_part(place, after(hidden, far_0), tile, pairs[1], size)
    other_1, last_1 = after((other_1, last_1))
    far_1, near_1 = (parts_1[0], other_1), (last_1[0], send(last_1[1], c=1))

    far = far_0, far_1
    corner = diagonal(far)
    to_z = total(*[v[:, :1] for v in near_1]).astype(jnp.bfloat16)
    passed_1 = send(to_z, z=1)
    to_x, to_y = plane_sums(far, *after(corner, to_z))
    from_3 = send(to_x[:1], x=1), send(to_y[:1], y=1)
    here = summed(far, 0, 0)
    to_2 = total(here[:1], *from_3).astype(jnp.bfloat16)
    to_x, to_y = after((to_x, to_y), to_2)
    to_2 = send(to_2, z=1)
    from_2 = send(to_x[1:], x=1), send(to_y[1:], y=1)
    last_block = lambda terms, passed: [v[:, 1:] for v in terms] + [passed]
    near = last_block(near_0, passed_0), last_block(near_1, passed_1)
    corner = diagonal(near)
    to_0 = total(here[1:], *from_2, to_2).astype(jnp.bfloat16)
    to_x, to_y = plane_sums(near, *after(corner, to_0))
    to_0 = send(to_0, z=2)
    from_0 = send(to_x, x=1), send(to_y, y=1)
    return total(summed(near, 0, 0), *from_0, to_0)[0].astype(jnp.bfloat16)


def body(tokens, expert_ids, pair_logits, gate_weight, up_weight, down_weight):
    capacity = 4 * tokens.shape[0] // lax.axis_size("expert")
    arrays = (tokens, expert_ids, pair_logits, gate_weight[0], up_weight[0], down_weight[0])
    splits = lax.axis_size("split")
    if capacity == tokens.shape[0] and splits == 8 and tokens.shape[0] <= tokens.shape[1]:
        return every_row(*arrays)
    return dispatched(*arrays, capacity)


def solution(mesh):
    in_specs = (
        P("expert", "split"),
        P("expert", None),
        P("expert", None),
        P("expert", None, "split"),
        P("expert", None, "split"),
        P("expert", "split", None),
    )
    out_specs = P("expert", "split")
    return jax.shard_map(body, mesh=mesh, in_specs=in_specs, out_specs=out_specs, check_vma=False)
```

```python
import jax
import jax.numpy as jnp
from jax import lax
from jax.experimental import pallas as pl
from jax.experimental.pallas import tpu as pltpu
from jax.sharding import PartitionSpec as P

BOTH = ("expert", "split")
HIDDEN_TILE = 1024
SCALE = 4


def pair_mix(pair_logits):
    first = jax.nn.sigmoid(pair_logits[:, 0] - pair_logits[:, 1])
    return jnp.stack([first, 1.0 - first], axis=1)


def dispatched(tokens, expert_ids, pair_logits, w_gate, w_up, w_down, capacity):
    experts = lax.axis_size("expert")
    tok_rows, narrow = tokens.shape
    flat = expert_ids.reshape(-1)
    labels = jnp.arange(experts, dtype=jnp.int32)
    onehot = (flat[:, None] == labels[None, :]).astype(jnp.int32)
    before = jnp.cumsum(onehot, axis=0) - onehot
    slot = jnp.sum(before * onehot, axis=1)
    dest = flat * capacity + slot
    mix = pair_mix(pair_logits).reshape(-1)
    select = (jnp.arange(experts * capacity, dtype=jnp.int32)[:, None] == dest[None, :]).astype(
        jnp.bfloat16
    )
    doubled = jnp.repeat(tokens, 2, axis=0)
    packed = jnp.dot(select, doubled, preferred_element_type=jnp.float32).astype(jnp.bfloat16)
    sending = packed.reshape(experts, capacity, narrow)
    arrived = lax.all_to_all(sending, "expert", split_axis=0, concat_axis=0, tiled=True).reshape(
        experts * capacity, narrow
    )
    piece = lax.all_gather(arrived, "split", axis=1, tiled=True)
    gate = jnp.dot(piece, w_gate, preferred_element_type=jnp.float32)
    up_part = jnp.dot(piece, w_up, preferred_element_type=jnp.float32)
    hidden = (jax.nn.silu(gate) * up_part).astype(jnp.bfloat16)
    terms = jnp.dot(hidden, w_down, preferred_element_type=jnp.float32)
    result = lax.psum_scatter(
        terms.astype(jnp.bfloat16), "split", scatter_dimension=1, tiled=True
    ).astype(jnp.float32)
    narrow = result.shape[1]
    returned = lax.all_to_all(
        result.reshape(experts, capacity, narrow).astype(jnp.bfloat16),
        "expert",
        split_axis=0,
        concat_axis=0,
        tiled=True,
    ).astype(jnp.float32)
    returned = returned.reshape(experts * capacity, narrow)
    picked = returned[dest] * mix[:, None]
    mixed = picked.reshape(tok_rows, 2, narrow).sum(axis=1)
    return mixed.astype(jnp.bfloat16)


def send(value, x=0, c=0, z=0, y=0):
    experts, splits = lax.axis_size("expert"), lax.axis_size("split")
    flip_expert, flip_split = x * 2 + c, z * 2 + y
    pairs = [
        (e * splits + s, (e ^ flip_expert) * splits + (s ^ flip_split))
        for e in range(experts)
        for s in range(splits)
    ]
    return lax.ppermute(value, BOTH, pairs)


def after(value, *earlier):
    return lax.optimization_barrier((value, earlier))[0]


def relayed(over_x, over_y):
    half = over_y[0].shape[1] // 2
    first = jnp.concatenate([v[:, :half] for v in over_y])
    last = jnp.concatenate([v[:, half : 2 * half] for v in over_x])
    return send(first, x=1), send(last, y=1)


def swapped(*blocks):
    return [(v, send(v, c=1)) for v in blocks]


def summed(terms, y, x, rows=slice(None)):
    return total(*[term[y, :, rows] for term in terms[x]])


def diagonal(terms):
    half = terms[0][0].shape[2] // 2
    first = summed(terms, 1, 1, slice(0, half)).astype(jnp.bfloat16)
    last = summed(terms, 1, 1, slice(half, 2 * half)).astype(jnp.bfloat16)
    return first, last


def across(halves):
    return send(halves[0], x=1), send(halves[1], y=1)


def plane_sums(terms, first, last):
    half = terms[0][0].shape[2] // 2
    first, last = first.astype(jnp.float32), last.astype(jnp.float32)
    to_x = summed(terms, 0, 1) + jnp.pad(last, ((0, 0), (half, 0), (0, 0)))
    to_y = summed(terms, 1, 0) + jnp.pad(first, ((0, 0), (0, half), (0, 0)))
    return to_x.astype(jnp.bfloat16), to_y.astype(jnp.bfloat16)


def total(*terms):
    result = terms[0].astype(jnp.float32)
    for term in terms[1:]:
        result = result + term.astype(jnp.float32)
    return result


def pieces(x, pair):
    blocks, over_x, over_y, first, last = pair
    size = blocks[1][0][0].shape[1]
    arrays, found = [], []
    for z in range(2):
        for c in range(2):
            parts = [(blocks[z], 0, 0), (over_y[z], 0, 1)]
            if x:
                parts = [(over_x[z], 0, 0), (first[z], 0, 1), (last[z], size // 2, 1)]
            for (array, index), row, y in parts:
                array = array[c]
                if not any(array is v for v in arrays):
                    arrays.append(array)
                place = [i for i, v in enumerate(arrays) if v is array][0]
                found.append((place, index, z, c * size + row, y, min(size, array.shape[1])))
    return arrays, found


def fill(place, arrays, found, z_places, rows, sems):
    my_y = place[place.shape[0] - 1]
    copies = []
    for i, (which, index, z, row, y, count) in enumerate(found):
        source = arrays[which].at[index, pl.ds(0, count)]
        column = ((place[z_places[z]] & 1) * 2 + (my_y ^ y)) * source.shape[1]
        columns = pl.ds(pl.multiple_of(column, 128), source.shape[1])
        target = rows.at[pl.ds(row, count), columns]
        copies.append(pltpu.make_async_copy(source, target, sems.at[i]))
    return copies


def all_of(copies):
    for copy in copies:
        copy.start()
    for copy in copies:
        copy.wait()


def weight_copies(place, z, weight, result, sems):
    depth = result.shape[0]
    quarter = depth // 4
    base = pl.multiple_of((place[z] // 2) * depth, depth)
    return [
        pltpu.make_async_copy(
            weight.at[pl.ds(base + q * quarter, quarter)],
            result.at[pl.ds(q * quarter, quarter)],
            sems.at[q],
        )
        for q in range(4)
    ]


def weights_kernel(place, *refs, z):
    w_gate, w_up, gate, up, gate_sems, up_sems = refs[-6:]
    all_of(
        weight_copies(place, z, w_gate, gate, gate_sems)
        + weight_copies(place, z, w_up, up, up_sems)
    )


def first_kernel(place, *refs, found, z_places, following):
    arrays, refs = refs[:-9], refs[-9:]
    w_gate, w_up, later, gate, up, later_rows, rows, sems, later_sems = refs
    later = weight_copies(place, following, later, later_rows, later_sems)
    copies = fill(place, arrays, found, z_places, rows, sems)
    for copy in copies + later:
        copy.start()
    for copy in copies:
        copy.wait()
    for weight, result in ((w_gate, gate), (w_up, up)):
        for t in range(result.shape[0]):
            tile = slice(t * HIDDEN_TILE, (t + 1) * HIDDEN_TILE)
            result[t] = jnp.dot(rows[...], weight[:, tile], preferred_element_type=jnp.float32)
    for copy in later:
        copy.wait()


def share_column(place, blocks, tails, sems, size):
    experts = place[place.shape[0] - 2]
    expert = place[place.shape[0] - 3]
    copies = []
    for c, block in enumerate(blocks):
        tail = pl.ds(size, tails.shape[1])
        copies.append(pltpu.make_async_copy(block.at[0, tail], tails.at[c], sems.at[c]))
    all_of(copies)
    column = []
    for c in range(2):
        row = lax.broadcasted_iota(jnp.int32, tails.shape[1:], 0)
        mine = (row == expert) | (row == expert + experts)
        shares = jnp.where(mine, tails[c].astype(jnp.float32), 0.0)
        shares = jnp.sum(shares, axis=0, keepdims=True)[:, :size]
        column.append(jnp.broadcast_to(shares, (128, size)).T)
    return jnp.concatenate(column)[:, :1]


def down_copy(place, pair, w_down, tile, sem):
    span = tile.shape[1]
    columns = pl.ds(pl.multiple_of((place[pair[0]] // 2) * span, span), span)
    return pltpu.make_async_copy(w_down.at[:, columns], tile, sem)


def down_products(place, pair, hidden, tile, results):
    my_y = place[place.shape[0] - 1]
    size, narrow = results[0].shape[2:]
    terms = jnp.dot(hidden[...], tile[...], preferred_element_type=jnp.float32)
    terms = terms.astype(jnp.bfloat16)
    for r, result in enumerate(results):
        for z in range(2):
            n = (place[pair[0]] & 1) ^ z
            for y in range(2):
                start = (z * 2 + y) * narrow
                piece = terms[r * size : (r + 1) * size, start : start + narrow]
                result[my_y ^ y, n] = piece


def second_kernel(place, *refs, x, found, z_places, pairs):
    count = 16 if x else 17
    arrays, refs = refs[:-count], refs[-count:]
    w_gate, w_up, gate, up, w_down = refs[:5]
    shares, results, hidden = refs[5:7], refs[7:9], refs[9]
    rows, tails, sems, t_sems, d_sems, tile = refs[-6:]
    copies = fill(place, arrays, found, z_places, rows, sems)
    downs_in = [down_copy(place, pairs[0], w_down, tile, d_sems.at[0])]
    if x == 0:
        downs_in.append(down_copy(place, pairs[1], w_down, refs[10], d_sems.at[1]))
    for copy in copies + downs_in:
        copy.start()
    share = 0.5 * share_column(place, shares, tails, t_sems, results[0].shape[2])
    for copy in copies:
        copy.wait()
    for t in range(gate.shape[0]):
        span = slice(t * HIDDEN_TILE, (t + 1) * HIDDEN_TILE)
        g = gate[t] + jnp.dot(rows[...], w_gate[:, span], preferred_element_type=jnp.float32)
        u = up[t] + jnp.dot(rows[...], w_up[:, span], preferred_element_type=jnp.float32)
        value = (g + g * jnp.tanh(0.5 * g)) * u * share
        hidden[:, span] = value.astype(jnp.bfloat16)
    downs_in[0].wait()
    down_products(place, pairs[0], hidden, tile, results)
    for copy in downs_in[1:]:
        copy.wait()


def third_kernel(place, hidden, tile, own, sibling, pair):
    down_products(place, pair, hidden, tile, (own, sibling))


def cost(flops, bytes_accessed, transcendentals):
    return pl.CostEstimate(
        flops=flops // SCALE,
        bytes_accessed=bytes_accessed // SCALE,
        transcendentals=transcendentals // SCALE,
    )


def in_hbm(value):
    return pltpu.with_memory_space_constraint(value, pltpu.HBM)


def in_vmem(value):
    return pltpu.with_memory_space_constraint(value, pltpu.VMEM)


ANY = pl.BlockSpec(memory_space=pl.ANY)
SCALARS = pl.BlockSpec(memory_space=pltpu.SMEM)
VMEM = pl.BlockSpec(memory_space=pltpu.VMEM)
SEMS = pltpu.SemaphoreType.DMA


def params(mebibytes):
    return pltpu.CompilerParams(vmem_limit_bytes=mebibytes * 1024 * 1024)


def pair_weights(place, z, w_gate, w_up, narrow, *earlier):
    width, depth = w_gate.shape[1], 4 * narrow
    return pl.pallas_call(
        lambda *refs: weights_kernel(*refs, z=z),
        in_specs=[SCALARS] + [ANY] * (len(earlier) + 2),
        out_specs=[VMEM] * 2,
        scratch_shapes=[SEMS((4,)), SEMS((4,))],
        out_shape=[pltpu.VMEM((depth, width), jnp.bfloat16)] * 2,
        compiler_params=params(2),
        cost_estimate=cost(flops=0, bytes_accessed=8 * depth * width, transcendentals=0),
        name="pair_weights",
    )(place, *earlier, w_gate, w_up)


def first_part(place, x, pair, z_places, weights, following, later):
    arrays, found = pieces(x, pair)
    size, narrow = pair[0][1][0][0].shape[1:]
    depth, width = weights[0].shape
    rows = 2 * size
    sums = pltpu.VMEM((width // HIDDEN_TILE, rows, HIDDEN_TILE), jnp.float32)
    return pl.pallas_call(
        lambda *refs: first_kernel(*refs, found=found, z_places=z_places, following=following),
        in_specs=[SCALARS] + [ANY] * len(arrays) + [VMEM, VMEM, ANY],
        out_specs=[VMEM] * 3,
        scratch_shapes=[
            pltpu.VMEM((rows, depth), jnp.bfloat16),
            SEMS((len(found),)),
            SEMS((4,)),
        ],
        out_shape=[sums, sums, pltpu.VMEM((depth, width), jnp.bfloat16)],
        compiler_params=params(4),
        cost_estimate=cost(
            flops=4 * rows * depth * width,
            bytes_accessed=4 * depth * width + 2 * rows * depth + 8 * rows * width,
            transcendentals=0,
        ),
        name="first_part",
    )(place, *arrays, *[in_vmem(v) for v in weights], later)


def second_part(place, x, pair, z_places, weights, sums, shares, w_down, pairs):
    arrays, found = pieces(x, pair)
    size, narrow = pair[0][1][0][0].shape[1:]
    depth, width = weights[0].shape
    rows, tail = 2 * size, shares[0].shape[1] - size
    part = pltpu.VMEM((2, 2, size, narrow), jnp.bfloat16)
    hidden, tile = [pltpu.VMEM(v, jnp.bfloat16) for v in ((rows, width), (width, depth))]
    return pl.pallas_call(
        lambda *refs: second_kernel(
            *refs, x=x, found=found, z_places=z_places, pairs=pairs
        ),
        in_specs=[SCALARS] + [ANY] * len(arrays) + [VMEM] * 4 + [ANY] * 3,
        out_specs=[VMEM] * (3 if x else 4),
        scratch_shapes=[
            pltpu.VMEM((rows, depth), jnp.bfloat16),
            pltpu.VMEM((2, tail, narrow), jnp.bfloat16),
            SEMS((len(found),)),
            SEMS((2,)),
            SEMS((2,)),
            tile,
        ],
        out_shape=[part, part, hidden] + ([] if x else [tile]),
        compiler_params=params(9),
        cost_estimate=cost(
            flops=4 * rows * depth * width + 4 * rows * width * depth,
            bytes_accessed=8 * depth * width + 6 * rows * depth + 8 * rows * width,
            transcendentals=rows * width,
        ),
        name="second_part",
    )(place, *arrays, *[in_vmem(v) for v in (*weights, *sums)], w_down, *shares)


def third_part(place, hidden, tile, pair, size):
    rows, width = hidden.shape
    narrow = tile.shape[1] // 4
    return pl.pallas_call(
        lambda *refs: third_kernel(*refs, pair=pair),
        in_specs=[SCALARS, VMEM, VMEM],
        out_specs=[VMEM] * 2,
        out_shape=[pltpu.VMEM((2, 2, size, narrow), jnp.bfloat16)] * 2,
        compiler_params=params(8),
        cost_estimate=cost(
            flops=2 * rows * width * tile.shape[1],
            bytes_accessed=2 * width * (rows + tile.shape[1]) + 2 * rows * tile.shape[1],
            transcendentals=0,
        ),
        name="third_part",
    )(place, in_vmem(hidden), in_vmem(tile))


def shares_of(expert_ids, pair_logits):
    mix = pair_mix(pair_logits)
    labels = jnp.arange(lax.axis_size("expert"), dtype=jnp.int32)
    named = expert_ids[None, :, :] == labels[:, None, None]
    return jnp.sum(jnp.where(named, mix[None], 0.0), axis=2)


def share_rows(shares, narrow):
    high = lax.reduce_precision(shares, 8, 7)
    rows = jnp.concatenate([high, shares - high]).astype(jnp.bfloat16)
    return jnp.pad(rows, ((0, -rows.shape[0] % 16), (0, narrow - rows.shape[1])))


def every_row(tokens, expert_ids, pair_logits, w_gate, w_up, w_down):
    expert, split = lax.axis_index("expert"), lax.axis_index("split")
    size, narrow = tokens.shape
    place = [(split // 2) ^ z for z in range(4)]
    place = jnp.stack(place + [expert, lax.axis_size("expert"), split % 2]).astype(jnp.int32)
    w_gate, w_up, w_down = in_hbm(w_gate), in_hbm(w_up), in_hbm(w_down)

    w_gate, w_up, w_down = in_hbm(w_gate), in_hbm(w_up), in_hbm(w_down)
    z0 = tokens[None]
    z1 = send(z0, z=1)
    own = shares_of(expert_ids, pair_logits)
    block = jnp.concatenate([tokens, share_rows(own, narrow)])[None]
    sent = after(z0, own)
    x0, y0, z2 = send(block, x=1), send(sent, y=1), send(sent, z=2)
    x1, y1 = send(z1, x=1), send(z1, y=1)
    sz0, sz1, sx0, sx1, sy0, sy1 = swapped(block, z1, x0, x1, y0, y1)
    near_weights = pair_weights(place, 0, w_gate, w_up, narrow, x0)
    (x1_, y1_), z2, near_weights = after(((x1, y1), z2, near_weights))
    first, last = relayed([x0, x1_], [y0, y1_])
    z3 = send(z2, z=1)
    x2, y2 = send(z2, x=1), send(z2, y=1)
    near = [[(sz0, 0), (sz1, 0)], [(sx0, 0), (sx1, 0)], [(sy0, 0), (sy1, 0)], None, None]
    *sums_0, far_gate = first_part(place, 0, near, (0, 1), near_weights, 2, w_gate)

    z3, sums_0 = after((z3, sums_0))
    (first, last, x2, y2), sums_0 = after(((first, last, x2, y2), sums_0))
    x3, y3 = send(z3, x=1), send(z3, y=1)
    both_of = lambda v: [(v, 0), (v, 1)]
    near[3:] = [both_of(v) for v in swapped(first, last)]
    sz2, sz3, sx2, sy2 = swapped(z2, z3, x2, y2)
    *sums_1, far_up = first_part(place, 1, near, (0, 1), near_weights, 2, w_up)
    far_weights = far_gate, far_up
    (x3, y3), sums_1 = after(((x3, y3), sums_1))
    first, last = relayed([x2, x3], [y2, y3])
    sx3, sy3 = swapped(x3, y3)
    far = [[(sz2, 0), (sz3, 0)], [(sx2, 0), (sx3, 0)], [(sy2, 0), (sy3, 0)], None, None]
    pairs = (3, 2), (1, 0)
    *parts_0, hidden, tile = second_part(
        place, 0, far, (2, 3), far_weights, sums_0, sz0, w_down, pairs
    )
    (first, last, sx2, sx3), parts_0 = after(((first, last, sx2, sx3), parts_0))
    far[1] = [(sx2, 0), (sx3, 0)]
    corners = swapped(first, last)
    last_0 = third_part(place, hidden, tile, pairs[1], size)
    corners, last_0 = after((corners, last_0))
    far[3:] = [both_of(v) for v in corners]
    far_0 = parts_0[0], send(parts_0[1], c=1)
    near_0 = last_0[0], send(last_0[1], c=1)
    *parts_1, hidden = second_part(
        place, 1, far, (2, 3), far_weights, sums_1, sx0, w_down, pairs
    )
    far_0, near_0, parts_1 = after((far_0, near_0, parts_1))
    other_1 = send(parts_1[1], c=1)
    last_1 = third_part(place, after(hidden, far_0), tile, pairs[1], size)
    other_1, last_1 = after((other_1, last_1))
    far_1, near_1 = (parts_1[0], other_1), (last_1[0], send(last_1[1], c=1))

    far = far_0, far_1
    halves = diagonal(far)
    corner = across(halves)
    to_z = total(*[v[:, :1] for v in near_0]).astype(jnp.bfloat16)
    passed_0 = send(after(to_z, halves), z=1)
    to_z = total(*[v[:, :1] for v in near_1]).astype(jnp.bfloat16)
    passed_1 = send(to_z, z=1)
    to_x, to_y = plane_sums(far, *after(corner, to_z))
    from_3 = send(to_x[:1], x=1), send(to_y[:1], y=1)
    here = summed(far, 0, 0)
    to_2 = total(here[:1], *from_3).astype(jnp.bfloat16)
    to_x, to_y = after((to_x, to_y), to_2)
    to_2 = send(to_2, z=1)
    from_2 = send(to_x[1:], x=1), send(to_y[1:], y=1)
    last_block = lambda terms, passed: [v[:, 1:] for v in terms] + [passed]
    near = last_block(near_0, passed_0), last_block(near_1, passed_1)
    corner = across(diagonal(near))
    to_0 = total(here[1:], *from_2, to_2).astype(jnp.bfloat16)
    to_x, to_y = plane_sums(near, *after(corner, to_0))
    to_0 = send(to_0, z=2)
    from_0 = send(to_x, x=1), send(to_y, y=1)
    return total(summed(near, 0, 0), *from_0, to_0)[0].astype(jnp.bfloat16)


def body(tokens, expert_ids, pair_logits, gate_weight, up_weight, down_weight):
    capacity = 4 * tokens.shape[0] // lax.axis_size("expert")
    arrays = (tokens, expert_ids, pair_logits, gate_weight[0], up_weight[0], down_weight[0])
    splits = lax.axis_size("split")
    if capacity == tokens.shape[0] and splits == 8 and tokens.shape[0] <= tokens.shape[1]:
        return every_row(*arrays)
    return dispatched(*arrays, capacity)


def solution(mesh):
    in_specs = (
        P("expert", "split"),
        P("expert", None),
        P("expert", None),
        P("expert", None, "split"),
        P("expert", None, "split"),
        P("expert", "split", None),
    )
    out_specs = P("expert", "split")
    return jax.shard_map(body, mesh=mesh, in_specs=in_specs, out_specs=out_specs, check_vma=False)
```

```python
import jax
import jax.numpy as jnp
from jax import lax
from jax.experimental import pallas as pl
from jax.experimental.pallas import tpu as pltpu
from jax.sharding import PartitionSpec as P

BOTH = ("expert", "split")
HIDDEN_TILE = 1024
SCALE = 4


def pair_mix(pair_logits):
    first = jax.nn.sigmoid(pair_logits[:, 0] - pair_logits[:, 1])
    return jnp.stack([first, 1.0 - first], axis=1)


def dispatched(tokens, expert_ids, pair_logits, w_gate, w_up, w_down, capacity):
    experts = lax.axis_size("expert")
    tok_rows, narrow = tokens.shape
    flat = expert_ids.reshape(-1)
    labels = jnp.arange(experts, dtype=jnp.int32)
    onehot = (flat[:, None] == labels[None, :]).astype(jnp.int32)
    before = jnp.cumsum(onehot, axis=0) - onehot
    slot = jnp.sum(before * onehot, axis=1)
    dest = flat * capacity + slot
    mix = pair_mix(pair_logits).reshape(-1)
    select = (jnp.arange(experts * capacity, dtype=jnp.int32)[:, None] == dest[None, :]).astype(
        jnp.bfloat16
    )
    doubled = jnp.repeat(tokens, 2, axis=0)
    packed = jnp.dot(select, doubled, preferred_element_type=jnp.float32).astype(jnp.bfloat16)
    sending = packed.reshape(experts, capacity, narrow)
    arrived = lax.all_to_all(sending, "expert", split_axis=0, concat_axis=0, tiled=True).reshape(
        experts * capacity, narrow
    )
    piece = lax.all_gather(arrived, "split", axis=1, tiled=True)
    gate = jnp.dot(piece, w_gate, preferred_element_type=jnp.float32)
    up_part = jnp.dot(piece, w_up, preferred_element_type=jnp.float32)
    hidden = (jax.nn.silu(gate) * up_part).astype(jnp.bfloat16)
    terms = jnp.dot(hidden, w_down, preferred_element_type=jnp.float32)
    result = lax.psum_scatter(
        terms.astype(jnp.bfloat16), "split", scatter_dimension=1, tiled=True
    ).astype(jnp.float32)
    narrow = result.shape[1]
    returned = lax.all_to_all(
        result.reshape(experts, capacity, narrow).astype(jnp.bfloat16),
        "expert",
        split_axis=0,
        concat_axis=0,
        tiled=True,
    ).astype(jnp.float32)
    returned = returned.reshape(experts * capacity, narrow)
    picked = returned[dest] * mix[:, None]
    mixed = picked.reshape(tok_rows, 2, narrow).sum(axis=1)
    return mixed.astype(jnp.bfloat16)


def send(value, x=0, c=0, z=0, y=0):
    experts, splits = lax.axis_size("expert"), lax.axis_size("split")
    flip_expert, flip_split = x * 2 + c, z * 2 + y
    pairs = [
        (e * splits + s, (e ^ flip_expert) * splits + (s ^ flip_split))
        for e in range(experts)
        for s in range(splits)
    ]
    return lax.ppermute(value, BOTH, pairs)


def after(value, *earlier):
    return lax.optimization_barrier((value, earlier))[0]


def relayed(over_x, over_y):
    half = over_y[0].shape[1] // 2
    first = jnp.concatenate([v[:, :half] for v in over_y])
    last = jnp.concatenate([v[:, half : 2 * half] for v in over_x])
    return send(first, x=1), send(last, y=1)


def swapped(*blocks):
    return [(v, send(v, c=1)) for v in blocks]


def summed(terms, y, x, rows=slice(None)):
    return total(*[term[y, :, rows] for term in terms[x]])


def diagonal(terms):
    half = terms[0][0].shape[2] // 2
    first = summed(terms, 1, 1, slice(0, half)).astype(jnp.bfloat16)
    last = summed(terms, 1, 1, slice(half, 2 * half)).astype(jnp.bfloat16)
    return send(first, x=1), send(last, y=1)


def plane_sums(terms, first, last):
    half = terms[0][0].shape[2] // 2
    first, last = first.astype(jnp.float32), last.astype(jnp.float32)
    to_x = summed(terms, 0, 1) + jnp.pad(last, ((0, 0), (half, 0), (0, 0)))
    to_y = summed(terms, 1, 0) + jnp.pad(first, ((0, 0), (0, half), (0, 0)))
    return to_x.astype(jnp.bfloat16), to_y.astype(jnp.bfloat16)


def total(*terms):
    result = terms[0].astype(jnp.float32)
    for term in terms[1:]:
        result = result + term.astype(jnp.float32)
    return result


def pieces(x, pair):
    blocks, over_x, over_y, first, last = pair
    size = blocks[1][0][0].shape[1]
    arrays, found = [], []
    for z in range(2):
        for c in range(2):
            parts = [(blocks[z], 0, 0), (over_y[z], 0, 1)]
            if x:
                parts = [(over_x[z], 0, 0), (first[z], 0, 1), (last[z], size // 2, 1)]
            for (array, index), row, y in parts:
                array = array[c]
                if not any(array is v for v in arrays):
                    arrays.append(array)
                place = [i for i, v in enumerate(arrays) if v is array][0]
                found.append((place, index, z, c * size + row, y, min(size, array.shape[1])))
    return arrays, found


def fill(place, arrays, found, z_places, rows, sems):
    my_y = place[place.shape[0] - 1]
    copies = []
    for i, (which, index, z, row, y, count) in enumerate(found):
        source = arrays[which].at[index, pl.ds(0, count)]
        column = ((place[z_places[z]] & 1) * 2 + (my_y ^ y)) * source.shape[1]
        columns = pl.ds(pl.multiple_of(column, 128), source.shape[1])
        target = rows.at[pl.ds(row, count), columns]
        copies.append(pltpu.make_async_copy(source, target, sems.at[i]))
    return copies


def store(place, arrays, found, z_places, rows):
    my_y = place[place.shape[0] - 1]
    for which, index, z, row, y, count in found:
        narrow = arrays[which].shape[2]
        column = ((place[z_places[z]] & 1) * 2 + (my_y ^ y)) * narrow
        columns = pl.ds(pl.multiple_of(column, 128), narrow)
        rows[row : row + count, columns] = arrays[which][index, :count]


def all_of(copies):
    for copy in copies:
        copy.start()
    for copy in copies:
        copy.wait()


def weight_copies(place, z, weight, result, sems):
    depth = result.shape[0]
    quarter = depth // 4
    base = pl.multiple_of((place[z] // 2) * depth, depth)
    return [
        pltpu.make_async_copy(
            weight.at[pl.ds(base + q * quarter, quarter)],
            result.at[pl.ds(q * quarter, quarter)],
            sems.at[q],
        )
        for q in range(4)
    ]


def weights_kernel(place, *refs, z):
    w_gate, w_up, gate, up, gate_sems, up_sems = refs[-6:]
    all_of(
        weight_copies(place, z, w_gate, gate, gate_sems)
        + weight_copies(place, z, w_up, up, up_sems)
    )


def first_kernel(place, *refs, found, z_places, following):
    arrays, refs = refs[:-9], refs[-9:]
    w_gate, w_up, later, gate, up, later_rows, rows, sems, later_sems = refs
    later = weight_copies(place, following, later, later_rows, later_sems)
    copies = fill(place, arrays, found, z_places, rows, sems)
    for copy in copies + later:
        copy.start()
    for copy in copies:
        copy.wait()
    for weight, result in ((w_gate, gate), (w_up, up)):
        for t in range(result.shape[0]):
            tile = slice(t * HIDDEN_TILE, (t + 1) * HIDDEN_TILE)
            result[t] = jnp.dot(rows[...], weight[:, tile], preferred_element_type=jnp.float32)
    for copy in later:
        copy.wait()


def share_column(place, blocks, tails, sems, size):
    experts = place[place.shape[0] - 2]
    expert = place[place.shape[0] - 3]
    copies = []
    for c, block in enumerate(blocks):
        tail = pl.ds(size, tails.shape[1])
        copies.append(pltpu.make_async_copy(block.at[0, tail], tails.at[c], sems.at[c]))
    all_of(copies)
    column = []
    for c in range(2):
        row = lax.broadcasted_iota(jnp.int32, tails.shape[1:], 0)
        mine = (row == expert) | (row == expert + experts)
        shares = jnp.where(mine, tails[c].astype(jnp.float32), 0.0)
        shares = jnp.sum(shares, axis=0, keepdims=True)[:, :size]
        column.append(jnp.broadcast_to(shares, (128, size)).T)
    return jnp.concatenate(column)[:, :1]


def down_copy(place, pair, w_down, tile, sem):
    span = tile.shape[1]
    columns = pl.ds(pl.multiple_of((place[pair[0]] // 2) * span, span), span)
    return pltpu.make_async_copy(w_down.at[:, columns], tile, sem)


def down_products(place, pair, hidden, tile, results):
    my_y = place[place.shape[0] - 1]
    size, narrow = results[0].shape[2:]
    terms = jnp.dot(hidden[...], tile[...], preferred_element_type=jnp.float32)
    terms = terms.astype(jnp.bfloat16)
    for r, result in enumerate(results):
        for z in range(2):
            n = (place[pair[0]] & 1) ^ z
            for y in range(2):
                start = (z * 2 + y) * narrow
                piece = terms[r * size : (r + 1) * size, start : start + narrow]
                result[my_y ^ y, n] = piece


def second_kernel(place, *refs, x, found, z_places, pairs):
    count = 15 if x else 16
    arrays, refs = refs[:-count], refs[-count:]
    w_gate, w_up, gate, up, w_down = refs[:5]
    shares, results, hidden = refs[5:7], refs[7:9], refs[9]
    rows, tails, t_sems, d_sems, tile = refs[-5:]
    downs_in = [down_copy(place, pairs[0], w_down, tile, d_sems.at[0])]
    if x == 0:
        downs_in.append(down_copy(place, pairs[1], w_down, refs[10], d_sems.at[1]))
    for copy in downs_in:
        copy.start()
    store(place, arrays, found, z_places, rows)
    share = 0.5 * share_column(place, shares, tails, t_sems, results[0].shape[2])
    for t in range(gate.shape[0]):
        span = slice(t * HIDDEN_TILE, (t + 1) * HIDDEN_TILE)
        g = gate[t] + jnp.dot(rows[...], w_gate[:, span], preferred_element_type=jnp.float32)
        u = up[t] + jnp.dot(rows[...], w_up[:, span], preferred_element_type=jnp.float32)
        value = (g + g * jnp.tanh(0.5 * g)) * u * share
        hidden[:, span] = value.astype(jnp.bfloat16)
    downs_in[0].wait()
    down_products(place, pairs[0], hidden, tile, results)
    for copy in downs_in[1:]:
        copy.wait()


def third_kernel(place, hidden, tile, own, sibling, pair):
    down_products(place, pair, hidden, tile, (own, sibling))


def cost(flops, bytes_accessed, transcendentals):
    return pl.CostEstimate(
        flops=flops // SCALE,
        bytes_accessed=bytes_accessed // SCALE,
        transcendentals=transcendentals // SCALE,
    )


def in_hbm(value):
    return pltpu.with_memory_space_constraint(value, pltpu.HBM)


def in_vmem(value):
    return pltpu.with_memory_space_constraint(value, pltpu.VMEM)


ANY = pl.BlockSpec(memory_space=pl.ANY)
SCALARS = pl.BlockSpec(memory_space=pltpu.SMEM)
VMEM = pl.BlockSpec(memory_space=pltpu.VMEM)
SEMS = pltpu.SemaphoreType.DMA


def params(mebibytes):
    return pltpu.CompilerParams(vmem_limit_bytes=mebibytes * 1024 * 1024)


def pair_weights(place, z, w_gate, w_up, narrow, *earlier):
    width, depth = w_gate.shape[1], 4 * narrow
    return pl.pallas_call(
        lambda *refs: weights_kernel(*refs, z=z),
        in_specs=[SCALARS] + [ANY] * (len(earlier) + 2),
        out_specs=[VMEM] * 2,
        scratch_shapes=[SEMS((4,)), SEMS((4,))],
        out_shape=[pltpu.VMEM((depth, width), jnp.bfloat16)] * 2,
        compiler_params=params(2),
        cost_estimate=cost(flops=0, bytes_accessed=8 * depth * width, transcendentals=0),
        name="pair_weights",
    )(place, *earlier, w_gate, w_up)


def first_part(place, x, pair, z_places, weights, following, later):
    arrays, found = pieces(x, pair)
    size, narrow = pair[0][1][0][0].shape[1:]
    depth, width = weights[0].shape
    rows = 2 * size
    sums = pltpu.VMEM((width // HIDDEN_TILE, rows, HIDDEN_TILE), jnp.float32)
    return pl.pallas_call(
        lambda *refs: first_kernel(*refs, found=found, z_places=z_places, following=following),
        in_specs=[SCALARS] + [ANY] * len(arrays) + [VMEM, VMEM, ANY],
        out_specs=[VMEM] * 3,
        scratch_shapes=[
            pltpu.VMEM((rows, depth), jnp.bfloat16),
            SEMS((len(found),)),
            SEMS((4,)),
        ],
        out_shape=[sums, sums, pltpu.VMEM((depth, width), jnp.bfloat16)],
        compiler_params=params(4),
        cost_estimate=cost(
            flops=4 * rows * depth * width,
            bytes_accessed=4 * depth * width + 2 * rows * depth + 8 * rows * width,
            transcendentals=0,
        ),
        name="first_part",
    )(place, *arrays, *[in_vmem(v) for v in weights], later)


def second_part(place, x, pair, z_places, weights, sums, shares, w_down, pairs):
    arrays, found = pieces(x, pair)
    size, narrow = pair[0][1][0][0].shape[1:]
    depth, width = weights[0].shape
    rows, tail = 2 * size, shares[0].shape[1] - size
    part = pltpu.VMEM((2, 2, size, narrow), jnp.bfloat16)
    hidden, tile = [pltpu.VMEM(v, jnp.bfloat16) for v in ((rows, width), (width, depth))]
    return pl.pallas_call(
        lambda *refs: second_kernel(
            *refs, x=x, found=found, z_places=z_places, pairs=pairs
        ),
        in_specs=[SCALARS] + [VMEM] * (len(arrays) + 4) + [ANY] * 3,
        out_specs=[VMEM] * (3 if x else 4),
        scratch_shapes=[
            pltpu.VMEM((rows, depth), jnp.bfloat16),
            pltpu.VMEM((2, tail, narrow), jnp.bfloat16),
            SEMS((2,)),
            SEMS((2,)),
            tile,
        ],
        out_shape=[part, part, hidden] + ([] if x else [tile]),
        compiler_params=params(9),
        cost_estimate=cost(
            flops=4 * rows * depth * width + 4 * rows * width * depth,
            bytes_accessed=8 * depth * width + 6 * rows * depth + 8 * rows * width,
            transcendentals=rows * width,
        ),
        name="second_part",
    )(place, *[in_vmem(v) for v in (*arrays, *weights, *sums)], w_down, *shares)


def third_part(place, hidden, tile, pair, size):
    rows, width = hidden.shape
    narrow = tile.shape[1] // 4
    return pl.pallas_call(
        lambda *refs: third_kernel(*refs, pair=pair),
        in_specs=[SCALARS, VMEM, VMEM],
        out_specs=[VMEM] * 2,
        out_shape=[pltpu.VMEM((2, 2, size, narrow), jnp.bfloat16)] * 2,
        compiler_params=params(8),
        cost_estimate=cost(
            flops=2 * rows * width * tile.shape[1],
            bytes_accessed=2 * width * (rows + tile.shape[1]) + 2 * rows * tile.shape[1],
            transcendentals=0,
        ),
        name="third_part",
    )(place, in_vmem(hidden), in_vmem(tile))


def shares_of(expert_ids, pair_logits):
    mix = pair_mix(pair_logits)
    labels = jnp.arange(lax.axis_size("expert"), dtype=jnp.int32)
    named = expert_ids[None, :, :] == labels[:, None, None]
    return jnp.sum(jnp.where(named, mix[None], 0.0), axis=2)


def share_rows(shares, narrow):
    high = lax.reduce_precision(shares, 8, 7)
    rows = jnp.concatenate([high, shares - high]).astype(jnp.bfloat16)
    return jnp.pad(rows, ((0, -rows.shape[0] % 16), (0, narrow - rows.shape[1])))


def every_row(tokens, expert_ids, pair_logits, w_gate, w_up, w_down):
    expert, split = lax.axis_index("expert"), lax.axis_index("split")
    size, narrow = tokens.shape
    place = [(split // 2) ^ z for z in range(4)]
    place = jnp.stack(place + [expert, lax.axis_size("expert"), split % 2]).astype(jnp.int32)
    w_gate, w_up, w_down = in_hbm(w_gate), in_hbm(w_up), in_hbm(w_down)

    w_gate, w_up, w_down = in_hbm(w_gate), in_hbm(w_up), in_hbm(w_down)
    z0 = tokens[None]
    z1 = send(z0, z=1)
    own = shares_of(expert_ids, pair_logits)
    block = jnp.concatenate([tokens, share_rows(own, narrow)])[None]
    sent = after(z0, own)
    x0, y0, z2 = send(block, x=1), send(sent, y=1), send(sent, z=2)
    x1, y1 = send(z1, x=1), send(z1, y=1)
    sz0, sz1, sx0, sx1, sy0, sy1 = swapped(block, z1, x0, x1, y0, y1)
    near_weights = pair_weights(place, 0, w_gate, w_up, narrow, x0)
    (x1_, y1_), z2, near_weights = after(((x1, y1), z2, near_weights))
    first, last = relayed([x0, x1_], [y0, y1_])
    z3 = send(z2, z=1)
    x2, y2 = send(z2, x=1), send(z2, y=1)
    near = [[(sz0, 0), (sz1, 0)], [(sx0, 0), (sx1, 0)], [(sy0, 0), (sy1, 0)], None, None]
    *sums_0, far_gate = first_part(place, 0, near, (0, 1), near_weights, 2, w_gate)

    z3, sums_0 = after((z3, sums_0))
    (first, last, x2, y2), sums_0 = after(((first, last, x2, y2), sums_0))
    x3, y3 = send(z3, x=1), send(z3, y=1)
    both_of = lambda v: [(v, 0), (v, 1)]
    near[3:] = [both_of(v) for v in swapped(first, last)]
    sz2, sz3, sx2, sy2 = swapped(z2, z3, x2, y2)
    *sums_1, far_up = first_part(place, 1, near, (0, 1), near_weights, 2, w_up)
    far_weights = far_gate, far_up
    (x3, y3), sums_1 = after(((x3, y3), sums_1))
    first, last = relayed([x2, x3], [y2, y3])
    sx3, sy3 = swapped(x3, y3)
    far = [[(sz2, 0), (sz3, 0)], [(sx2, 0), (sx3, 0)], [(sy2, 0), (sy3, 0)], None, None]
    pairs = (3, 2), (1, 0)
    *parts_0, hidden, tile = second_part(
        place, 0, far, (2, 3), far_weights, sums_0, sz0, w_down, pairs
    )
    (first, last, sx2, sx3), parts_0 = after(((first, last, sx2, sx3), parts_0))
    far[1] = [(sx2, 0), (sx3, 0)]
    corners = swapped(first, last)
    last_0 = third_part(place, hidden, tile, pairs[1], size)
    corners, last_0 = after((corners, last_0))
    far[3:] = [both_of(v) for v in corners]
    far_0 = parts_0[0], send(parts_0[1], c=1)
    near_0 = last_0[0], send(last_0[1], c=1)
    *parts_1, hidden = second_part(
        place, 1, far, (2, 3), far_weights, sums_1, sx0, w_down, pairs
    )
    far_0, near_0, parts_1 = after((far_0, near_0, parts_1))
    to_z = total(*[v[:, :1] for v in near_0]).astype(jnp.bfloat16)
    passed_0 = send(to_z, z=1)
    other_1 = send(parts_1[1], c=1)
    last_1 = third_part(place, after(hidden, far_0), tile, pairs[1], size)
    other_1, last_1 = after((other_1, last_1))
    far_1, near_1 = (parts_1[0], other_1), (last_1[0], send(last_1[1], c=1))

    far = far_0, far_1
    corner = diagonal(far)
    to_z = total(*[v[:, :1] for v in near_1]).astype(jnp.bfloat16)
    passed_1 = send(to_z, z=1)
    to_x, to_y = plane_sums(far, *after(corner, to_z))
    from_3 = send(to_x[:1], x=1), send(to_y[:1], y=1)
    here = summed(far, 0, 0)
    to_2 = total(here[:1], *from_3).astype(jnp.bfloat16)
    to_x, to_y = after((to_x, to_y), to_2)
    to_2 = send(to_2, z=1)
    from_2 = send(to_x[1:], x=1), send(to_y[1:], y=1)
    last_block = lambda terms, passed: [v[:, 1:] for v in terms] + [passed]
    near = last_block(near_0, passed_0), last_block(near_1, passed_1)
    corner = diagonal(near)
    to_0 = total(here[1:], *from_2, to_2).astype(jnp.bfloat16)
    to_x, to_y = plane_sums(near, *after(corner, to_0))
    to_0 = send(to_0, z=2)
    from_0 = send(to_x, x=1), send(to_y, y=1)
    return total(summed(near, 0, 0), *from_0, to_0)[0].astype(jnp.bfloat16)


def body(tokens, expert_ids, pair_logits, gate_weight, up_weight, down_weight):
    capacity = 4 * tokens.shape[0] // lax.axis_size("expert")
    arrays = (tokens, expert_ids, pair_logits, gate_weight[0], up_weight[0], down_weight[0])
    splits = lax.axis_size("split")
    if capacity == tokens.shape[0] and splits == 8 and tokens.shape[0] <= tokens.shape[1]:
        return every_row(*arrays)
    return dispatched(*arrays, capacity)


def solution(mesh):
    in_specs = (
        P("expert", "split"),
        P("expert", None),
        P("expert", None),
        P("expert", None, "split"),
        P("expert", None, "split"),
        P("expert", "split", None),
    )
    out_specs = P("expert", "split")
    return jax.shard_map(body, mesh=mesh, in_specs=in_specs, out_specs=out_specs, check_vma=False)
```

```python
import jax
import jax.numpy as jnp
from jax import lax
from jax.experimental import pallas as pl
from jax.experimental.pallas import tpu as pltpu
from jax.sharding import PartitionSpec as P

BOTH = ("expert", "split")
HIDDEN_TILE = 1024
SCALE = 4


def pair_mix(pair_logits):
    first = jax.nn.sigmoid(pair_logits[:, 0] - pair_logits[:, 1])
    return jnp.stack([first, 1.0 - first], axis=1)


def dispatched(tokens, expert_ids, pair_logits, w_gate, w_up, w_down, capacity):
    experts = lax.axis_size("expert")
    tok_rows, narrow = tokens.shape
    flat = expert_ids.reshape(-1)
    labels = jnp.arange(experts, dtype=jnp.int32)
    onehot = (flat[:, None] == labels[None, :]).astype(jnp.int32)
    before = jnp.cumsum(onehot, axis=0) - onehot
    slot = jnp.sum(before * onehot, axis=1)
    dest = flat * capacity + slot
    mix = pair_mix(pair_logits).reshape(-1)
    select = (jnp.arange(experts * capacity, dtype=jnp.int32)[:, None] == dest[None, :]).astype(
        jnp.bfloat16
    )
    doubled = jnp.repeat(tokens, 2, axis=0)
    packed = jnp.dot(select, doubled, preferred_element_type=jnp.float32).astype(jnp.bfloat16)
    sending = packed.reshape(experts, capacity, narrow)
    arrived = lax.all_to_all(sending, "expert", split_axis=0, concat_axis=0, tiled=True).reshape(
        experts * capacity, narrow
    )
    piece = lax.all_gather(arrived, "split", axis=1, tiled=True)
    gate = jnp.dot(piece, w_gate, preferred_element_type=jnp.float32)
    up_part = jnp.dot(piece, w_up, preferred_element_type=jnp.float32)
    hidden = (jax.nn.silu(gate) * up_part).astype(jnp.bfloat16)
    terms = jnp.dot(hidden, w_down, preferred_element_type=jnp.float32)
    result = lax.psum_scatter(
        terms.astype(jnp.bfloat16), "split", scatter_dimension=1, tiled=True
    ).astype(jnp.float32)
    narrow = result.shape[1]
    returned = lax.all_to_all(
        result.reshape(experts, capacity, narrow).astype(jnp.bfloat16),
        "expert",
        split_axis=0,
        concat_axis=0,
        tiled=True,
    ).astype(jnp.float32)
    returned = returned.reshape(experts * capacity, narrow)
    picked = returned[dest] * mix[:, None]
    mixed = picked.reshape(tok_rows, 2, narrow).sum(axis=1)
    return mixed.astype(jnp.bfloat16)


def send(value, x=0, c=0, z=0, y=0):
    experts, splits = lax.axis_size("expert"), lax.axis_size("split")
    flip_expert, flip_split = x * 2 + c, z * 2 + y
    pairs = [
        (e * splits + s, (e ^ flip_expert) * splits + (s ^ flip_split))
        for e in range(experts)
        for s in range(splits)
    ]
    return lax.ppermute(value, BOTH, pairs)


def after(value, *earlier):
    return lax.optimization_barrier((value, earlier))[0]


def relayed(over_x, over_y):
    half = over_y[0].shape[1] // 2
    first = jnp.concatenate([v[:, :half] for v in over_y])
    last = jnp.concatenate([v[:, half : 2 * half] for v in over_x])
    return send(first, x=1), send(last, y=1)


def swapped(*blocks):
    return [(v, send(v, c=1)) for v in blocks]


def summed(terms, y, x, rows=slice(None)):
    return total(*[term[y, :, rows] for term in terms[x]])


def diagonal(terms):
    half = terms[0][0].shape[2] // 2
    first = summed(terms, 1, 1, slice(0, half)).astype(jnp.bfloat16)
    last = summed(terms, 1, 1, slice(half, 2 * half)).astype(jnp.bfloat16)
    return send(first, x=1), send(last, y=1)


def plane_sums(terms, first, last):
    half = terms[0][0].shape[2] // 2
    first, last = first.astype(jnp.float32), last.astype(jnp.float32)
    to_x = summed(terms, 0, 1) + jnp.pad(last, ((0, 0), (half, 0), (0, 0)))
    to_y = summed(terms, 1, 0) + jnp.pad(first, ((0, 0), (0, half), (0, 0)))
    return to_x.astype(jnp.bfloat16), to_y.astype(jnp.bfloat16)


def total(*terms):
    result = terms[0].astype(jnp.float32)
    for term in terms[1:]:
        result = result + term.astype(jnp.float32)
    return result


def pieces(x, pair):
    blocks, over_x, over_y, first, last = pair
    size = blocks[1][0][0].shape[1]
    arrays, found = [], []
    for z in range(2):
        for c in range(2):
            parts = [(blocks[z], 0, 0), (over_y[z], 0, 1)]
            if x:
                parts = [(over_x[z], 0, 0), (first[z], 0, 1), (last[z], size // 2, 1)]
            for (array, index), row, y in parts:
                array = array[c]
                if not any(array is v for v in arrays):
                    arrays.append(array)
                place = [i for i, v in enumerate(arrays) if v is array][0]
                found.append((place, index, z, c * size + row, y, min(size, array.shape[1])))
    return arrays, found


def fill(place, arrays, found, z_places, rows, sems):
    my_y = place[place.shape[0] - 1]
    copies = []
    for i, (which, index, z, row, y, count) in enumerate(found):
        source = arrays[which].at[index, pl.ds(0, count)]
        column = ((place[z_places[z]] & 1) * 2 + (my_y ^ y)) * source.shape[1]
        columns = pl.ds(pl.multiple_of(column, 128), source.shape[1])
        target = rows.at[pl.ds(row, count), columns]
        copies.append(pltpu.make_async_copy(source, target, sems.at[i]))
    return copies


def store(place, arrays, found, z_places, rows):
    my_y = place[place.shape[0] - 1]
    for which, index, z, row, y, count in found:
        narrow = arrays[which].shape[2]
        column = ((place[z_places[z]] & 1) * 2 + (my_y ^ y)) * narrow
        columns = pl.ds(pl.multiple_of(column, 128), narrow)
        rows[row : row + count, columns] = arrays[which][index, :count]


def all_of(copies):
    for copy in copies:
        copy.start()
    for copy in copies:
        copy.wait()


def weight_copies(place, z, weight, result, sems):
    depth = result.shape[0]
    quarter = depth // 4
    base = pl.multiple_of((place[z] // 2) * depth, depth)
    return [
        pltpu.make_async_copy(
            weight.at[pl.ds(base + q * quarter, quarter)],
            result.at[pl.ds(q * quarter, quarter)],
            sems.at[q],
        )
        for q in range(4)
    ]


def weights_kernel(place, *refs, z):
    w_gate, w_up, gate, up, gate_sems, up_sems = refs[-6:]
    all_of(
        weight_copies(place, z, w_gate, gate, gate_sems)
        + weight_copies(place, z, w_up, up, up_sems)
    )


def first_kernel(place, *refs, found, z_places, following):
    arrays, refs = refs[:-9], refs[-9:]
    w_gate, w_up, later, gate, up, later_rows, rows, sems, later_sems = refs
    later = weight_copies(place, following, later, later_rows, later_sems)
    copies = fill(place, arrays, found, z_places, rows, sems)
    for copy in copies + later:
        copy.start()
    for copy in copies:
        copy.wait()
    for weight, result in ((w_gate, gate), (w_up, up)):
        for t in range(result.shape[0]):
            tile = slice(t * HIDDEN_TILE, (t + 1) * HIDDEN_TILE)
            result[t] = jnp.dot(rows[...], weight[:, tile], preferred_element_type=jnp.float32)
    for copy in later:
        copy.wait()


def share_column(place, blocks, tails, sems, size):
    experts = place[place.shape[0] - 2]
    expert = place[place.shape[0] - 3]
    copies = []
    for c, block in enumerate(blocks):
        tail = pl.ds(size, tails.shape[1])
        copies.append(pltpu.make_async_copy(block.at[0, tail], tails.at[c], sems.at[c]))
    all_of(copies)
    column = []
    for c in range(2):
        row = lax.broadcasted_iota(jnp.int32, tails.shape[1:], 0)
        mine = (row == expert) | (row == expert + experts)
        shares = jnp.where(mine, tails[c].astype(jnp.float32), 0.0)
        shares = jnp.sum(shares, axis=0, keepdims=True)[:, :size]
        column.append(jnp.broadcast_to(shares, (128, size)).T)
    return jnp.concatenate(column)[:, :1]


def down_copy(place, pair, w_down, tile, sem):
    span = tile.shape[1]
    columns = pl.ds(pl.multiple_of((place[pair[0]] // 2) * span, span), span)
    return pltpu.make_async_copy(w_down.at[:, columns], tile, sem)


def down_products(place, pair, hidden, tile, results):
    my_y = place[place.shape[0] - 1]
    size, narrow = results[0].shape[2:]
    terms = jnp.dot(hidden[...], tile[...], preferred_element_type=jnp.float32)
    terms = terms.astype(jnp.bfloat16)
    for r, result in enumerate(results):
        for z in range(2):
            n = (place[pair[0]] & 1) ^ z
            for y in range(2):
                start = (z * 2 + y) * narrow
                piece = terms[r * size : (r + 1) * size, start : start + narrow]
                result[my_y ^ y, n] = piece


def second_kernel(place, *refs, x, found, z_places, pairs):
    count = 15 if x else 16
    arrays, refs = refs[:-count], refs[-count:]
    w_gate, w_up, gate, up, w_down = refs[:5]
    shares, results, hidden = refs[5:7], refs[7:9], refs[9]
    rows, tails, t_sems, d_sems, tile = refs[-5:]
    downs_in = [down_copy(place, pairs[0], w_down, tile, d_sems.at[0])]
    if x == 0:
        downs_in.append(down_copy(place, pairs[1], w_down, refs[10], d_sems.at[1]))
    for copy in downs_in:
        copy.start()
    store(place, arrays, found, z_places, rows)
    share = 0.5 * share_column(place, shares, tails, t_sems, results[0].shape[2])
    for t in range(gate.shape[0]):
        span = slice(t * HIDDEN_TILE, (t + 1) * HIDDEN_TILE)
        g = gate[t] + jnp.dot(rows[...], w_gate[:, span], preferred_element_type=jnp.float32)
        gated = (g + g * jnp.tanh(0.5 * g)) * share
        u = up[t] + jnp.dot(rows[...], w_up[:, span], preferred_element_type=jnp.float32)
        value = gated * u
        hidden[:, span] = value.astype(jnp.bfloat16)
    downs_in[0].wait()
    down_products(place, pairs[0], hidden, tile, results)
    for copy in downs_in[1:]:
        copy.wait()


def third_kernel(place, hidden, tile, own, sibling, pair):
    down_products(place, pair, hidden, tile, (own, sibling))


def cost(flops, bytes_accessed, transcendentals):
    return pl.CostEstimate(
        flops=flops // SCALE,
        bytes_accessed=bytes_accessed // SCALE,
        transcendentals=transcendentals // SCALE,
    )


def in_hbm(value):
    return pltpu.with_memory_space_constraint(value, pltpu.HBM)


def in_vmem(value):
    return pltpu.with_memory_space_constraint(value, pltpu.VMEM)


ANY = pl.BlockSpec(memory_space=pl.ANY)
SCALARS = pl.BlockSpec(memory_space=pltpu.SMEM)
VMEM = pl.BlockSpec(memory_space=pltpu.VMEM)
SEMS = pltpu.SemaphoreType.DMA


def params(mebibytes):
    return pltpu.CompilerParams(vmem_limit_bytes=mebibytes * 1024 * 1024)


def pair_weights(place, z, w_gate, w_up, narrow, *earlier):
    width, depth = w_gate.shape[1], 4 * narrow
    return pl.pallas_call(
        lambda *refs: weights_kernel(*refs, z=z),
        in_specs=[SCALARS] + [ANY] * (len(earlier) + 2),
        out_specs=[VMEM] * 2,
        scratch_shapes=[SEMS((4,)), SEMS((4,))],
        out_shape=[pltpu.VMEM((depth, width), jnp.bfloat16)] * 2,
        compiler_params=params(2),
        cost_estimate=cost(flops=0, bytes_accessed=8 * depth * width, transcendentals=0),
        name="pair_weights",
    )(place, *earlier, w_gate, w_up)


def first_part(place, x, pair, z_places, weights, following, later):
    arrays, found = pieces(x, pair)
    size, narrow = pair[0][1][0][0].shape[1:]
    depth, width = weights[0].shape
    rows = 2 * size
    sums = pltpu.VMEM((width // HIDDEN_TILE, rows, HIDDEN_TILE), jnp.float32)
    return pl.pallas_call(
        lambda *refs: first_kernel(*refs, found=found, z_places=z_places, following=following),
        in_specs=[SCALARS] + [ANY] * len(arrays) + [VMEM, VMEM, ANY],
        out_specs=[VMEM] * 3,
        scratch_shapes=[
            pltpu.VMEM((rows, depth), jnp.bfloat16),
            SEMS((len(found),)),
            SEMS((4,)),
        ],
        out_shape=[sums, sums, pltpu.VMEM((depth, width), jnp.bfloat16)],
        compiler_params=params(4),
        cost_estimate=cost(
            flops=4 * rows * depth * width,
            bytes_accessed=4 * depth * width + 2 * rows * depth + 8 * rows * width,
            transcendentals=0,
        ),
        name="first_part",
    )(place, *arrays, *[in_vmem(v) for v in weights], later)


def second_part(place, x, pair, z_places, weights, sums, shares, w_down, pairs):
    arrays, found = pieces(x, pair)
    size, narrow = pair[0][1][0][0].shape[1:]
    depth, width = weights[0].shape
    rows, tail = 2 * size, shares[0].shape[1] - size
    part = pltpu.VMEM((2, 2, size, narrow), jnp.bfloat16)
    hidden, tile = [pltpu.VMEM(v, jnp.bfloat16) for v in ((rows, width), (width, depth))]
    return pl.pallas_call(
        lambda *refs: second_kernel(
            *refs, x=x, found=found, z_places=z_places, pairs=pairs
        ),
        in_specs=[SCALARS] + [VMEM] * (len(arrays) + 4) + [ANY] * 3,
        out_specs=[VMEM] * (3 if x else 4),
        scratch_shapes=[
            pltpu.VMEM((rows, depth), jnp.bfloat16),
            pltpu.VMEM((2, tail, narrow), jnp.bfloat16),
            SEMS((2,)),
            SEMS((2,)),
            tile,
        ],
        out_shape=[part, part, hidden] + ([] if x else [tile]),
        compiler_params=params(9),
        cost_estimate=cost(
            flops=4 * rows * depth * width + 4 * rows * width * depth,
            bytes_accessed=8 * depth * width + 6 * rows * depth + 8 * rows * width,
            transcendentals=rows * width,
        ),
        name="second_part",
    )(place, *[in_vmem(v) for v in (*arrays, *weights, *sums)], w_down, *shares)


def third_part(place, hidden, tile, pair, size):
    rows, width = hidden.shape
    narrow = tile.shape[1] // 4
    return pl.pallas_call(
        lambda *refs: third_kernel(*refs, pair=pair),
        in_specs=[SCALARS, VMEM, VMEM],
        out_specs=[VMEM] * 2,
        out_shape=[pltpu.VMEM((2, 2, size, narrow), jnp.bfloat16)] * 2,
        compiler_params=params(8),
        cost_estimate=cost(
            flops=2 * rows * width * tile.shape[1],
            bytes_accessed=2 * width * (rows + tile.shape[1]) + 2 * rows * tile.shape[1],
            transcendentals=0,
        ),
        name="third_part",
    )(place, in_vmem(hidden), in_vmem(tile))


def shares_of(expert_ids, pair_logits):
    mix = pair_mix(pair_logits)
    labels = jnp.arange(lax.axis_size("expert"), dtype=jnp.int32)
    named = expert_ids[None, :, :] == labels[:, None, None]
    return jnp.sum(jnp.where(named, mix[None], 0.0), axis=2)


def share_rows(shares, narrow):
    high = lax.reduce_precision(shares, 8, 7)
    rows = jnp.concatenate([high, shares - high]).astype(jnp.bfloat16)
    return jnp.pad(rows, ((0, -rows.shape[0] % 16), (0, narrow - rows.shape[1])))


def every_row(tokens, expert_ids, pair_logits, w_gate, w_up, w_down):
    expert, split = lax.axis_index("expert"), lax.axis_index("split")
    size, narrow = tokens.shape
    place = [(split // 2) ^ z for z in range(4)]
    place = jnp.stack(place + [expert, lax.axis_size("expert"), split % 2]).astype(jnp.int32)
    w_gate, w_up, w_down = in_hbm(w_gate), in_hbm(w_up), in_hbm(w_down)

    w_gate, w_up, w_down = in_hbm(w_gate), in_hbm(w_up), in_hbm(w_down)
    z0 = tokens[None]
    z1 = send(z0, z=1)
    own = shares_of(expert_ids, pair_logits)
    block = jnp.concatenate([tokens, share_rows(own, narrow)])[None]
    sent = after(z0, own)
    x0, y0, z2 = send(block, x=1), send(sent, y=1), send(sent, z=2)
    x1, y1 = send(z1, x=1), send(z1, y=1)
    sz0, sz1, sx0, sx1, sy0, sy1 = swapped(block, z1, x0, x1, y0, y1)
    near_weights = pair_weights(place, 0, w_gate, w_up, narrow, x0)
    (x1_, y1_), z2, near_weights = after(((x1, y1), z2, near_weights))
    first, last = relayed([x0, x1_], [y0, y1_])
    z3 = send(z2, z=1)
    x2, y2 = send(z2, x=1), send(z2, y=1)
    near = [[(sz0, 0), (sz1, 0)], [(sx0, 0), (sx1, 0)], [(sy0, 0), (sy1, 0)], None, None]
    *sums_0, far_gate = first_part(place, 0, near, (0, 1), near_weights, 2, w_gate)

    z3, sums_0 = after((z3, sums_0))
    (first, last, x2, y2), sums_0 = after(((first, last, x2, y2), sums_0))
    x3, y3 = send(z3, x=1), send(z3, y=1)
    both_of = lambda v: [(v, 0), (v, 1)]
    near[3:] = [both_of(v) for v in swapped(first, last)]
    sz2, sz3, sx2, sy2 = swapped(z2, z3, x2, y2)
    *sums_1, far_up = first_part(place, 1, near, (0, 1), near_weights, 2, w_up)
    far_weights = far_gate, far_up
    (x3, y3), sums_1 = after(((x3, y3), sums_1))
    first, last = relayed([x2, x3], [y2, y3])
    sx3, sy3 = swapped(x3, y3)
    far = [[(sz2, 0), (sz3, 0)], [(sx2, 0), (sx3, 0)], [(sy2, 0), (sy3, 0)], None, None]
    pairs = (3, 2), (1, 0)
    *parts_0, hidden, tile = second_part(
        place, 0, far, (2, 3), far_weights, sums_0, sz0, w_down, pairs
    )
    (first, last, sx2, sx3), parts_0 = after(((first, last, sx2, sx3), parts_0))
    far[1] = [(sx2, 0), (sx3, 0)]
    corners = swapped(first, last)
    last_0 = third_part(place, hidden, tile, pairs[1], size)
    corners, last_0 = after((corners, last_0))
    far[3:] = [both_of(v) for v in corners]
    far_0 = parts_0[0], send(parts_0[1], c=1)
    near_0 = last_0[0], send(last_0[1], c=1)
    *parts_1, hidden = second_part(
        place, 1, far, (2, 3), far_weights, sums_1, sx0, w_down, pairs
    )
    far_0, near_0, parts_1 = after((far_0, near_0, parts_1))
    to_z = total(*[v[:, :1] for v in near_0]).astype(jnp.bfloat16)
    passed_0 = send(to_z, z=1)
    other_1 = send(parts_1[1], c=1)
    last_1 = third_part(place, after(hidden, far_0), tile, pairs[1], size)
    other_1, last_1 = after((other_1, last_1))
    far_1, near_1 = (parts_1[0], other_1), (last_1[0], send(last_1[1], c=1))

    far = far_0, far_1
    corner = diagonal(far)
    to_z = total(*[v[:, :1] for v in near_1]).astype(jnp.bfloat16)
    passed_1 = send(to_z, z=1)
    to_x, to_y = plane_sums(far, *after(corner, to_z))
    from_3 = send(to_x[:1], x=1), send(to_y[:1], y=1)
    here = summed(far, 0, 0)
    to_2 = total(here[:1], *from_3).astype(jnp.bfloat16)
    to_x, to_y = after((to_x, to_y), to_2)
    to_2 = send(to_2, z=1)
    from_2 = send(to_x[1:], x=1), send(to_y[1:], y=1)
    last_block = lambda terms, passed: [v[:, 1:] for v in terms] + [passed]
    near = last_block(near_0, passed_0), last_block(near_1, passed_1)
    corner = diagonal(near)
    to_0 = total(here[1:], *from_2, to_2).astype(jnp.bfloat16)
    to_x, to_y = plane_sums(near, *after(corner, to_0))
    to_0 = send(to_0, z=2)
    from_0 = send(to_x, x=1), send(to_y, y=1)
    return total(summed(near, 0, 0), *from_0, to_0)[0].astype(jnp.bfloat16)


def body(tokens, expert_ids, pair_logits, gate_weight, up_weight, down_weight):
    capacity = 4 * tokens.shape[0] // lax.axis_size("expert")
    arrays = (tokens, expert_ids, pair_logits, gate_weight[0], up_weight[0], down_weight[0])
    splits = lax.axis_size("split")
    if capacity == tokens.shape[0] and splits == 8 and tokens.shape[0] <= tokens.shape[1]:
        return every_row(*arrays)
    return dispatched(*arrays, capacity)


def solution(mesh):
    in_specs = (
        P("expert", "split"),
        P("expert", None),
        P("expert", None),
        P("expert", None, "split"),
        P("expert", None, "split"),
        P("expert", "split", None),
    )
    out_specs = P("expert", "split")
    return jax.shard_map(body, mesh=mesh, in_specs=in_specs, out_specs=out_specs, check_vma=False)
```
